32 devices in a mesh: dp: 8 (over z, y), ulysses: 4 (over x, core).
Axes of the slice: x: 2, y: 2, z: 4, core: 2. Of those that a mesh axis runs over, the one named last changes fastest.
Arguments:
- tokens: bfloat16 [8, 1024, 2048], P('dp', 'ulysses'), may hold values from -6 to 6
- seq_lengths: int32 [8], P('dp'), may hold values from 769 to 1024, as said below
- cotangent: bfloat16 [8, 1024, 2048], P('dp', 'ulysses'), may hold values from -6 to 6
- norm1_gain: float32 [2048], replicated, may hold values from 0.1 to 1.9
- input_weight: bfloat16 [2048, 6144], P('dp'), may hold values from -0.125 to 0.125
- query_gain: float32 [128], replicated, may hold values from 0.1 to 1.9
- key_gain: float32 [128], replicated, may hold values from 0.1 to 1.9
- output_weight: bfloat16 [2048, 2048], P('dp'), may hold values from -2 to 2
- norm2_gain: float32 [2048], replicated, may hold values from 0.1 to 1.9
- perceptron_input_weight: bfloat16 [2048, 12288], P('dp'), may hold values from -0.125 to 0.125
- down_weight: bfloat16 [6144, 2048], P('dp'), may hold values from -0.078125 to 0.078125
Outputs:
- layer_out: float32 [8, 1024, 2048], P('dp', 'ulysses')
- tokens_grad: float32 [8, 1024, 2048], P('dp', 'ulysses')
- norm1_gain_grad: float32 [2048], replicated
- w_in_grad: float32 [2048, 6144], P('dp')
- query_gain_grad: float32 [128], replicated
- key_gain_grad: float32 [128], replicated
- w_out_grad: float32 [2048, 2048], P('dp')
- norm2_gain_grad: float32 [2048], replicated
- w_mlp_in_grad: float32 [2048, 12288], P('dp')
- w_down_grad: float32 [6144, 2048], P('dp')
The draws below stay inside these ranges and needn't reach their ends.
Inputs may be any that keep to these rules, and one draw needn't show every extreme that they name: `seq_lengths`: some slot has length 1024; every slot reaches into the last 1024 / 4 positions of its bucket.
All inputs are finite; a program needn't handle non-finite values.
Results may differ from the reference program's by a relative error of at most 0.02.
Values may be sent and summed in bfloat16 or wider, within the bound.
A program may use at most 576 MiB of HBM per device.

```python
import jax
import jax.numpy as jnp
from jax import lax

D = 2048
QUERY_HEADS = 16
KEY_VALUE_HEADS = 8
HEAD_DIMENSION = 128
FF = 6144
SEQS_G = 1
BUCKET = 1024
NSEQ = 8
PROJ = 6144
N_ULYSSES = 4


def draw_seq_lengths(key, part):
    key = jax.random.fold_in(key, 11)
    first_key, second_key, third_key, fourth_key = jax.random.split(key, 4)
    lowest = BUCKET - BUCKET // N_ULYSSES + 1
    first_draw = jax.random.randint(first_key, (NSEQ,), lowest, BUCKET + 1)
    second_draw = jax.random.randint(second_key, (NSEQ,), lowest, BUCKET + 1)
    ragged = jnp.minimum(first_draw, second_draw)
    longest = jax.random.randint(third_key, (), 0, NSEQ)
    offset = jax.random.randint(fourth_key, (), 1, NSEQ)
    shortest = (longest + offset) % NSEQ
    slot_index = jnp.arange(NSEQ)
    lengths = jnp.where(slot_index == longest, BUCKET, jnp.where(slot_index == shortest, lowest, ragged))
    return lengths.astype(jnp.int32)


def levels(stream_key, extent, cuts, low, top_value):
    gain, own = 1.0, jax.random.fold_in(stream_key, 6)
    for axis_at, parts in cuts:
        steps = jnp.exp(jax.random.uniform(jax.random.fold_in(own, axis_at), (parts,), jnp.float32, low / len(cuts), top_value / len(cuts)))
        gain = gain * jnp.repeat(steps, extent[axis_at] // parts).reshape([-1 if axis == axis_at else 1 for axis in range(len(extent))])
    return gain


def scatter_about(rng, extent, spread, reach, shards=(), dtype=jnp.bfloat16):
    loudness = levels(rng, extent, shards, -0.22, 0.18) if shards else 1.0
    values = jax.random.normal(rng, extent, jnp.float32) * spread * loudness
    return jnp.minimum(jnp.maximum(values, -reach), reach).astype(dtype)


def setup_inputs(seed: int = 0) -> dict:
    key_of = jax.random.split(jax.random.key(seed), 12)
    return {
        "tokens": scatter_about(key_of[0], (NSEQ, BUCKET, D), 1.0, 6.0, ((0, 8), (1, 4))),
        "seq_lengths": draw_seq_lengths(jax.random.fold_in(key_of[11], 71), 0),
        "cotangent": scatter_about(key_of[2], (NSEQ, BUCKET, D), 1.0, 6.0, ((0, 8), (1, 4))),
        "norm1_gain": jnp.clip(1.0 + 0.18 * jax.random.normal(key_of[3], (D,), jnp.float32), 0.1, 1.9),
        "input_weight": scatter_about(key_of[4], (D, PROJ), D ** -0.5, 0.125, ((0, 8),)),
        "query_gain": jnp.clip(1.0 + 0.18 * jax.random.normal(key_of[5], (HEAD_DIMENSION,), jnp.float32), 0.1, 1.9),
        "key_gain": jnp.clip(1.0 + 0.18 * jax.random.normal(key_of[6], (HEAD_DIMENSION,), jnp.float32), 0.1, 1.9),
        "output_weight": scatter_about(key_of[7], (QUERY_HEADS * HEAD_DIMENSION, D), (QUERY_HEADS * HEAD_DIMENSION // 256) ** -0.5, 2.0, ((0, 8),)),
        "norm2_gain": jnp.clip(1.0 + 0.18 * jax.random.normal(key_of[8], (D,), jnp.float32), 0.1, 1.9),
        "perceptron_input_weight": scatter_about(key_of[9], (D, 2 * FF), D ** -0.5, 0.125, ((0, 8),)),
        "down_weight": scatter_about(key_of[10], (FF, D), FF ** -0.5, 0.078125, ((0, 8),)),
    }


@jax.custom_vjp
def low(v):
    return lax.optimization_barrier(v.astype(jnp.bfloat16)).astype(jnp.float32)

@jax.custom_vjp
def low_back(v):
    return v

def low_keep(v):
    return (low(v), None)

def low_pass(kept, grad):
    return (grad,)

def back_keep(v):
    return (v, None)

def back_low(kept, grad):
    return (low(grad),)
low.defvjp(low_keep, low_pass)
low_back.defvjp(back_keep, back_low)
EPSILON = 1e-06
ROPE_BASE = 1000000.0
TOP_PRECISION = lax.Precision.HIGHEST

def rms_scale(values):
    return lax.rsqrt(lax.optimization_barrier(jnp.mean(values * values, axis=-1, keepdims=True)) + EPSILON)

def rope_tables(positions, head_size):
    half_size = head_size // 2
    frequency = ROPE_BASE ** (-2.0 * jnp.arange(half_size).astype(jnp.float32) / head_size)
    angles = positions.astype(jnp.float32)[:, None] * frequency[None, :]
    return (jnp.cos(angles), jnp.sin(angles))

def rotate(values, cosine, sine):
    half_size = values.shape[-1] // 2
    front = values[..., :half_size]
    behind = values[..., half_size:]
    return jnp.concatenate([front * cosine - behind * sine, behind * cosine + front * sine], axis=-1)

def attend(queries, keys, values, lengths):
    sequence_count, bucket_size, head_count, head_size = queries.shape
    head_copies = head_count // keys.shape[2]
    keys_all = jnp.repeat(keys, head_copies, axis=2)
    values_all = jnp.repeat(values, head_copies, axis=2)
    block_rows = min(512, bucket_size)
    block_count = bucket_size // block_rows
    key_index = jnp.arange(bucket_size)
    score_scale = head_size ** (-0.5)
    blocks = queries.reshape(sequence_count, block_count, block_rows, head_count, head_size).transpose(1, 0, 2, 3, 4)
    starts = jnp.arange(block_count) * block_rows

    def one_block(inputs):
        query_block, first_row = inputs
        query_index = first_row + jnp.arange(block_rows)
        scores = low_back(score_scale * jnp.einsum('sqhd,skhd->shqk', query_block, keys_all, precision=TOP_PRECISION))
        causal = (key_index[None, :] <= query_index[:, None])[None, None]
        within = (key_index[None, :] < lengths[:, None])[:, None, None, :]
        scores = jnp.where(causal & within, scores, -1e+30)
        row_top = lax.optimization_barrier(jnp.max(scores, axis=-1, keepdims=True))
        log_total = row_top + jnp.log(lax.optimization_barrier(jnp.sum(jnp.exp(scores - row_top), axis=-1, keepdims=True)))
        soft_weights = low(jnp.exp(scores - log_total))
        return jnp.einsum('shqk,skhd->sqhd', soft_weights, values_all, precision=TOP_PRECISION)
    outputs = lax.map(jax.checkpoint(one_block), (blocks, starts))
    return outputs.transpose(1, 0, 2, 3, 4).reshape(sequence_count, bucket_size, head_count, head_size)

def layer_forward(inputs, lengths, cosine, sine, norm1_gain, input_weight, query_gain, key_gain, output_weight, norm2_gain, perceptron_input_weight, down_weight):
    sequence_count, bucket_size, model_width = inputs.shape
    query_width = QUERY_HEADS * HEAD_DIMENSION
    key_value_width = KEY_VALUE_HEADS * HEAD_DIMENSION
    normalized_input = low(inputs * rms_scale(inputs) * norm1_gain)
    projected_output = low_back(jnp.einsum('aiv,vn->ain', normalized_input, input_weight, precision=TOP_PRECISION))
    query_raw = projected_output[..., :query_width].reshape(sequence_count, bucket_size, QUERY_HEADS, HEAD_DIMENSION)
    key_unrotated = projected_output[..., query_width:query_width + key_value_width].reshape(sequence_count, bucket_size, KEY_VALUE_HEADS, HEAD_DIMENSION)
    value_unprojected = projected_output[..., query_width + key_value_width:query_width + 2 * key_value_width].reshape(sequence_count, bucket_size, KEY_VALUE_HEADS, HEAD_DIMENSION)
    gate_raw = projected_output[..., query_width + 2 * key_value_width:]
    queries = low_back(low(rotate(query_raw * rms_scale(query_raw) * query_gain, cosine, sine)))
    keys = low_back(low(rotate(key_unrotated * rms_scale(key_unrotated) * key_gain, cosine, sine)))
    values = low_back(low(value_unprojected))
    attended = low_back(low(attend(queries, keys, values, lengths)))
    gated_product = low(attended.reshape(sequence_count, bucket_size, query_width) * jax.nn.sigmoid(gate_raw))
    branch_output = low_back(jnp.einsum('hzm,mw->hzw', gated_product, output_weight, precision=TOP_PRECISION))
    hidden_in = inputs + branch_output
    second_normalized = low(hidden_in * rms_scale(hidden_in) * norm2_gain)
    gate_up_product = low_back(jnp.einsum('hmr,rz->hmz', second_normalized, perceptron_input_weight, precision=TOP_PRECISION))
    hidden_state = low(jax.nn.silu(gate_up_product[..., :FF]) * gate_up_product[..., FF:])
    mixed_output = low_back(jnp.einsum('zbo,oh->zbh', hidden_state, down_weight, precision=TOP_PRECISION))
    return hidden_in + mixed_output

def reference(tokens, seq_lengths, cotangent, norm1_gain, input_weight, query_gain, key_gain, output_weight, norm2_gain, perceptron_input_weight, down_weight):
    group_count = NSEQ // SEQS_G
    cosine, sine = rope_tables(jnp.arange(BUCKET), HEAD_DIMENSION)
    cosine = cosine[None, :, None, :]
    sine = sine[None, :, None, :]
    weights = (norm1_gain.astype(jnp.float32), input_weight.astype(jnp.float32), query_gain.astype(jnp.float32), key_gain.astype(jnp.float32), output_weight.astype(jnp.float32), norm2_gain.astype(jnp.float32), perceptron_input_weight.astype(jnp.float32), down_weight.astype(jnp.float32))
    token_groups = tokens.reshape(group_count, SEQS_G, BUCKET, D)
    cot_groups = cotangent.reshape(group_count, SEQS_G, BUCKET, D)
    length_groups = seq_lengths.reshape(group_count, SEQS_G)
    slot_index = jnp.arange(BUCKET)

    def one_group(totals, group_item):
        group_tokens, group_cot, group_lengths = group_item

        def forward(inputs, *params):
            return layer_forward(inputs, group_lengths, cosine, sine, *params)
        result, pullback = jax.vjp(forward, group_tokens.astype(jnp.float32), *weights)
        live_rows = (slot_index[None, :] < group_lengths[:, None]).astype(jnp.float32)[..., None]
        gradients = pullback(group_cot.astype(jnp.float32) * live_rows)
        totals = tuple((running + fresh for running, fresh in zip(totals, gradients[1:])))
        return (totals, (result, gradients[0]))
    initial = tuple((jnp.zeros_like(weight) for weight in weights))
    totals, (results, token_grads) = lax.scan(one_group, initial, (token_groups, cot_groups, length_groups))
    return (results.reshape(NSEQ, BUCKET, D), token_grads.reshape(NSEQ, BUCKET, D), totals[0], totals[1], totals[2], totals[3], totals[4], totals[5], totals[6], totals[7])
```

```python
import functools

import jax
import jax.numpy as jnp
import numpy as np
from jax import lax
from jax.experimental import pallas as pl
from jax.experimental.pallas import tpu as pltpu
from jax.sharding import PartitionSpec as P

QUERY_HEADS = 16
KEY_VALUE_HEADS = 8
HEAD_DIMENSION = 128
FF = 6144


EPSILON = 1e-06
ROPE_BASE = 1000000.0
MASKED = -1e30


def rms_scale(values):
    return lax.rsqrt(jnp.mean(values * values, axis=-1, keepdims=True) + EPSILON)


VMEM_LIMIT = 56 * 1024 * 1024
NT = (((1,), (1,)), ((), ()))
TN = (((0,), (0,)), ((), ()))


def params():
    return pltpu.CompilerParams(vmem_limit_bytes=VMEM_LIMIT)


def cost(*_):
    return pl.CostEstimate(flops=1, bytes_accessed=1, transcendentals=0)


def steady(shape):
    return pl.BlockSpec(shape, lambda *_: (0,) * len(shape), pipeline_mode=pl.Buffered(1))


def tile_of(size):
    return 256 if size % 256 == 0 else 128


def head_scale(raw):
    return lax.rsqrt(jnp.mean(raw * raw, axis=-1, keepdims=True) + EPSILON)


def turn_pairs(value, cosine, sine):
    return value * cosine + pltpu.roll(value, HEAD_DIMENSION // 2, 1) * sine


def masked_scores(q, k, first_row, length):
    scores = lax.dot_general(q, k, NT, preferred_element_type=jnp.float32)
    scores = scores * HEAD_DIMENSION ** (-0.5)
    row = first_row + lax.broadcasted_iota(jnp.int32, scores.shape, 0)
    column = lax.broadcasted_iota(jnp.int32, scores.shape, 1)
    return jnp.where((column <= row) & (column < length), scores, MASKED)


def in_order(ref, me):
    return jnp.concatenate([ref[me ^ t] for t in range(ref.shape[0])], axis=0)


def attend_back_kernel(
    block, copies, heads, kv_heads, place_ref, q_raw, k_raw, q_ref, k_ref, v_ref, gate_ref, attended_ref, up_ref,
    total_ref, q_gain, k_gain, cosine, sine, qk_out, vg_out, q_gain_out, k_gain_out, grad_ref, dq_ref, dk_ref, dv_ref,
):
    group = pl.program_id(0)
    bucket, size = k_ref.shape
    n_u, rows_own, _ = q_raw.shape
    scale = size ** (-0.5)
    length, me = place_ref[0], place_ref[1]

    @pl.when(group == 0)
    def _():
        q_gain_out[...] = jnp.zeros_like(q_gain_out)
        k_gain_out[...] = jnp.zeros_like(k_gain_out)

    def store(out, at, width, value):
        for t in range(n_u):
            out[me ^ t, :, pl.ds(pl.multiple_of(at, size), width)] = value[t * rows_own : (t + 1) * rows_own]

    up, gate = in_order(up_ref, me), gate_ref[...]
    grad_ref[...] = (up * gate).astype(jnp.bfloat16)
    grad_gate = (up * attended_ref[...].astype(jnp.float32) * gate * (1.0 - gate)).astype(jnp.bfloat16)
    store(vg_out, (kv_heads + group * copies) * size, copies * size, grad_gate)
    dk_ref[...] = jnp.zeros_like(dk_ref)
    dv_ref[...] = jnp.zeros_like(dv_ref)

    def norm_grad(raw, gain, upstream, gain_out):
        factor = head_scale(raw)
        weighted = upstream * gain
        inner = jnp.mean(weighted * raw, axis=-1, keepdims=True)
        gain_out[...] += jnp.sum(upstream * raw * factor, axis=0, keepdims=True)
        return (factor * weighted - raw * (factor * factor * factor) * inner).astype(jnp.bfloat16)

    raw_q = in_order(q_raw, me)
    for copy in range(copies):
        columns = slice(copy * size, (copy + 1) * size)
        for first in range(0, bucket, block):
            rows = slice(first, first + block)
            reach = slice(0, first + block)
            q, g = q_ref[rows, columns], grad_ref[rows, columns]
            soft = jnp.exp(masked_scores(q, k_ref[reach], first, length) - total_ref[copy, rows])
            soft_grad = lax.dot_general(g, v_ref[reach], NT, preferred_element_type=jnp.float32)
            inner = jnp.sum(soft * soft_grad, axis=-1, keepdims=True)
            score_grad = (soft * (soft_grad - inner)).astype(jnp.bfloat16)
            dq_ref[rows] = jnp.dot(score_grad, k_ref[reach], preferred_element_type=jnp.float32) * scale
            dk_ref[reach] += lax.dot_general(score_grad, q, TN, preferred_element_type=jnp.float32)
            dv_ref[reach] += lax.dot_general(soft.astype(jnp.bfloat16), g, TN, preferred_element_type=jnp.float32)
        plain = turn_pairs(dq_ref[...].astype(jnp.bfloat16).astype(jnp.float32), cosine[...], -sine[...])
        store(qk_out, (group * copies + copy) * size, size, norm_grad(raw_q[:, columns], q_gain[...], plain, q_gain_out))
    plain = turn_pairs((dk_ref[...] * scale).astype(jnp.bfloat16).astype(jnp.float32), cosine[...], -sine[...])
    store(qk_out, (heads + group) * size, size, norm_grad(in_order(k_raw, me), k_gain[...], plain, k_gain_out))
    store(vg_out, group * size, size, dv_ref[...].astype(jnp.bfloat16))


def attend_back(place, raw_qk, q, k, v, gate, attended, upstream, totals, q_gain, k_gain, cosine, sine):
    size = HEAD_DIMENSION
    n_u, rows_own, _ = raw_qk.shape
    bucket = n_u * rows_own
    heads, kv_heads = q.shape[1] // size, k.shape[1] // size
    copies = heads // kv_heads

    def blocks(width, start):
        return pl.BlockSpec((n_u, rows_own, width), lambda g: (0, 0, start + g))

    wide = pl.BlockSpec((bucket, copies * size), lambda g: (0, g))
    slim = pl.BlockSpec((bucket, size), lambda g: (0, g))
    total = (heads + kv_heads) * size
    whole = pl.BlockSpec((n_u, rows_own, total), lambda g: (0, 0, 0))
    gain = pl.BlockSpec((1, size), lambda g: (0, 0))
    return pl.pallas_call(
        functools.partial(attend_back_kernel, min(256, bucket), copies, heads, kv_heads),
        grid=(kv_heads,),
        in_specs=[
            pl.BlockSpec(memory_space=pltpu.SMEM),
            blocks(copies * size, 0),
            blocks(size, heads),
            wide,
            slim,
            slim,
            wide,
            wide,
            blocks(copies * size, 0),
            pl.BlockSpec((copies, bucket, 1), lambda g: (g, 0, 0)),
            steady((1, size)),
            steady((1, size)),
            steady((bucket, size)),
            steady((bucket, size)),
        ],
        out_specs=[whole, whole, gain, gain],
        out_shape=[
            jax.ShapeDtypeStruct((n_u, rows_own, total), jnp.bfloat16),
            jax.ShapeDtypeStruct((n_u, rows_own, total), jnp.bfloat16),
            jax.ShapeDtypeStruct((1, size), jnp.float32),
            jax.ShapeDtypeStruct((1, size), jnp.float32),
        ],
        scratch_shapes=[
            pltpu.VMEM((bucket, copies * size), jnp.bfloat16),
            pltpu.VMEM((bucket, size), jnp.float32),
            pltpu.VMEM((bucket, size), jnp.float32),
            pltpu.VMEM((bucket, size), jnp.float32),
        ],
        compiler_params=params(),
        cost_estimate=cost(5 * heads * bucket * bucket * size, 24 * bucket * heads * size, heads * bucket * bucket // 2),
        name="attention_back",
    )(place, raw_qk, raw_qk, q, k, v, gate, attended, upstream, totals, q_gain, k_gain, cosine, sine)


def gate_up(x, first, second):
    m, width = x.shape
    n = first.shape[1]
    tile = tile_of(n)
    step_rows = min(256, m)

    def kernel(x_ref, first_ref, second_ref, a_out, b_out, hidden_out):
        for at in range(0, m, step_rows):
            rows = slice(at, at + step_rows)
            a = jnp.dot(x_ref[rows], first_ref[...], preferred_element_type=jnp.float32)
            b = jnp.dot(x_ref[rows], second_ref[...], preferred_element_type=jnp.float32)
            a_out[rows] = a
            b_out[rows] = b
            hidden_out[rows] = (a * jax.nn.sigmoid(a) * b).astype(jnp.bfloat16)

    weight = pl.BlockSpec((width, tile), lambda j: (0, j))
    out = pl.BlockSpec((m, tile), lambda j: (0, j))
    return pl.pallas_call(
        kernel,
        grid=(n // tile,),
        in_specs=[steady((m, width)), weight, weight],
        out_specs=[out] * 3,
        out_shape=[jax.ShapeDtypeStruct((m, n), d) for d in (jnp.float32, jnp.float32, jnp.bfloat16)],
        compiler_params=params(),
        cost_estimate=cost(),
        name="gate_up",
    )(x, first, second)


def back_matmul(a, b, first, second, rows):
    m, n = a.shape
    width = first.shape[0]
    part = 256

    def kernel(a_ref, b_ref, first_ref, second_ref, keep_ref, send_ref):
        for at in range(0, width, part):
            where = slice(at, at + part)
            out = lax.dot_general(a_ref[...], first_ref[where], NT, preferred_element_type=jnp.float32)
            out += lax.dot_general(b_ref[...], second_ref[where], NT, preferred_element_type=jnp.float32)
            out = out.astype(jnp.bfloat16)
            keep_ref[0, :, where] = out[:rows]
            send_ref[0, :, where] = out[rows:]

    step = pl.BlockSpec((2 * rows, n), lambda i: (i, 0))
    out = pl.BlockSpec((1, rows, width), lambda i: (i, 0, 0))
    shape = jax.ShapeDtypeStruct((m // rows // 2, rows, width), jnp.bfloat16)
    return pl.pallas_call(
        kernel,
        grid=(m // rows // 2,),
        in_specs=[step, step, steady(first.shape), steady(second.shape)],
        out_specs=[out, out],
        out_shape=[shape, shape],
        compiler_params=params(),
        cost_estimate=cost(),
        name="back_matmul",
    )(a, b, first, second)


def outer_terms(x, y, count):
    m, width = x.shape
    n = y.shape[1]
    depth = width // count

    def kernel(x_ref, y_ref, out_ref):
        out_ref[...] = lax.dot_general(x_ref[...], y_ref[...], TN, preferred_element_type=jnp.float32).astype(jnp.bfloat16)

    return pl.pallas_call(
        kernel,
        grid=(count,),
        in_specs=[pl.BlockSpec((m, depth), lambda k: (0, k)), steady((m, n))],
        out_specs=pl.BlockSpec((depth, n), lambda k: (k, 0)),
        out_shape=jax.ShapeDtypeStruct((width, n), jnp.bfloat16),
        compiler_params=params(),
        cost_estimate=cost(2 * m * n * width, 2 * m * width + 2 * m * n + 2 * n * width),
        name="outer_terms",
    )(x, y)


def down_back(upstream, a, b, weight):
    m, width = upstream.shape
    n = a.shape[1]
    rows = min(256, m)

    def kernel(up_ref, a_ref, b_ref, weight_ref, gate_out, up_out):
        grad = lax.dot_general(up_ref[...], weight_ref[...], NT, preferred_element_type=jnp.float32)
        a, b = a_ref[...], b_ref[...]
        sig = jax.nn.sigmoid(a)
        gate_out[...] = (grad * b * sig * (1.0 + a * (1.0 - sig))).astype(jnp.bfloat16)
        up_out[...] = (grad * a * sig).astype(jnp.bfloat16)

    step = pl.BlockSpec((rows, n), lambda i: (i, 0))
    shape = jax.ShapeDtypeStruct((m, n), jnp.bfloat16)
    return pl.pallas_call(
        kernel,
        grid=(m // rows,),
        in_specs=[pl.BlockSpec((rows, width), lambda i: (i, 0)), step, step, steady((n, width))],
        out_specs=[step, step],
        out_shape=[shape, shape],
        compiler_params=params(),
        cost_estimate=cost(2 * m * n * width, 2 * m * width + 12 * m * n + 2 * n * width),
        name="down_back",
    )(upstream, a, b, weight)


def strips_kernel(n_dp, n_u, strip, place_ref, w_ref, gate_ref, up_ref):
    for t in range(n_u):

        @pl.when(place_ref[1] == t)
        def _():
            for half, out in enumerate((gate_ref, up_ref)):
                starts = [((half * n_dp + b) * n_u + t) * strip for b in range(n_dp)]
                out[...] = jnp.concatenate([w_ref[:, s : s + strip] for s in starts], axis=1)


def take_strips(place, w, n_dp, n_u, strip):
    depth, total = w.shape
    rows = 64
    out = pl.BlockSpec((rows, n_dp * strip), lambda i: (i, 0))
    shape = jax.ShapeDtypeStruct((depth, n_dp * strip), w.dtype)
    return pl.pallas_call(
        functools.partial(strips_kernel, n_dp, n_u, strip),
        grid=(depth // rows,),
        in_specs=[pl.BlockSpec(memory_space=pltpu.SMEM), pl.BlockSpec((rows, total), lambda i: (i, 0))],
        out_specs=[out, out],
        out_shape=[shape, shape],
        compiler_params=params(),
        cost_estimate=cost(0, 2 * depth * total + 4 * depth * n_dp * strip),
        name="take_strips",
    )(place, w)


def fill(scratch, keys, refs):
    for key_list, ref in zip(keys, refs):
        for at, key in enumerate(key_list):
            scratch[key] = ref[at]


def put_call(kernel, place, helds, grid, blocks, at, out_block, out_at, out_shape, name):
    n_u = sum(len(k) for k in helds[0][0])
    count = sum(len(b) for _, b in helds)

    def body(place_ref, *refs):
        refs = list(refs)
        scratches = refs[count + 1 :]
        for (keys, _), scratch in zip(helds, scratches):
            fill(scratch, keys, [refs.pop(0) for _ in keys])
        kernel(place_ref[1], scratches, refs[0])

    return pl.pallas_call(
        body,
        grid=(grid,),
        in_specs=[pl.BlockSpec(memory_space=pltpu.SMEM)]
        + [pl.BlockSpec((len(k),) + block, at) for (keys, _), block in zip(helds, blocks) for k in keys],
        out_specs=pl.BlockSpec(out_block, out_at),
        out_shape=jax.ShapeDtypeStruct(out_shape, jnp.float32),
        scratch_shapes=[pltpu.VMEM((n_u,) + block, jnp.bfloat16) for block in blocks],
        compiler_params=params(),
        cost_estimate=cost(0, 6 * out_shape[0] * out_shape[1]),
        name=name,
    )(place, *[v for _, held in helds for v in held])


def put_strips(place, helds, n_dp, strip):
    n_u = sum(len(k) for k in helds[0][0])
    depth, width = helds[0][1][0].shape[1:]
    rows = min(32, depth)

    def kernel(me, scratches, out_ref):
        size = n_u * strip
        for h, scratch in enumerate(scratches):
            parts = [scratch[me ^ t].astype(jnp.float32) for t in range(n_u)]
            for b in range(n_dp):
                at = (h * n_dp + b) * size
                out_ref[:, at : at + size] = jnp.concatenate(
                    [p[:, b * strip : (b + 1) * strip] for p in parts], axis=1
                )

    total = len(helds) * n_u * width
    return put_call(
        kernel, place, helds, depth // rows, [(rows, width)] * len(helds), lambda i: (0, i, 0),
        (rows, total), lambda i: (i, 0), (depth, total), "put_strips",
    )


def put_columns(place, helds, sections):
    n_u = sum(len(k) for k in helds[0][0])
    depth = helds[0][1][0].shape[1]
    rows = min(64, depth)

    def kernel(me, scratches, out_ref):
        at = 0
        for scratch, parts in zip(scratches, sections):
            for start, size in parts:
                for t in range(n_u):
                    out_ref[:, at : at + size] = scratch[me ^ t, :, start : start + size].astype(jnp.float32)
                    at += size

    total = n_u * sum(size for parts in sections for _, size in parts)
    return put_call(
        kernel, place, helds, depth // rows, [(rows, held[0].shape[2]) for _, held in helds], lambda i: (0, i, 0),
        (rows, total), lambda i: (i, 0), (depth, total), "put_columns",
    )


def put_rows(place, held):
    n_u = sum(len(k) for k in held[0])
    depth, width = held[1][0].shape[1:]
    tile = 512

    def kernel(me, scratches, out_ref):
        for t in range(n_u):
            out_ref[t * depth : (t + 1) * depth] = scratches[0][me ^ t].astype(jnp.float32)

    return put_call(
        kernel, place, [held], width // tile, [(depth, tile)], lambda i: (0, 0, i),
        (n_u * depth, tile), lambda i: (0, i), (n_u * depth, width), "put_rows",
    )


def norm_call(kernel, inputs, gain, outs, gain_sum, name):
    r, width = inputs[0].shape
    tile = min(64, r)
    step = pl.BlockSpec((tile, width), lambda i: (i, 0))
    one = pl.BlockSpec((1, width), lambda i: (0, 0))
    shapes = [jax.ShapeDtypeStruct((r, width), o) for o in outs]
    if gain_sum:
        shapes.append(jax.ShapeDtypeStruct((1, width), jnp.float32))
    return pl.pallas_call(
        kernel,
        grid=(r // tile,),
        in_specs=[step] * len(inputs) + [one],
        out_specs=[step] * len(outs) + [one] * gain_sum,
        out_shape=shapes,
        compiler_params=params(),
        cost_estimate=cost(0, sum(4 * v.size for v in inputs)),
        name=name,
    )(*inputs, gain)


def norm_back(source, keep, got, residual, gain, rounded):
    def kernel(source_ref, keep_ref, got_ref, residual_ref, gain_ref, *outs):
        @pl.when(pl.program_id(0) == 0)
        def _():
            outs[-1][...] = jnp.zeros_like(outs[-1])

        up = keep_ref[...] + got_ref[...].astype(jnp.float32)
        source = source_ref[...].astype(jnp.float32)
        factor = head_scale(source)
        weighted = up * gain_ref[...]
        inner = jnp.mean(weighted * source, axis=-1, keepdims=True)
        total = residual_ref[...].astype(jnp.float32) + factor * weighted
        total = total - source * (factor * factor * factor) * inner
        outs[0][...] = total
        if rounded:
            outs[1][...] = total.astype(jnp.bfloat16)
        outs[-1][...] += jnp.sum(up * source * factor, axis=0, keepdims=True)

    outs = [jnp.float32] + [jnp.bfloat16] * rounded
    return norm_call(kernel, (source, keep, got, residual), gain, outs, 1, "norm_back")


def halve(keep, got):
    pairs, (r, c) = keep.shape[0] // 2, keep.shape[1:]
    tile = min(64, r)

    def kernel(keep_ref, got_ref, even_ref, odd_ref):
        even_ref[0] = keep_ref[0].astype(jnp.float32) + got_ref[0].astype(jnp.float32)
        odd_ref[0] = (keep_ref[1].astype(jnp.float32) + got_ref[1].astype(jnp.float32)).astype(jnp.bfloat16)

    two = pl.BlockSpec((2, tile, c), lambda p, i: (p, i, 0))
    one = pl.BlockSpec((1, tile, c), lambda p, i: (p, i, 0))
    return pl.pallas_call(
        kernel,
        grid=(pairs, r // tile),
        in_specs=[two, two],
        out_specs=[one, one],
        out_shape=[jax.ShapeDtypeStruct((pairs, r, c), jnp.float32), jax.ShapeDtypeStruct((pairs, r, c), jnp.bfloat16)],
        compiler_params=params(),
        cost_estimate=cost(0, 16 * pairs * r * c),
        name="halve",
    )(keep, got)


def out_terms(place, gated, upstream, n_u):
    m, q = gated.shape
    c = upstream.shape[1] // n_u

    def kernel(place_ref, x_ref, y_ref, out_ref):
        out_ref[0] = lax.dot_general(x_ref[...], y_ref[...], TN, preferred_element_type=jnp.float32).astype(jnp.bfloat16)

    return pl.pallas_call(
        kernel,
        grid_spec=pltpu.PrefetchScalarGridSpec(
            num_scalar_prefetch=1,
            grid=(n_u,),
            in_specs=[
                pl.BlockSpec((m, q), lambda k, p: (0, 0)),
                pl.BlockSpec((m, c), lambda k, p: (0, p[1] ^ k)),
            ],
            out_specs=pl.BlockSpec((1, q, c), lambda k, p: (k, 0, 0)),
        ),
        out_shape=jax.ShapeDtypeStruct((n_u, q, c), jnp.bfloat16),
        compiler_params=params(),
        cost_estimate=cost(2 * m * q * c * n_u, 2 * m * q + 4 * m * c * n_u),
        name="out_terms",
    )(place, gated, upstream)


MESH = pl.DeviceIdType.MESH


class Group:
    def __init__(self, n_dp, n_u):
        self.n_dp, self.n_u = n_dp, n_u
        index = lax.axis_index("dp")
        self.me = lax.axis_index("ulysses")
        odd = index % 2
        self.position = (1 - odd) * (index // 2) + odd * (n_dp - 1 - index // 2)
        self.next = (self.owner(1), self.owner(-1))
        self.bits = [1 << k for k in range(n_u.bit_length() - 1)]

    def owner(self, offset):
        place = (self.position + offset + self.n_dp) % self.n_dp
        late = place // (self.n_dp // 2)
        return (1 - late) * (2 * place) + late * (2 * (self.n_dp - 1 - place) + 1)

    def greet(self):
        barrier = pltpu.get_barrier_semaphore()
        for way in (0, 1):
            pl.semaphore_signal(barrier, inc=1, device_id={"dp": self.next[way]}, device_id_type=MESH)
        for other in range(1, self.n_u):
            pl.semaphore_signal(barrier, inc=1, device_id={"ulysses": self.me ^ other}, device_id_type=MESH)
        pl.semaphore_wait(barrier, 1 + self.n_u)

    def to_ring(self, way, source, target, send, recv):
        copy = pltpu.make_async_remote_copy(
            src_ref=source, dst_ref=target, send_sem=send, recv_sem=recv,
            device_id={"dp": self.next[way]}, device_id_type=MESH,
        )
        copy.start()
        return copy

    def to_cube(self, bit, source, target, send, recv):
        copy = pltpu.make_async_remote_copy(
            src_ref=source, dst_ref=target, send_sem=send, recv_sem=recv,
            device_id={"ulysses": self.me ^ bit}, device_id_type=MESH,
        )
        copy.start()
        return copy

    def reach(self, more_ahead):
        longer = self.n_dp // 2
        shorter = self.n_dp - 1 - longer
        return (longer, shorter) if more_ahead else (shorter, longer)


class Spread:
    def __init__(self, group, own, out, send, recv):
        self.group, self.own, self.out, self.send, self.recv = group, own, out, send, recv
        self.keys, self.levels, self.copies, self.used, self.waited = [0], group.bits[::-1], [], 0, 0

    def level(self):
        for copy in self.copies[self.waited :]:
            copy.wait_recv()
        self.waited = len(self.copies)
        if not self.levels:
            return False
        bit = self.levels.pop(0)
        for key in sorted(self.keys):
            source = self.own if key == 0 else self.out.at[key]
            at = self.used
            self.copies.append(
                self.group.to_cube(bit, source, self.out.at[key ^ bit], self.send.at[at], self.recv.at[at])
            )
            self.used += 1
        self.keys += [key ^ bit for key in self.keys]
        return True

    def finish(self):
        while self.level():
            pass
        for copy in self.copies:
            copy.wait_send()


class RingGather:
    def __init__(self, group, chains, send, recv):
        self.group, self.chains, self.send_sems, self.recv_sems = group, chains, send, recv
        self.copies = {}

    def place(self, c, owner):
        _, out, block, low, rows, _ = self.chains[c]
        return out.at[pl.ds(pl.multiple_of(owner * block + low, 16), rows)]

    def item(self, c):
        item, _, _, low, rows, _ = self.chains[c]
        return item.at[low : low + rows]

    def reach(self, c, way):
        return self.group.reach(self.chains[c][5])[way]

    def send(self, c, way, step):
        owner = self.group.owner(1 - step if way == 0 else step - 1)
        source = self.item(c) if step == 1 else self.place(c, owner)
        sems = (c, way, step - 1)
        self.copies[sems] = self.group.to_ring(
            way, source, self.place(c, owner), self.send_sems.at[sems], self.recv_sems.at[sems]
        )

    def start(self, c):
        for way in (0, 1):
            self.send(c, way, 1)

    def event(self, c, way, step):
        if step <= self.reach(c, way):
            self.copies[c, way, step - 1].wait_recv()
            if step < self.reach(c, way):
                self.send(c, way, step + 1)

    def finish(self):
        for copy in self.copies.values():
            copy.wait_send()


def by_rows(count, tile, function):
    def body(i, carry):
        function(pl.ds(pl.multiple_of(i * tile, tile), tile))
        return carry

    lax.fori_loop(0, count // tile, body, 0)


def forward_kernel(
    n_dp, n_u, heads, kv_heads, length_ref, tokens_ref, gain_one, gain_two, q_gain, k_gain, cosine, sine, grad_ref,
    out_item, qk_item, vg_item, gate_item, up_item, down_item,
    w_qk, w_vg, w_gate, w_up, w_down, normed_out, grad_out, second_out,
    raw_qk, raw_vg, q_out, k_out, v_out, gate_out, attended_out, gated_out, total_out, w_out, hidden_out,
    normed, own, qk_local, vg_local, columns, turned, parts, core_got, total, second_own,
    ring_send, ring_recv, cube_send, cube_recv, turn_send, turn_recv, sum_send, sum_recv, local,
):
    rows_own, width = tokens_ref.shape
    bucket = rows_own * n_u
    size = HEAD_DIMENSION
    copies = heads // kv_heads
    depth = width // n_dp
    group = Group(n_dp, n_u)
    me, mine = group.me, group.owner(0)
    group.greet()
    strip = down_item.shape[0]
    halves = 2 if strip % 32 == 0 else 1
    chains = [
        (out_item, columns, depth, 0, depth, True),
        (qk_item, w_qk, depth, 0, depth, False),
        (vg_item, w_vg, depth, 0, depth, True),
        (gate_item, w_gate, depth, 0, depth, True),
        (up_item, w_up, depth, 0, depth, False),
    ]
    for p in range(halves):
        chains.append((down_item, w_down, strip, p * strip // halves, strip // halves, p == 0))
    ring = RingGather(group, chains, ring_send, ring_recv)
    kept = []

    def keep(source, target):
        copy = pltpu.make_async_copy(source, target, local.at[len(kept)])
        copy.start()
        kept.append(copy)
        return copy

    for c in (0, 1, 2):
        ring.start(c)
    own_rows = lambda out, block: out.at[pl.ds(pl.multiple_of(mine * block, 16), block)]
    for item, out, block in (
        (out_item, columns, depth), (qk_item, w_qk, depth), (vg_item, w_vg, depth),
        (gate_item, w_gate, depth), (up_item, w_up, depth), (down_item, w_down, strip),
    ):
        keep(item, own_rows(out, block))

    def first(rows):
        x = tokens_ref[rows].astype(jnp.float32)
        own[rows] = (x * head_scale(x) * gain_one[...]).astype(jnp.bfloat16)

    by_rows(rows_own, 64, first)
    keep(own, normed.at[0]).wait()
    keep(grad_ref, grad_out.at[0])
    spreads = [
        Spread(group, own, normed, cube_send.at[0], cube_recv.at[0]),
        Spread(group, grad_ref, grad_out, cube_send.at[1], cube_recv.at[1]),
    ]
    spreads[0].level()
    longest = n_dp // 2
    for step in range(1, longest + 1):
        for c in (0, 1, 2):
            for way in (0, 1):
                ring.event(c, way, step)
        if step == 1:
            spreads[1].level()
        if step < longest:
            spreads[0 if step % 2 == 1 else 1].level()
        if step == longest - 1:
            for c in (3, 4):
                ring.start(c)
    spreads[0].finish()
    events = []
    for step in range(1, longest + 1):
        events += [[(3, 0, step), (4, 1, step)], [(4, 0, step), (3, 1, step)]]
        if step == longest - 1:
            events.append([("start",)])
    for step in range(1, longest + 1):
        if halves == 2:
            events += [[(5, 0, step), (6, 1, step)], [(6, 0, step), (5, 1, step)]]
        else:
            events += [[(5, 0, step), (5, 1, step)]]

    def pump(count=1):
        while count and events:
            pair = events.pop(0)
            if pair[0][0] == "start":
                for c in range(5, len(chains)):
                    ring.start(c)
                continue
            for event in pair:
                ring.event(*event)
            count -= 1

    for copy in kept[:3]:
        copy.wait()
    share = depth * n_dp // n_u
    turns = []
    for k in range(1, n_u):
        source = columns.at[pl.ds(pl.multiple_of((me ^ k) * share, 16), share)]
        turns.append(group.to_cube(k, source, turned.at[k], turn_send.at[k - 1], turn_recv.at[k - 1]))
    keep(columns.at[pl.ds(pl.multiple_of(me * share, 16), share)], turned.at[0]).wait()
    one, two = keep(w_qk, qk_local), keep(w_vg, vg_local)
    keep(normed, normed_out)
    one.wait()
    two.wait()

    def project(b, carry):
        x = normed[b]
        raw_qk[b] = jnp.dot(x, qk_local[...], preferred_element_type=jnp.float32)
        raw_vg[b] = jnp.dot(x, vg_local[...], preferred_element_type=jnp.float32)
        return carry

    lax.fori_loop(0, n_u, project, 0)
    pump()

    length = length_ref[0]
    block = min(256, bucket)

    def attention(h, carry):
        def column(ref, at):
            at = pl.multiple_of(at * size, size)
            return jnp.concatenate([ref[me ^ t, :, pl.ds(at, size)] for t in range(n_u)], axis=0)

        at = pl.ds(pl.multiple_of(h * size, size), size)
        kv = pl.ds(pl.multiple_of(h // copies * size, size), size)
        q = column(raw_qk, h)
        q = turn_pairs(q * head_scale(q) * q_gain[...], cosine[...], sine[...]).astype(jnp.bfloat16)
        q_out[:, at] = q
        k = column(raw_qk, heads + h // copies)
        k = turn_pairs(k * head_scale(k) * k_gain[...], cosine[...], sine[...]).astype(jnp.bfloat16)
        k_out[:, kv] = k
        v = column(raw_vg, h // copies).astype(jnp.bfloat16)
        v_out[:, kv] = v
        gate = jax.nn.sigmoid(column(raw_vg, kv_heads + h))
        gate_out[:, at] = gate
        for start in range(0, bucket, block):
            rows = slice(start, start + block)
            scores = masked_scores(q[rows], k[: start + block], start, length)
            top = jnp.max(scores, axis=-1, keepdims=True)
            soft = jnp.exp(scores - top)
            sums = jnp.sum(soft, axis=-1, keepdims=True)
            out = jnp.dot(soft.astype(jnp.bfloat16), v[: start + block], preferred_element_type=jnp.float32) / sums
            out = out.astype(jnp.bfloat16)
            attended_out[rows, at] = out
            total_out[h, rows] = top + jnp.log(sums)
            gated = (out.astype(jnp.float32) * gate[rows]).astype(jnp.bfloat16)
            for t in range(start // rows_own, (start + block) // rows_own):
                inside = slice(t * rows_own - start, (t + 1) * rows_own - start)
                gated_out[me ^ t, :, at] = gated[inside]
        return carry

    lax.fori_loop(0, heads, attention, 0)
    pump()
    for copy in turns:
        copy.wait_recv()
    c_width = columns.shape[1]
    for k in range(n_u):
        w_out[:, pl.ds(pl.multiple_of((me ^ k) * c_width, c_width), c_width)] = turned[k]

    def branch(b, carry):
        parts[b] = jnp.dot(gated_out[b], w_out[...], preferred_element_type=jnp.float32).astype(jnp.bfloat16)
        return carry

    lax.fori_loop(0, n_u, branch, 0)
    held = list(range(n_u))
    used = 0
    sums = []
    for bit in group.bits:
        keys = [key for key in held if not key & bit]
        level = []
        for key in keys:
            level.append(
                group.to_cube(bit, parts.at[key | bit], core_got.at[used], sum_send.at[used], sum_recv.at[used])
            )
            used += 1
        sums += level
        pump()
        for at, (key, copy) in enumerate(zip(keys, level)):
            copy.wait_recv()
            slot = used - len(keys) + at

            def add(rows, key=key, slot=slot):
                got = core_got[slot, rows].astype(jnp.float32)
                if key:
                    parts[key, rows] = (parts[key, rows].astype(jnp.float32) + got).astype(jnp.bfloat16)
                elif bit == 1:
                    total[rows] = tokens_ref[rows].astype(jnp.float32) + parts[0, rows].astype(jnp.float32) + got
                else:
                    total[rows] = total[rows] + got

            by_rows(rows_own, 64, add)
        held = keys

    def second(rows):
        hidden = total[rows]
        hidden_out[rows] = hidden
        second_own[rows] = (hidden * head_scale(hidden) * gain_two[...]).astype(jnp.bfloat16)

    by_rows(rows_own, 64, second)
    spread = Spread(group, second_own, second_out, cube_send.at[2], cube_recv.at[2])
    keep(second_own, second_out.at[0])
    while spread.level():
        pump(2)
    spreads[1].finish()
    spread.finish()
    pump(1000)
    ring.finish()
    for copy in turns + sums:
        copy.wait_send()
    for copy in kept[3:6] + kept[7:8] + kept[11:]:
        copy.wait()


def forward(length, tokens_own, gains, tables, grad_own, items, n_dp, n_u, heads, kv_heads):
    anywhere = pl.BlockSpec(memory_space=pl.ANY)
    local = pl.BlockSpec(memory_space=pltpu.VMEM)
    rows, width = tokens_own.shape
    bucket, size = rows * n_u, HEAD_DIMENSION
    total = (heads + kv_heads) * size
    depth = width // n_dp
    columns = items[0].shape[1]
    share = width // n_u
    longest = n_dp // 2

    def shape(*dims, dtype=jnp.bfloat16):
        return jax.ShapeDtypeStruct(dims, dtype)

    out_shape = [shape(n_dp * i.shape[0], i.shape[1]) for i in items[1:]]
    out_shape += [shape(n_u, rows, width)] * 3
    out_shape += [shape(n_u, rows, total, dtype=jnp.float32)] * 2
    out_shape += [
        shape(bucket, heads * size), shape(bucket, kv_heads * size), shape(bucket, kv_heads * size),
        shape(bucket, heads * size, dtype=jnp.float32), shape(bucket, heads * size),
        shape(n_u, rows, heads * size), shape(heads, bucket, 1, dtype=jnp.float32),
        shape(share, width), shape(rows, width, dtype=jnp.float32),
    ]
    dma = pltpu.SemaphoreType.DMA
    return pl.pallas_call(
        functools.partial(forward_kernel, n_dp, n_u, heads, kv_heads),
        in_specs=[pl.BlockSpec(memory_space=pltpu.SMEM)] + [local] * 7 + [anywhere] * 7,
        out_specs=[anywhere] * 8 + [local] * 11,
        out_shape=out_shape,
        scratch_shapes=[
            pltpu.VMEM((n_u, rows, width), jnp.bfloat16),
            pltpu.VMEM((rows, width), jnp.bfloat16),
            pltpu.VMEM((width, total), jnp.bfloat16),
            pltpu.VMEM((width, total), jnp.bfloat16),
            pltpu.VMEM((width, columns), jnp.bfloat16),
            pltpu.VMEM((n_u, share, columns), jnp.bfloat16),
            pltpu.VMEM((n_u, rows, width), jnp.bfloat16),
            pltpu.VMEM((n_u - 1, rows, width), jnp.bfloat16),
            pltpu.VMEM((rows, width), jnp.float32),
            pltpu.VMEM((rows, width), jnp.bfloat16),
            dma((7, 2, longest)), dma((7, 2, longest)), dma((3, n_u - 1)), dma((3, n_u - 1)),
            dma((n_u - 1,)), dma((n_u - 1,)), dma((n_u - 1,)), dma((n_u - 1,)), dma((13,)),
        ],
        compiler_params=pltpu.CompilerParams(vmem_limit_bytes=60 * 1024 * 1024, collective_id=0, has_side_effects=True),
        cost_estimate=cost(),
        name="forward",
    )(length, tokens_own, *gains, *tables, grad_own, *items)


def reduce_kernel(n_dp, n_u, count, blocks_ref, *refs):
    terms, outs = list(refs[: count - 1]), refs[count - 1 : 2 * count - 1]
    refs = refs[2 * count - 1 :]
    slots, sums = refs[:count], refs[count : 2 * count]
    out_terms_ref, ring_send, ring_recv, cube_send, cube_recv, turn_send, turn_recv, local = refs[2 * count :]
    terms.append(out_terms_ref)
    group = Group(n_dp, n_u)
    group.greet()
    copies = {}
    reaches = [group.reach(c % 2 == 0) for c in range(count)]
    longest = n_dp // 2
    share = blocks_ref.shape[1]
    here = out_terms_ref.at[pl.ds(pl.multiple_of(group.me * share, share), share)]

    def add(c, target, offset, others):
        r = target.shape[0]
        tile = 16
        first = group.owner(offset) * r

        def body(i, carry):
            rows = pl.ds(pl.multiple_of(i * tile, tile), tile)
            total = terms[c][pl.ds(pl.multiple_of(first + i * tile, tile), tile)].astype(jnp.float32)
            for other in others:
                total = total + other[rows].astype(jnp.float32)
            target[rows] = total.astype(jnp.bfloat16)
            return carry

        lax.fori_loop(0, r // tile, body, 0)

    def slot(c, way, step):
        return slots[c].at[way, step]

    def send(c, way, step):
        reach = reaches[c][way]
        offset = (reach - step) if way == 0 else (step - reach)
        if step == 0:
            r = sums[c].shape[0]
            source = terms[c].at[pl.ds(pl.multiple_of(group.owner(offset) * r, r), r)]
        else:
            source = slot(c, way, step - 1)
            add(c, source, offset, [source])
        sems = (c, way, step)
        copies[sems] = group.to_ring(way, source, slot(c, way, step), ring_send.at[sems], ring_recv.at[sems])

    def start(chains):
        for c in chains:
            for way in (0, 1):
                send(c, way, 0)

    phases = [(0, 1), (2, 3)]
    start(phases[0])
    turns = []
    for k in range(1, n_u):
        turns.append(group.to_cube(k, blocks_ref.at[k], here, turn_send.at[k - 1], turn_recv.at[k - 1]))
    own = pltpu.make_async_copy(blocks_ref.at[0], here, local.at[count])
    own.start()
    own.wait()
    spreads, kept = [], []
    for phase, chains in enumerate(phases):
        for step in range(longest):
            for c in chains:
                for way in (0, 1):
                    if step < reaches[c][way]:
                        copies[c, way, step].wait_recv()
                        if step + 1 < reaches[c][way]:
                            send(c, way, step + 1)
            if step == longest - 2 and phase == 0:
                for copy in turns:
                    copy.wait_recv()
                start(phases[1])
            if phase == 1 and step % 2 == 1 and step < longest - 1:
                for spread in spreads:
                    spread.level()
            if step == longest - 1:
                for c in chains:
                    add(c, sums[c], 0, [slot(c, way, reaches[c][way] - 1) for way in (0, 1)])
                    spread = Spread(group, sums[c], outs[c], cube_send.at[c], cube_recv.at[c])
                    copy = pltpu.make_async_copy(sums[c], outs[c].at[0], local.at[c])
                    copy.start()
                    kept.append(copy)
                    spread.level()
                    spreads.append(spread)
    for spread in spreads:
        spread.level()
    for spread in spreads:
        spread.finish()
    for copy in list(copies.values()) + turns:
        copy.wait_send()
    for copy in kept:
        copy.wait()


def reduce_all(blocks, terms, n_dp, n_u):
    count = len(terms) + 1
    anywhere = pl.BlockSpec(memory_space=pl.ANY)
    local = pl.BlockSpec(memory_space=pltpu.VMEM)
    longest = n_dp // 2
    whole = (blocks.shape[0] * blocks.shape[1], blocks.shape[2])
    sizes = [(r // n_dp, c) for r, c in [t.shape for t in terms] + [whole]]
    dma = pltpu.SemaphoreType.DMA
    return pl.pallas_call(
        functools.partial(reduce_kernel, n_dp, n_u, count),
        in_specs=[local] * count,
        out_specs=[anywhere] * count,
        out_shape=[jax.ShapeDtypeStruct((n_u,) + b, jnp.bfloat16) for b in sizes],
        scratch_shapes=[pltpu.VMEM((2, longest) + b, jnp.bfloat16) for b in sizes]
        + [pltpu.VMEM(b, jnp.bfloat16) for b in sizes]
        + [
            pltpu.VMEM(whole, jnp.bfloat16),
            dma((count, 2, longest)), dma((count, 2, longest)), dma((count, n_u - 1)), dma((count, n_u - 1)),
            dma((n_u - 1,)), dma((n_u - 1,)), dma((count + 1,)),
        ],
        compiler_params=pltpu.CompilerParams(vmem_limit_bytes=VMEM_LIMIT, collective_id=1, has_side_effects=True),
        cost_estimate=cost(),
        name="reduce_all",
    )(blocks, *terms)


START = 0.9
LATENCY = 2.0
RATES = {"ring": 50.0, "x": 50.0, "core": 250.0}


class Flight:
    def __init__(self, value, arrival):
        self.value, self.arrival = value, arrival


class Sequence:
    def __init__(self):
        self.last = ()
        self.now = 0.0
        self.free = {}
        self.sources = []
        self.fillers = []

    def tie(self, *values):
        tied, _ = lax.optimization_barrier((values, self.last))
        self.last = tied
        return tied

    def run(self, cost, function, *values):
        self.poll()
        out = function(*self.tie(*values))
        self.now += cost
        if isinstance(out, (tuple, list)):
            return self.tie(*out)
        return self.tie(out)[0]

    def fly(self, value, axis, pairs, link, kind):
        (value,) = self.tie(value)
        got = lax.ppermute(value, axis, pairs)
        start = max(self.now + START, self.free.get(link, 0.0))
        end = start + value.size * value.dtype.itemsize / 1000.0 / RATES[kind]
        self.free[link] = end
        self.now += START
        return Flight(got, end + LATENCY)

    def land(self, *flights):
        self.idle(max(f.arrival for f in flights))
        return self.tie(*[f.value for f in flights])

    def poll(self):
        moved = True
        while moved:
            moved = any([source.poll(self.now) for source in self.sources])

    def later(self, cost, ready, function):
        self.fillers.append((cost, ready, function))

    def fill(self):
        for at, (cost, ready, function) in enumerate(self.fillers):
            if ready():
                self.fillers.pop(at)
                function()
                return True
        return False

    def idle(self, until):
        while True:
            self.poll()
            if self.now >= until:
                return
            if until - self.now > 2.0 and self.fill():
                continue
            events = [e for source in self.sources for e in [source.next()] if e is not None]
            self.now = max(self.now, min(events + [until]))

    def drain(self, done):
        while not done():
            self.poll()
            if done():
                return
            if self.fill():
                continue
            events = [e for source in self.sources for e in [source.next()] if e is not None]
            assert events
            self.now = max(self.now, min(events))


def pick(value, index):
    return lax.dynamic_index_in_dim(value, index, 0, keepdims=False, allow_negative_indices=False)


class Cube:
    def __init__(self, axis, seq):
        self.axis = axis
        self.seq = seq
        self.count = lax.axis_size(axis)
        self.me = lax.axis_index(axis)
        bits = []
        bit = 1
        while bit < self.count:
            bits.append(bit)
            bit *= 2
        self.bits = bits

    def swap(self, value, bit):
        kind = "core" if bit == 1 else "x"
        return self.seq.fly(value, self.axis, [(i, i ^ bit) for i in range(self.count)], kind, kind)

    def gather(self, item):
        keys, blocks = [[0]], [item[None]]
        for bit in self.bits[::-1]:
            order = sorted((key, at, sub) for at, ks in enumerate(keys) for sub, key in enumerate(ks))
            if len(order) > 1:
                sent = self.seq.run(
                    2.0, lambda *b: jnp.concatenate([b[at][sub : sub + 1] for _, at, sub in order]), *blocks
                )
            else:
                sent = blocks[0]
            (got,) = yield [self.swap(sent, bit)]
            keys = keys + [[key ^ bit for key, _, _ in order]]
            blocks = blocks + [got]
        return (keys, blocks)

    def joined(self, held):
        keys, blocks = held
        order = sorted((key, at, sub) for at, ks in enumerate(keys) for sub, key in enumerate(ks))
        return self.seq.run(3.0, lambda *b: jnp.concatenate([b[at][sub : sub + 1] for _, at, sub in order]), *blocks)

    def reduce(self, keep, send):
        for bit in self.bits:
            (got,) = yield [self.swap(send, bit)]
            if bit != self.bits[-1]:
                keep, send = self.seq.run(4.4, halve, keep, got)
        return (keep[0], got[0])

    def turn(self, blocks):
        got = yield [self.swap(blocks[bit], bit) for bit in range(1, self.count)]
        return [blocks[0]] + list(got)

    def total(self, value, axes):
        for axis in axes:
            count = lax.axis_size(axis)
            bit = 1
            while bit < count:
                pairs = [(i, i ^ bit) for i in range(count)]
                (got,) = yield [self.seq.fly(value, axis, pairs, "sum", "ring")]
                value = self.seq.run(1.0, lambda a, b: a + b, value, got)
                bit *= 2
        return value


class Task:
    def __init__(self, seq, generator, urgent=True):
        self.seq, self.generator = seq, generator
        self.value, self.flights, self.over, self.busy = None, None, False, False
        seq.sources.append(self)
        self.go(None)

    def go(self, values):
        self.busy = True
        try:
            self.flights = self.generator.send(values)
        except StopIteration as stop:
            self.value, self.over = stop.value, True
            self.seq.sources.remove(self)
        self.busy = False

    def next(self):
        return None if self.busy or self.over else max(f.arrival for f in self.flights)

    def poll(self, now):
        if self.busy or self.over or self.next() > now + 0.5:
            return False
        self.go(self.seq.tie(*[f.value for f in self.flights]))
        return True

    def finish(self):
        while not self.over:
            if self.busy:
                raise RuntimeError
            self.seq.idle(self.next())
        return self.value


def dot(a, b):
    return jnp.einsum("mk,kn->mn", a, b, preferred_element_type=jnp.float32)


def dot_nt(a, b):
    return jnp.einsum("mk,nk->mn", a, b, preferred_element_type=jnp.float32)


def dot_tn(a, b):
    return jnp.einsum("km,kn->mn", a, b, preferred_element_type=jnp.float32)


def low(value):
    return value.astype(jnp.bfloat16)


def high(value):
    return value.astype(jnp.float32)


def shards(
    tokens,
    seq_lengths,
    cotangent,
    norm1_gain,
    input_weight,
    query_gain,
    key_gain,
    output_weight,
    norm2_gain,
    perceptron_input_weight,
    down_weight,
):
    _, rows, width = tokens.shape
    seq = Sequence()
    cube = Cube("ulysses", seq)
    n_dp = lax.axis_size("dp")
    n_u, me = cube.count, cube.me
    bucket = rows * n_u
    depth = width // n_dp
    heads = QUERY_HEADS // n_u
    kv_heads = KEY_VALUE_HEADS // n_u
    copies = QUERY_HEADS // KEY_VALUE_HEADS
    head_width = HEAD_DIMENSION
    q_w, kv_w = heads * head_width, kv_heads * head_width
    query_width = QUERY_HEADS * head_width
    kv_all = KEY_VALUE_HEADS * head_width
    ff_strip = FF // n_dp // n_u
    ff_local = FF // n_u
    half = width // 2
    out_cols = width // n_u
    place = jnp.stack([seq_lengths[0], me])
    length = seq_lengths[0]
    q_gain, k_gain = query_gain[None], key_gain[None]
    gain_one, gain_two = norm1_gain[None], norm2_gain[None]
    positions = me * rows + jnp.arange(rows)
    def cut(value, start, size):
        return lax.dynamic_slice_in_dim(value, start, size, 1)

    def task(generator):
        return Task(seq, generator)

    frequency = np.float32(ROPE_BASE) ** (np.float32(-2.0) * np.arange(head_width // 2, dtype=np.float32) / head_width)
    angles = np.arange(bucket, dtype=np.float32)[:, None] * frequency.astype(np.float32)[None, :]
    cosine, sine = np.cos(angles), np.sin(angles)
    tables = (
        jnp.asarray(np.concatenate([cosine, cosine], axis=1), jnp.float32),
        jnp.asarray(np.concatenate([-sine, sine], axis=1), jnp.float32),
    )

    gate_item, up_item = seq.run(
        4.9, lambda p, w: take_strips(p, w, n_dp, n_u, ff_strip), place, perceptron_input_weight
    )
    out_item, qk_item, vg_item, grad_own, down_item = seq.run(
        3.0,
        lambda o, w, c, d: (
            cut(o, me * out_cols, out_cols),
            jnp.concatenate([cut(w, me * q_w, q_w), cut(w, query_width + me * kv_w, kv_w)], axis=1),
            jnp.concatenate(
                [
                    cut(w, query_width + kv_all + me * kv_w, kv_w),
                    cut(w, query_width + 2 * kv_all + me * q_w, q_w),
                ],
                axis=1,
            ),
            jnp.where((positions < length)[:, None], c, jnp.zeros_like(c)),
            lax.dynamic_slice_in_dim(d, me * ff_strip, ff_strip, 0),
        ),
        output_weight,
        input_weight,
        cotangent[0],
        down_weight,
    )
    (
        w_qk, w_vg, w_gate, w_up, w_down, normed, grad_result, second,
        raw_qk, raw_vg, queries, keys, values, gate, attended, gated, log_totals, w_out, hidden_in,
    ) = seq.run(
        250.0,
        lambda t, g, *items: forward(
            seq_lengths, t, (gain_one, gain_two, q_gain, k_gain), tables, g, items, n_dp, n_u, heads, kv_heads
        ),
        tokens[0], grad_own, out_item, qk_item, vg_item, gate_item, up_item, down_item,
    )
    normed, grad_result = normed.reshape(bucket, width), grad_result.reshape(bucket, width)
    second, gated = second.reshape(bucket, width), gated.reshape(bucket, q_w)

    def even_odd(value):
        value = low(value).reshape(n_u, rows, width)
        return (value[0::2], value[1::2])

    act_gate, act_up, hidden = seq.run(20.0, gate_up, second, w_gate, w_up)
    down_own = lax.psum_scatter(
        seq.run(10.7, lambda h, g: low(dot_tn(h, g)), hidden, grad_result), "dp", scatter_dimension=0, tiled=True
    )

    grad_gate, grad_up = seq.run(15.5, down_back, grad_result, act_gate, act_up, w_down)
    up_own = lax.psum_scatter(
        seq.run(12.5, lambda a, b: outer_terms(a, b, n_dp), second, grad_up), "dp", scatter_dimension=0, tiled=True
    )

    def input_grads(a, b, first, second):
        return back_matmul(a, b, first, second, rows)

    two_keep, two_send = seq.run(20.5, input_grads, grad_gate, grad_up, w_gate, w_up)
    t_two = task(cube.reduce(two_keep, two_send))
    gate_terms = seq.run(12.5, lambda a, b: outer_terms(a, b, n_dp), second, grad_gate)
    down_keep, down_send = seq.run(11.5, lambda h, w: even_odd(dot(h, w)), hidden, w_down)
    grad_hidden_in, branch_own, gain_two_own = seq.run(
        5.8, lambda *a: norm_back(*a, True), hidden_in, *t_two.finish(), grad_own, gain_two
    )
    t_branch_grad = task(cube.gather(branch_own))
    branch_grad = cube.joined(t_branch_grad.finish()).reshape(bucket, width)

    grad_gated = seq.run(3.8, dot_nt, branch_grad, w_out)
    t_down = task(cube.reduce(down_keep, down_send))
    t_down_all = task(cube.gather(seq.tie(down_own)[0]))
    grad_qk, grad_vg, gain_query_own, gain_key_own = seq.run(
        20.0,
        attend_back,
        place, raw_qk, queries, keys, values, gate, attended, grad_gated.reshape(n_u, rows, q_w), log_totals,
        q_gain, k_gain, *tables,
    )
    grad_qk, grad_vg = grad_qk.reshape(bucket, -1), grad_vg.reshape(bucket, -1)
    one_keep, one_send = seq.run(12.0, input_grads, grad_qk, grad_vg, w_qk, w_vg)
    t_one = task(cube.reduce(one_keep, one_send))
    out_parts = seq.run(7.0, lambda p, a, b: out_terms(p, a, b, n_u), place, gated, branch_grad)
    qk_terms = seq.run(9.3, lambda a, b: outer_terms(a, b, n_dp), normed, grad_qk)
    vg_terms = seq.run(9.3, lambda a, b: outer_terms(a, b, n_dp), normed, grad_vg)

    gate_all, qk_all, vg_all, out_all = seq.run(
        150.0, lambda b, *t: reduce_all(b, t, n_dp, n_u), out_parts, gate_terms, qk_terms, vg_terms
    )
    t_up_all = task(cube.gather(seq.tie(up_own)[0]))
    tokens_grad, gain_one_own = seq.run(
        5.6, lambda *a: norm_back(*a, False), tokens[0], *t_one.finish(), grad_hidden_in, gain_one
    )
    gains = seq.run(
        1.0, lambda *g: jnp.concatenate(g, axis=1)[0], gain_one_own, gain_query_own, gain_key_own, gain_two_own
    )
    t_gains = task(cube.total(gains, ("ulysses", "dp")))
    keys_all = [list(range(n_u))]
    in_all = seq.run(
        5.5,
        lambda p, a, b: put_columns(
            p, [(keys_all, [a]), (keys_all, [b])], [[(0, q_w), (q_w, kv_w)], [(0, kv_w), (kv_w, q_w)]]
        ),
        place, qk_all, vg_all,
    )
    out_all = seq.run(4.0, lambda p, a: put_columns(p, [(keys_all, [a])], [[(0, out_cols)]]), place, out_all)
    down_held = t_down_all.finish()
    down_all = seq.run(5.3, lambda p, *b: put_rows(p, (down_held[0], b)), place, *down_held[1])
    up_held = t_up_all.finish()
    mlp_all = seq.run(
        10.0, lambda p, a, *b: put_strips(p, [(keys_all, [a]), (up_held[0], b)], n_dp, ff_strip), place, gate_all, *up_held[1]
    )
    layer_out = seq.run(2.2, lambda a, b, c: a + high(b) + high(c), hidden_in, *t_down.finish())
    gains = t_gains.finish()

    gain_one_sum = gains[:width]
    gain_query_sum = gains[width : width + head_width]
    gain_key_sum = gains[width + head_width : width + 2 * head_width]
    gain_two_sum = gains[width + 2 * head_width :]
    return (
        layer_out[None],
        tokens_grad[None],
        gain_one_sum,
        in_all,
        gain_query_sum,
        gain_key_sum,
        out_all,
        gain_two_sum,
        mlp_all,
        down_all,
    )


def solution(mesh):
    placed = (
        P("dp", "ulysses", None),
        P("dp"),
        P("dp", "ulysses", None),
        P(),
        P("dp", None),
        P(),
        P(),
        P("dp", None),
        P(),
        P("dp", None),
        P("dp", None),
    )
    return jax.shard_map(
        shards,
        mesh=mesh,
        in_specs=placed,
        out_specs=(
            P("dp", "ulysses", None),
            P("dp", "ulysses", None),
            P(),
            P("dp", None),
            P(),
            P(),
            P("dp", None),
            P(),
            P("dp", None),
            P("dp", None),
        ),
        check_vma=False,
    )
```

```python
import functools

import jax
import jax.numpy as jnp
import numpy as np
from jax import lax
from jax.experimental import pallas as pl
from jax.experimental.pallas import tpu as pltpu
from jax.sharding import PartitionSpec as P

QUERY_HEADS = 16
KEY_VALUE_HEADS = 8
HEAD_DIMENSION = 128
FF = 6144


EPSILON = 1e-06
ROPE_BASE = 1000000.0
MASKED = -1e30


def rms_scale(values):
    return lax.rsqrt(jnp.mean(values * values, axis=-1, keepdims=True) + EPSILON)


VMEM_LIMIT = 56 * 1024 * 1024
NT = (((1,), (1,)), ((), ()))
TN = (((0,), (0,)), ((), ()))


def params():
    return pltpu.CompilerParams(vmem_limit_bytes=VMEM_LIMIT)


def cost(*_):
    return pl.CostEstimate(flops=1, bytes_accessed=1, transcendentals=0)


def steady(shape):
    return pl.BlockSpec(shape, lambda *_: (0,) * len(shape), pipeline_mode=pl.Buffered(1))


def tile_of(size):
    return 256 if size % 256 == 0 else 128


def head_scale(raw):
    return lax.rsqrt(jnp.mean(raw * raw, axis=-1, keepdims=True) + EPSILON)


def turn_pairs(value, cosine, sine):
    return value * cosine + pltpu.roll(value, HEAD_DIMENSION // 2, 1) * sine


def masked_scores(q, k, first_row, length):
    scores = lax.dot_general(q, k, NT, preferred_element_type=jnp.float32)
    scores = scores * HEAD_DIMENSION ** (-0.5)
    row = first_row + lax.broadcasted_iota(jnp.int32, scores.shape, 0)
    column = lax.broadcasted_iota(jnp.int32, scores.shape, 1)
    return jnp.where((column <= row) & (column < length), scores, MASKED)


def in_order(ref, me):
    return jnp.concatenate([ref[me ^ t] for t in range(ref.shape[0])], axis=0)


def attend_back_kernel(
    block, copies, heads, kv_heads, place_ref, q_raw, k_raw, q_ref, k_ref, v_ref, gate_ref, attended_ref, up_ref,
    total_ref, q_gain, k_gain, cosine, sine, qk_out, vg_out, q_gain_out, k_gain_out, grad_ref, dq_ref, dk_ref, dv_ref,
):
    group = pl.program_id(0)
    bucket, size = k_ref.shape
    n_u, rows_own, _ = q_raw.shape
    scale = size ** (-0.5)
    length, me = place_ref[0], place_ref[1]

    @pl.when(group == 0)
    def _():
        q_gain_out[...] = jnp.zeros_like(q_gain_out)
        k_gain_out[...] = jnp.zeros_like(k_gain_out)

    def store(out, at, width, value):
        for t in range(n_u):
            out[me ^ t, :, pl.ds(pl.multiple_of(at, size), width)] = value[t * rows_own : (t + 1) * rows_own]

    up, gate = in_order(up_ref, me), gate_ref[...]
    grad_ref[...] = (up * gate).astype(jnp.bfloat16)
    grad_gate = (up * attended_ref[...].astype(jnp.float32) * gate * (1.0 - gate)).astype(jnp.bfloat16)
    store(vg_out, (kv_heads + group * copies) * size, copies * size, grad_gate)
    dk_ref[...] = jnp.zeros_like(dk_ref)
    dv_ref[...] = jnp.zeros_like(dv_ref)

    def norm_grad(raw, gain, upstream, gain_out):
        factor = head_scale(raw)
        weighted = upstream * gain
        inner = jnp.mean(weighted * raw, axis=-1, keepdims=True)
        gain_out[...] += jnp.sum(upstream * raw * factor, axis=0, keepdims=True)
        return (factor * weighted - raw * (factor * factor * factor) * inner).astype(jnp.bfloat16)

    raw_q = in_order(q_raw, me)
    for copy in range(copies):
        columns = slice(copy * size, (copy + 1) * size)
        for first in range(0, bucket, block):
            rows = slice(first, first + block)
            reach = slice(0, first + block)
            q, g = q_ref[rows, columns], grad_ref[rows, columns]
            soft = jnp.exp(masked_scores(q, k_ref[reach], first, length) - total_ref[copy, rows])
            soft_grad = lax.dot_general(g, v_ref[reach], NT, preferred_element_type=jnp.float32)
            inner = jnp.sum(soft * soft_grad, axis=-1, keepdims=True)
            score_grad = (soft * (soft_grad - inner)).astype(jnp.bfloat16)
            dq_ref[rows] = jnp.dot(score_grad, k_ref[reach], preferred_element_type=jnp.float32) * scale
            dk_ref[reach] += lax.dot_general(score_grad, q, TN, preferred_element_type=jnp.float32)
            dv_ref[reach] += lax.dot_general(soft.astype(jnp.bfloat16), g, TN, preferred_element_type=jnp.float32)
        plain = turn_pairs(dq_ref[...].astype(jnp.bfloat16).astype(jnp.float32), cosine[...], -sine[...])
        store(qk_out, (group * copies + copy) * size, size, norm_grad(raw_q[:, columns], q_gain[...], plain, q_gain_out))
    plain = turn_pairs((dk_ref[...] * scale).astype(jnp.bfloat16).astype(jnp.float32), cosine[...], -sine[...])
    store(qk_out, (heads + group) * size, size, norm_grad(in_order(k_raw, me), k_gain[...], plain, k_gain_out))
    store(vg_out, group * size, size, dv_ref[...].astype(jnp.bfloat16))


def attend_back(place, raw_qk, q, k, v, gate, attended, upstream, totals, q_gain, k_gain, cosine, sine):
    size = HEAD_DIMENSION
    n_u, rows_own, _ = raw_qk.shape
    bucket = n_u * rows_own
    heads, kv_heads = q.shape[1] // size, k.shape[1] // size
    copies = heads // kv_heads

    def blocks(width, start):
        return pl.BlockSpec((n_u, rows_own, width), lambda g: (0, 0, start + g))

    wide = pl.BlockSpec((bucket, copies * size), lambda g: (0, g))
    slim = pl.BlockSpec((bucket, size), lambda g: (0, g))
    total = (heads + kv_heads) * size
    whole = pl.BlockSpec((n_u, rows_own, total), lambda g: (0, 0, 0))
    gain = pl.BlockSpec((1, size), lambda g: (0, 0))
    return pl.pallas_call(
        functools.partial(attend_back_kernel, min(256, bucket), copies, heads, kv_heads),
        grid=(kv_heads,),
        in_specs=[
            pl.BlockSpec(memory_space=pltpu.SMEM),
            blocks(copies * size, 0),
            blocks(size, heads),
            wide,
            slim,
            slim,
            wide,
            wide,
            blocks(copies * size, 0),
            pl.BlockSpec((copies, bucket, 1), lambda g: (g, 0, 0)),
            steady((1, size)),
            steady((1, size)),
            steady((bucket, size)),
            steady((bucket, size)),
        ],
        out_specs=[whole, whole, gain, gain],
        out_shape=[
            jax.ShapeDtypeStruct((n_u, rows_own, total), jnp.bfloat16),
            jax.ShapeDtypeStruct((n_u, rows_own, total), jnp.bfloat16),
            jax.ShapeDtypeStruct((1, size), jnp.float32),
            jax.ShapeDtypeStruct((1, size), jnp.float32),
        ],
        scratch_shapes=[
            pltpu.VMEM((bucket, copies * size), jnp.bfloat16),
            pltpu.VMEM((bucket, size), jnp.float32),
            pltpu.VMEM((bucket, size), jnp.float32),
            pltpu.VMEM((bucket, size), jnp.float32),
        ],
        compiler_params=params(),
        cost_estimate=cost(5 * heads * bucket * bucket * size, 24 * bucket * heads * size, heads * bucket * bucket // 2),
        name="attention_back",
    )(place, raw_qk, raw_qk, q, k, v, gate, attended, upstream, totals, q_gain, k_gain, cosine, sine)


def gate_up(x, first, second):
    m, width = x.shape
    n = first.shape[1]
    tile = tile_of(n)
    step_rows = min(256, m)

    def kernel(x_ref, first_ref, second_ref, a_out, b_out, hidden_out):
        for at in range(0, m, step_rows):
            rows = slice(at, at + step_rows)
            a = jnp.dot(x_ref[rows], first_ref[...], preferred_element_type=jnp.float32)
            b = jnp.dot(x_ref[rows], second_ref[...], preferred_element_type=jnp.float32)
            a_out[rows] = a
            b_out[rows] = b
            hidden_out[rows] = (a * jax.nn.sigmoid(a) * b).astype(jnp.bfloat16)

    weight = pl.BlockSpec((width, tile), lambda j: (0, j))
    out = pl.BlockSpec((m, tile), lambda j: (0, j))
    return pl.pallas_call(
        kernel,
        grid=(n // tile,),
        in_specs=[steady((m, width)), weight, weight],
        out_specs=[out] * 3,
        out_shape=[jax.ShapeDtypeStruct((m, n), d) for d in (jnp.float32, jnp.float32, jnp.bfloat16)],
        compiler_params=params(),
        cost_estimate=cost(),
        name="gate_up",
    )(x, first, second)


def back_matmul(a, b, first, second, rows):
    m, n = a.shape
    width = first.shape[0]
    part = 256

    def kernel(a_ref, b_ref, first_ref, second_ref, keep_ref, send_ref):
        for at in range(0, width, part):
            where = slice(at, at + part)
            out = lax.dot_general(a_ref[...], first_ref[where], NT, preferred_element_type=jnp.float32)
            out += lax.dot_general(b_ref[...], second_ref[where], NT, preferred_element_type=jnp.float32)
            out = out.astype(jnp.bfloat16)
            keep_ref[0, :, where] = out[:rows]
            send_ref[0, :, where] = out[rows:]

    step = pl.BlockSpec((2 * rows, n), lambda i: (i, 0))
    out = pl.BlockSpec((1, rows, width), lambda i: (i, 0, 0))
    shape = jax.ShapeDtypeStruct((m // rows // 2, rows, width), jnp.bfloat16)
    return pl.pallas_call(
        kernel,
        grid=(m // rows // 2,),
        in_specs=[step, step, steady(first.shape), steady(second.shape)],
        out_specs=[out, out],
        out_shape=[shape, shape],
        compiler_params=params(),
        cost_estimate=cost(),
        name="back_matmul",
    )(a, b, first, second)


def outer_terms(x, y, count):
    m, width = x.shape
    n = y.shape[1]
    depth = width // count

    def kernel(x_ref, y_ref, out_ref):
        out_ref[...] = lax.dot_general(x_ref[...], y_ref[...], TN, preferred_element_type=jnp.float32).astype(jnp.bfloat16)

    return pl.pallas_call(
        kernel,
        grid=(count,),
        in_specs=[pl.BlockSpec((m, depth), lambda k: (0, k)), steady((m, n))],
        out_specs=pl.BlockSpec((depth, n), lambda k: (k, 0)),
        out_shape=jax.ShapeDtypeStruct((width, n), jnp.bfloat16),
        compiler_params=params(),
        cost_estimate=cost(2 * m * n * width, 2 * m * width + 2 * m * n + 2 * n * width),
        name="outer_terms",
    )(x, y)


def down_back(upstream, a, b, weight):
    m, width = upstream.shape
    n = a.shape[1]
    rows = min(256, m)

    def kernel(up_ref, a_ref, b_ref, weight_ref, gate_out, up_out):
        grad = lax.dot_general(up_ref[...], weight_ref[...], NT, preferred_element_type=jnp.float32)
        a, b = a_ref[...], b_ref[...]
        sig = jax.nn.sigmoid(a)
        gate_out[...] = (grad * b * sig * (1.0 + a * (1.0 - sig))).astype(jnp.bfloat16)
        up_out[...] = (grad * a * sig).astype(jnp.bfloat16)

    step = pl.BlockSpec((rows, n), lambda i: (i, 0))
    shape = jax.ShapeDtypeStruct((m, n), jnp.bfloat16)
    return pl.pallas_call(
        kernel,
        grid=(m // rows,),
        in_specs=[pl.BlockSpec((rows, width), lambda i: (i, 0)), step, step, steady((n, width))],
        out_specs=[step, step],
        out_shape=[shape, shape],
        compiler_params=params(),
        cost_estimate=cost(2 * m * n * width, 2 * m * width + 12 * m * n + 2 * n * width),
        name="down_back",
    )(upstream, a, b, weight)


def strips_kernel(n_dp, n_u, strip, place_ref, w_ref, gate_ref, up_ref):
    for t in range(n_u):

        @pl.when(place_ref[1] == t)
        def _():
            for half, out in enumerate((gate_ref, up_ref)):
                starts = [((half * n_dp + b) * n_u + t) * strip for b in range(n_dp)]
                out[...] = jnp.concatenate([w_ref[:, s : s + strip] for s in starts], axis=1)


def take_strips(place, w, n_dp, n_u, strip):
    depth, total = w.shape
    rows = 64
    out = pl.BlockSpec((rows, n_dp * strip), lambda i: (i, 0))
    shape = jax.ShapeDtypeStruct((depth, n_dp * strip), w.dtype)
    return pl.pallas_call(
        functools.partial(strips_kernel, n_dp, n_u, strip),
        grid=(depth // rows,),
        in_specs=[pl.BlockSpec(memory_space=pltpu.SMEM), pl.BlockSpec((rows, total), lambda i: (i, 0))],
        out_specs=[out, out],
        out_shape=[shape, shape],
        compiler_params=params(),
        cost_estimate=cost(0, 2 * depth * total + 4 * depth * n_dp * strip),
        name="take_strips",
    )(place, w)


def fill(scratch, keys, refs):
    for key_list, ref in zip(keys, refs):
        for at, key in enumerate(key_list):
            scratch[key] = ref[at]


def put_call(kernel, place, helds, grid, blocks, at, out_block, out_at, out_shape, name):
    n_u = sum(len(k) for k in helds[0][0])
    count = sum(len(b) for _, b in helds)

    def body(place_ref, *refs):
        refs = list(refs)
        scratches = refs[count + 1 :]
        for (keys, _), scratch in zip(helds, scratches):
            fill(scratch, keys, [refs.pop(0) for _ in keys])
        kernel(place_ref[1], scratches, refs[0])

    return pl.pallas_call(
        body,
        grid=(grid,),
        in_specs=[pl.BlockSpec(memory_space=pltpu.SMEM)]
        + [pl.BlockSpec((len(k),) + block, at) for (keys, _), block in zip(helds, blocks) for k in keys],
        out_specs=pl.BlockSpec(out_block, out_at),
        out_shape=jax.ShapeDtypeStruct(out_shape, jnp.float32),
        scratch_shapes=[pltpu.VMEM((n_u,) + block, jnp.bfloat16) for block in blocks],
        compiler_params=params(),
        cost_estimate=cost(0, 6 * out_shape[0] * out_shape[1]),
        name=name,
    )(place, *[v for _, held in helds for v in held])


def put_strips(place, helds, n_dp, strip):
    n_u = sum(len(k) for k in helds[0][0])
    depth, width = helds[0][1][0].shape[1:]
    rows = min(32, depth)

    def kernel(me, scratches, out_ref):
        size = n_u * strip
        for h, scratch in enumerate(scratches):
            parts = [scratch[me ^ t].astype(jnp.float32) for t in range(n_u)]
            for b in range(n_dp):
                at = (h * n_dp + b) * size
                out_ref[:, at : at + size] = jnp.concatenate(
                    [p[:, b * strip : (b + 1) * strip] for p in parts], axis=1
                )

    total = len(helds) * n_u * width
    return put_call(
        kernel, place, helds, depth // rows, [(rows, width)] * len(helds), lambda i: (0, i, 0),
        (rows, total), lambda i: (i, 0), (depth, total), "put_strips",
    )


def put_columns(place, helds, sections):
    n_u = sum(len(k) for k in helds[0][0])
    depth = helds[0][1][0].shape[1]
    rows = min(64, depth)

    def kernel(me, scratches, out_ref):
        at = 0
        for scratch, parts in zip(scratches, sections):
            for start, size in parts:
                for t in range(n_u):
                    out_ref[:, at : at + size] = scratch[me ^ t, :, start : start + size].astype(jnp.float32)
                    at += size

    total = n_u * sum(size for parts in sections for _, size in parts)
    return put_call(
        kernel, place, helds, depth // rows, [(rows, held[0].shape[2]) for _, held in helds], lambda i: (0, i, 0),
        (rows, total), lambda i: (i, 0), (depth, total), "put_columns",
    )


def put_rows(place, held):
    n_u = sum(len(k) for k in held[0])
    depth, width = held[1][0].shape[1:]
    tile = 512

    def kernel(me, scratches, out_ref):
        for t in range(n_u):
            out_ref[t * depth : (t + 1) * depth] = scratches[0][me ^ t].astype(jnp.float32)

    return put_call(
        kernel, place, [held], width // tile, [(depth, tile)], lambda i: (0, 0, i),
        (n_u * depth, tile), lambda i: (0, i), (n_u * depth, width), "put_rows",
    )


def ring_sums(chains):
    steps = 2 if all(parts[0][0].shape[1] % 32 == 0 for parts, _, _ in chains) else 1
    scalars, operands, specs, out_shape, out_specs = [], [], [], [], []
    for parts, offset, arrived in chains:
        width = 0
        for terms, at in parts:
            r, c = terms.shape[1:]
            slot = [k for k, have in enumerate(scalars) if have is at]
            if not slot:
                slot = [len(scalars)]
                scalars.append(at)
            specs.append(
                pl.BlockSpec((1, r // steps, c), lambda i, *sc, slot=slot[0], offset=offset: (sc[slot][offset], i, 0))
            )
            operands.append(terms)
            width += c
        for value in arrived:
            specs.append(pl.BlockSpec((r // steps, width), lambda i, *sc: (i, 0)))
            operands.append(value)
        out_shape.append(jax.ShapeDtypeStruct((r, width), jnp.bfloat16))
        out_specs.append(pl.BlockSpec((r // steps, width), lambda i, *sc: (i, 0)))

    def kernel(*refs):
        refs = refs[len(scalars) :]
        ins, outs = list(refs[: len(operands)]), refs[len(operands) :]
        for (parts, _, arrived), out in zip(chains, outs):
            terms = [ins.pop(0) for _ in parts]
            got = [ins.pop(0) for _ in arrived]
            start = 0
            for term in terms:
                columns = slice(start, start + term.shape[2])
                total = term[0]
                if got:
                    total = total.astype(jnp.float32)
                    for value in got:
                        total = total + value[:, columns].astype(jnp.float32)
                    total = total.astype(jnp.bfloat16)
                out[:, columns] = total
                start += term.shape[2]

    return pl.pallas_call(
        kernel,
        grid_spec=pltpu.PrefetchScalarGridSpec(
            num_scalar_prefetch=len(scalars), grid=(steps,), in_specs=specs, out_specs=out_specs
        ),
        out_shape=out_shape,
        compiler_params=params(),
        cost_estimate=cost(0, sum(2 * o.size for o in out_shape) * 3),
        name="ring_sums",
    )(*scalars, *operands)


def norm_call(kernel, inputs, gain, outs, gain_sum, name):
    r, width = inputs[0].shape
    tile = min(64, r)
    step = pl.BlockSpec((tile, width), lambda i: (i, 0))
    one = pl.BlockSpec((1, width), lambda i: (0, 0))
    shapes = [jax.ShapeDtypeStruct((r, width), o) for o in outs]
    if gain_sum:
        shapes.append(jax.ShapeDtypeStruct((1, width), jnp.float32))
    return pl.pallas_call(
        kernel,
        grid=(r // tile,),
        in_specs=[step] * len(inputs) + [one],
        out_specs=[step] * len(outs) + [one] * gain_sum,
        out_shape=shapes,
        compiler_params=params(),
        cost_estimate=cost(0, sum(4 * v.size for v in inputs)),
        name=name,
    )(*inputs, gain)


def norm_back(source, keep, got, residual, gain, rounded):
    def kernel(source_ref, keep_ref, got_ref, residual_ref, gain_ref, *outs):
        @pl.when(pl.program_id(0) == 0)
        def _():
            outs[-1][...] = jnp.zeros_like(outs[-1])

        up = keep_ref[...] + got_ref[...].astype(jnp.float32)
        source = source_ref[...].astype(jnp.float32)
        factor = head_scale(source)
        weighted = up * gain_ref[...]
        inner = jnp.mean(weighted * source, axis=-1, keepdims=True)
        total = residual_ref[...].astype(jnp.float32) + factor * weighted
        total = total - source * (factor * factor * factor) * inner
        outs[0][...] = total
        if rounded:
            outs[1][...] = total.astype(jnp.bfloat16)
        outs[-1][...] += jnp.sum(up * source * factor, axis=0, keepdims=True)

    outs = [jnp.float32] + [jnp.bfloat16] * rounded
    return norm_call(kernel, (source, keep, got, residual), gain, outs, 1, "norm_back")


def halve(keep, got):
    pairs, (r, c) = keep.shape[0] // 2, keep.shape[1:]
    tile = min(64, r)

    def kernel(keep_ref, got_ref, even_ref, odd_ref):
        even_ref[0] = keep_ref[0].astype(jnp.float32) + got_ref[0].astype(jnp.float32)
        odd_ref[0] = (keep_ref[1].astype(jnp.float32) + got_ref[1].astype(jnp.float32)).astype(jnp.bfloat16)

    two = pl.BlockSpec((2, tile, c), lambda p, i: (p, i, 0))
    one = pl.BlockSpec((1, tile, c), lambda p, i: (p, i, 0))
    return pl.pallas_call(
        kernel,
        grid=(pairs, r // tile),
        in_specs=[two, two],
        out_specs=[one, one],
        out_shape=[jax.ShapeDtypeStruct((pairs, r, c), jnp.float32), jax.ShapeDtypeStruct((pairs, r, c), jnp.bfloat16)],
        compiler_params=params(),
        cost_estimate=cost(0, 16 * pairs * r * c),
        name="halve",
    )(keep, got)


def out_terms(place, gated, upstream, n_u):
    m, q = gated.shape
    c = upstream.shape[1] // n_u

    def kernel(place_ref, x_ref, y_ref, out_ref):
        out_ref[0] = lax.dot_general(x_ref[...], y_ref[...], TN, preferred_element_type=jnp.float32).astype(jnp.bfloat16)

    return pl.pallas_call(
        kernel,
        grid_spec=pltpu.PrefetchScalarGridSpec(
            num_scalar_prefetch=1,
            grid=(n_u,),
            in_specs=[
                pl.BlockSpec((m, q), lambda k, p: (0, 0)),
                pl.BlockSpec((m, c), lambda k, p: (0, p[1] ^ k)),
            ],
            out_specs=pl.BlockSpec((1, q, c), lambda k, p: (k, 0, 0)),
        ),
        out_shape=jax.ShapeDtypeStruct((n_u, q, c), jnp.bfloat16),
        compiler_params=params(),
        cost_estimate=cost(2 * m * q * c * n_u, 2 * m * q + 4 * m * c * n_u),
        name="out_terms",
    )(place, gated, upstream)


MESH = pl.DeviceIdType.MESH


class Group:
    def __init__(self, n_dp, n_u):
        self.n_dp, self.n_u = n_dp, n_u
        index = lax.axis_index("dp")
        self.me = lax.axis_index("ulysses")
        odd = index % 2
        self.position = (1 - odd) * (index // 2) + odd * (n_dp - 1 - index // 2)
        self.next = (self.owner(1), self.owner(-1))
        self.bits = [1 << k for k in range(n_u.bit_length() - 1)]

    def owner(self, offset):
        place = (self.position + offset + self.n_dp) % self.n_dp
        late = place // (self.n_dp // 2)
        return (1 - late) * (2 * place) + late * (2 * (self.n_dp - 1 - place) + 1)

    def greet(self):
        barrier = pltpu.get_barrier_semaphore()
        for way in (0, 1):
            pl.semaphore_signal(barrier, inc=1, device_id={"dp": self.next[way]}, device_id_type=MESH)
        for other in range(1, self.n_u):
            pl.semaphore_signal(barrier, inc=1, device_id={"ulysses": self.me ^ other}, device_id_type=MESH)
        pl.semaphore_wait(barrier, 1 + self.n_u)

    def to_ring(self, way, source, target, send, recv):
        copy = pltpu.make_async_remote_copy(
            src_ref=source, dst_ref=target, send_sem=send, recv_sem=recv,
            device_id={"dp": self.next[way]}, device_id_type=MESH,
        )
        copy.start()
        return copy

    def to_cube(self, bit, source, target, send, recv):
        copy = pltpu.make_async_remote_copy(
            src_ref=source, dst_ref=target, send_sem=send, recv_sem=recv,
            device_id={"ulysses": self.me ^ bit}, device_id_type=MESH,
        )
        copy.start()
        return copy

    def reach(self, more_ahead):
        longer = self.n_dp // 2
        shorter = self.n_dp - 1 - longer
        return (longer, shorter) if more_ahead else (shorter, longer)


class Spread:
    def __init__(self, group, own, out, send, recv):
        self.group, self.own, self.out, self.send, self.recv = group, own, out, send, recv
        self.keys, self.levels, self.copies, self.used, self.waited = [0], group.bits[::-1], [], 0, 0

    def level(self):
        for copy in self.copies[self.waited :]:
            copy.wait_recv()
        self.waited = len(self.copies)
        if not self.levels:
            return False
        bit = self.levels.pop(0)
        for key in sorted(self.keys):
            source = self.own if key == 0 else self.out.at[key]
            at = self.used
            self.copies.append(
                self.group.to_cube(bit, source, self.out.at[key ^ bit], self.send.at[at], self.recv.at[at])
            )
            self.used += 1
        self.keys += [key ^ bit for key in self.keys]
        return True

    def finish(self):
        while self.level():
            pass
        for copy in self.copies:
            copy.wait_send()


class RingGather:
    def __init__(self, group, chains, send, recv):
        self.group, self.chains, self.send_sems, self.recv_sems = group, chains, send, recv
        self.copies = {}

    def place(self, c, owner):
        _, out, block, low, rows, _ = self.chains[c]
        return out.at[pl.ds(pl.multiple_of(owner * block + low, 16), rows)]

    def item(self, c):
        item, _, _, low, rows, _ = self.chains[c]
        return item.at[low : low + rows]

    def reach(self, c, way):
        return self.group.reach(self.chains[c][5])[way]

    def send(self, c, way, step):
        owner = self.group.owner(1 - step if way == 0 else step - 1)
        source = self.item(c) if step == 1 else self.place(c, owner)
        sems = (c, way, step - 1)
        self.copies[sems] = self.group.to_ring(
            way, source, self.place(c, owner), self.send_sems.at[sems], self.recv_sems.at[sems]
        )

    def start(self, c):
        for way in (0, 1):
            self.send(c, way, 1)

    def event(self, c, way, step):
        if step <= self.reach(c, way):
            self.copies[c, way, step - 1].wait_recv()
            if step < self.reach(c, way):
                self.send(c, way, step + 1)

    def finish(self):
        for copy in self.copies.values():
            copy.wait_send()


def by_rows(count, tile, function):
    def body(i, carry):
        function(pl.ds(pl.multiple_of(i * tile, tile), tile))
        return carry

    lax.fori_loop(0, count // tile, body, 0)


def forward_kernel(
    n_dp, n_u, heads, kv_heads, length_ref, tokens_ref, gain_one, gain_two, q_gain, k_gain, cosine, sine, grad_ref,
    out_item, qk_item, vg_item, gate_item, up_item, down_item,
    w_qk, w_vg, w_gate, w_up, w_down, normed_out, grad_out, second_out,
    raw_qk, raw_vg, q_out, k_out, v_out, gate_out, attended_out, gated_out, total_out, w_out, hidden_out,
    normed, own, qk_local, vg_local, columns, turned, parts, core_got, total, second_own,
    ring_send, ring_recv, cube_send, cube_recv, turn_send, turn_recv, sum_send, sum_recv, local,
):
    rows_own, width = tokens_ref.shape
    bucket = rows_own * n_u
    size = HEAD_DIMENSION
    copies = heads // kv_heads
    depth = width // n_dp
    group = Group(n_dp, n_u)
    me, mine = group.me, group.owner(0)
    group.greet()
    strip = down_item.shape[0]
    halves = 2 if strip % 32 == 0 else 1
    chains = [
        (out_item, columns, depth, 0, depth, True),
        (qk_item, w_qk, depth, 0, depth, False),
        (vg_item, w_vg, depth, 0, depth, True),
        (gate_item, w_gate, depth, 0, depth, True),
        (up_item, w_up, depth, 0, depth, False),
    ]
    for p in range(halves):
        chains.append((down_item, w_down, strip, p * strip // halves, strip // halves, p == 0))
    ring = RingGather(group, chains, ring_send, ring_recv)
    kept = []

    def keep(source, target):
        copy = pltpu.make_async_copy(source, target, local.at[len(kept)])
        copy.start()
        kept.append(copy)
        return copy

    for c in (0, 1, 2):
        ring.start(c)
    own_rows = lambda out, block: out.at[pl.ds(pl.multiple_of(mine * block, 16), block)]
    for item, out, block in (
        (out_item, columns, depth), (qk_item, w_qk, depth), (vg_item, w_vg, depth),
        (gate_item, w_gate, depth), (up_item, w_up, depth), (down_item, w_down, strip),
    ):
        keep(item, own_rows(out, block))

    def first(rows):
        x = tokens_ref[rows].astype(jnp.float32)
        own[rows] = (x * head_scale(x) * gain_one[...]).astype(jnp.bfloat16)

    by_rows(rows_own, 64, first)
    keep(own, normed.at[0]).wait()
    keep(grad_ref, grad_out.at[0])
    spreads = [
        Spread(group, own, normed, cube_send.at[0], cube_recv.at[0]),
        Spread(group, grad_ref, grad_out, cube_send.at[1], cube_recv.at[1]),
    ]
    spreads[0].level()
    longest = n_dp // 2
    for step in range(1, longest + 1):
        for c in (0, 1, 2):
            for way in (0, 1):
                ring.event(c, way, step)
        if step == 1:
            spreads[1].level()
        if step < longest:
            spreads[0 if step % 2 == 1 else 1].level()
        if step == longest - 1:
            for c in (3, 4):
                ring.start(c)
    spreads[0].finish()
    events = []
    for step in range(1, longest + 1):
        events += [[(3, 0, step), (4, 1, step)], [(4, 0, step), (3, 1, step)]]
        if step == longest - 1:
            events.append([("start",)])
    for step in range(1, longest + 1):
        if halves == 2:
            events += [[(5, 0, step), (6, 1, step)], [(6, 0, step), (5, 1, step)]]
        else:
            events += [[(5, 0, step), (5, 1, step)]]

    def pump(count=1):
        while count and events:
            pair = events.pop(0)
            if pair[0][0] == "start":
                for c in range(5, len(chains)):
                    ring.start(c)
                continue
            for event in pair:
                ring.event(*event)
            count -= 1

    for copy in kept[:3]:
        copy.wait()
    share = depth * n_dp // n_u
    turns = []
    for k in range(1, n_u):
        source = columns.at[pl.ds(pl.multiple_of((me ^ k) * share, 16), share)]
        turns.append(group.to_cube(k, source, turned.at[k], turn_send.at[k - 1], turn_recv.at[k - 1]))
    keep(columns.at[pl.ds(pl.multiple_of(me * share, 16), share)], turned.at[0]).wait()
    one, two = keep(w_qk, qk_local), keep(w_vg, vg_local)
    keep(normed, normed_out)
    one.wait()
    two.wait()

    def project(b, carry):
        x = normed[b]
        raw_qk[b] = jnp.dot(x, qk_local[...], preferred_element_type=jnp.float32)
        raw_vg[b] = jnp.dot(x, vg_local[...], preferred_element_type=jnp.float32)
        return carry

    lax.fori_loop(0, n_u, project, 0)
    pump()

    length = length_ref[0]
    block = min(256, bucket)

    def attention(h, carry):
        def column(ref, at):
            at = pl.multiple_of(at * size, size)
            return jnp.concatenate([ref[me ^ t, :, pl.ds(at, size)] for t in range(n_u)], axis=0)

        at = pl.ds(pl.multiple_of(h * size, size), size)
        kv = pl.ds(pl.multiple_of(h // copies * size, size), size)
        q = column(raw_qk, h)
        q = turn_pairs(q * head_scale(q) * q_gain[...], cosine[...], sine[...]).astype(jnp.bfloat16)
        q_out[:, at] = q
        k = column(raw_qk, heads + h // copies)
        k = turn_pairs(k * head_scale(k) * k_gain[...], cosine[...], sine[...]).astype(jnp.bfloat16)
        k_out[:, kv] = k
        v = column(raw_vg, h // copies).astype(jnp.bfloat16)
        v_out[:, kv] = v
        gate = jax.nn.sigmoid(column(raw_vg, kv_heads + h))
        gate_out[:, at] = gate
        for start in range(0, bucket, block):
            rows = slice(start, start + block)
            scores = masked_scores(q[rows], k[: start + block], start, length)
            top = jnp.max(scores, axis=-1, keepdims=True)
            soft = jnp.exp(scores - top)
            sums = jnp.sum(soft, axis=-1, keepdims=True)
            out = jnp.dot(soft.astype(jnp.bfloat16), v[: start + block], preferred_element_type=jnp.float32) / sums
            out = out.astype(jnp.bfloat16)
            attended_out[rows, at] = out
            total_out[h, rows] = top + jnp.log(sums)
            gated = (out.astype(jnp.float32) * gate[rows]).astype(jnp.bfloat16)
            for t in range(start // rows_own, (start + block) // rows_own):
                inside = slice(t * rows_own - start, (t + 1) * rows_own - start)
                gated_out[me ^ t, :, at] = gated[inside]
        return carry

    lax.fori_loop(0, heads, attention, 0)
    pump()
    for copy in turns:
        copy.wait_recv()
    c_width = columns.shape[1]
    for k in range(n_u):
        w_out[:, pl.ds(pl.multiple_of((me ^ k) * c_width, c_width), c_width)] = turned[k]

    def branch(b, carry):
        parts[b] = jnp.dot(gated_out[b], w_out[...], preferred_element_type=jnp.float32).astype(jnp.bfloat16)
        return carry

    lax.fori_loop(0, n_u, branch, 0)
    held = list(range(n_u))
    used = 0
    sums = []
    for bit in group.bits:
        keys = [key for key in held if not key & bit]
        level = []
        for key in keys:
            level.append(
                group.to_cube(bit, parts.at[key | bit], core_got.at[used], sum_send.at[used], sum_recv.at[used])
            )
            used += 1
        sums += level
        pump()
        for at, (key, copy) in enumerate(zip(keys, level)):
            copy.wait_recv()
            slot = used - len(keys) + at

            def add(rows, key=key, slot=slot):
                got = core_got[slot, rows].astype(jnp.float32)
                if key:
                    parts[key, rows] = (parts[key, rows].astype(jnp.float32) + got).astype(jnp.bfloat16)
                elif bit == 1:
                    total[rows] = tokens_ref[rows].astype(jnp.float32) + parts[0, rows].astype(jnp.float32) + got
                else:
                    total[rows] = total[rows] + got

            by_rows(rows_own, 64, add)
        held = keys

    def second(rows):
        hidden = total[rows]
        hidden_out[rows] = hidden
        second_own[rows] = (hidden * head_scale(hidden) * gain_two[...]).astype(jnp.bfloat16)

    by_rows(rows_own, 64, second)
    spread = Spread(group, second_own, second_out, cube_send.at[2], cube_recv.at[2])
    keep(second_own, second_out.at[0])
    while spread.level():
        pump(2)
    spreads[1].finish()
    spread.finish()
    pump(1000)
    ring.finish()
    for copy in turns + sums:
        copy.wait_send()
    for copy in kept[3:6] + kept[7:8] + kept[11:]:
        copy.wait()


def forward(length, tokens_own, gains, tables, grad_own, items, n_dp, n_u, heads, kv_heads):
    anywhere = pl.BlockSpec(memory_space=pl.ANY)
    local = pl.BlockSpec(memory_space=pltpu.VMEM)
    rows, width = tokens_own.shape
    bucket, size = rows * n_u, HEAD_DIMENSION
    total = (heads + kv_heads) * size
    depth = width // n_dp
    columns = items[0].shape[1]
    share = width // n_u
    longest = n_dp // 2

    def shape(*dims, dtype=jnp.bfloat16):
        return jax.ShapeDtypeStruct(dims, dtype)

    out_shape = [shape(n_dp * i.shape[0], i.shape[1]) for i in items[1:]]
    out_shape += [shape(n_u, rows, width)] * 3
    out_shape += [shape(n_u, rows, total, dtype=jnp.float32)] * 2
    out_shape += [
        shape(bucket, heads * size), shape(bucket, kv_heads * size), shape(bucket, kv_heads * size),
        shape(bucket, heads * size, dtype=jnp.float32), shape(bucket, heads * size),
        shape(n_u, rows, heads * size), shape(heads, bucket, 1, dtype=jnp.float32),
        shape(share, width), shape(rows, width, dtype=jnp.float32),
    ]
    dma = pltpu.SemaphoreType.DMA
    return pl.pallas_call(
        functools.partial(forward_kernel, n_dp, n_u, heads, kv_heads),
        in_specs=[pl.BlockSpec(memory_space=pltpu.SMEM)] + [local] * 7 + [anywhere] * 7,
        out_specs=[anywhere] * 8 + [local] * 11,
        out_shape=out_shape,
        scratch_shapes=[
            pltpu.VMEM((n_u, rows, width), jnp.bfloat16),
            pltpu.VMEM((rows, width), jnp.bfloat16),
            pltpu.VMEM((width, total), jnp.bfloat16),
            pltpu.VMEM((width, total), jnp.bfloat16),
            pltpu.VMEM((width, columns), jnp.bfloat16),
            pltpu.VMEM((n_u, share, columns), jnp.bfloat16),
            pltpu.VMEM((n_u, rows, width), jnp.bfloat16),
            pltpu.VMEM((n_u - 1, rows, width), jnp.bfloat16),
            pltpu.VMEM((rows, width), jnp.float32),
            pltpu.VMEM((rows, width), jnp.bfloat16),
            dma((7, 2, longest)), dma((7, 2, longest)), dma((3, n_u - 1)), dma((3, n_u - 1)),
            dma((n_u - 1,)), dma((n_u - 1,)), dma((n_u - 1,)), dma((n_u - 1,)), dma((13,)),
        ],
        compiler_params=pltpu.CompilerParams(vmem_limit_bytes=60 * 1024 * 1024, collective_id=0, has_side_effects=True),
        cost_estimate=cost(),
        name="forward",
    )(length, tokens_own, *gains, *tables, grad_own, *items)


def reduce_kernel(n_dp, n_u, count, blocks_ref, *refs):
    terms, outs = list(refs[: count - 1]), refs[count - 1 : 2 * count - 1]
    refs = refs[2 * count - 1 :]
    slots, sums = refs[:count], refs[count : 2 * count]
    out_terms_ref, ring_send, ring_recv, cube_send, cube_recv, turn_send, turn_recv, local = refs[2 * count :]
    terms.append(out_terms_ref)
    group = Group(n_dp, n_u)
    group.greet()
    copies = {}
    reaches = [group.reach(c % 2 == 0) for c in range(count)]
    longest = n_dp // 2
    share = blocks_ref.shape[1]
    here = out_terms_ref.at[pl.ds(pl.multiple_of(group.me * share, share), share)]

    def add(c, target, offset, others):
        r = target.shape[0]
        tile = 16
        first = group.owner(offset) * r

        def body(i, carry):
            rows = pl.ds(pl.multiple_of(i * tile, tile), tile)
            total = terms[c][pl.ds(pl.multiple_of(first + i * tile, tile), tile)].astype(jnp.float32)
            for other in others:
                total = total + other[rows].astype(jnp.float32)
            target[rows] = total.astype(jnp.bfloat16)
            return carry

        lax.fori_loop(0, r // tile, body, 0)

    def slot(c, way, step):
        return slots[c].at[way, step]

    def send(c, way, step):
        reach = reaches[c][way]
        offset = (reach - step) if way == 0 else (step - reach)
        if step == 0:
            r = sums[c].shape[0]
            source = terms[c].at[pl.ds(pl.multiple_of(group.owner(offset) * r, r), r)]
        else:
            source = slot(c, way, step - 1)
            add(c, source, offset, [source])
        sems = (c, way, step)
        copies[sems] = group.to_ring(way, source, slot(c, way, step), ring_send.at[sems], ring_recv.at[sems])

    def start(chains):
        for c in chains:
            for way in (0, 1):
                send(c, way, 0)

    start(range(count - 1))
    turns = []
    for k in range(1, n_u):
        turns.append(group.to_cube(k, blocks_ref.at[k], here, turn_send.at[k - 1], turn_recv.at[k - 1]))
    own = pltpu.make_async_copy(blocks_ref.at[0], here, local.at[count])
    own.start()
    own.wait()
    spreads, kept = [], []
    for copy in turns:
        copy.wait_recv()
    start([count - 1])
    for step in range(longest):
        for c in range(count):
            for way in (0, 1):
                if step < reaches[c][way]:
                    copies[c, way, step].wait_recv()
                    if step + 1 < reaches[c][way]:
                        send(c, way, step + 1)
            if step == longest - 1:
                add(c, sums[c], 0, [slot(c, way, reaches[c][way] - 1) for way in (0, 1)])
                spread = Spread(group, sums[c], outs[c], cube_send.at[c], cube_recv.at[c])
                copy = pltpu.make_async_copy(sums[c], outs[c].at[0], local.at[c])
                copy.start()
                kept.append(copy)
                spread.level()
                spreads.append(spread)
    for spread in spreads:
        spread.level()
    for spread in spreads:
        spread.finish()
    for copy in list(copies.values()) + turns:
        copy.wait_send()
    for copy in kept:
        copy.wait()


def reduce_all(blocks, terms, n_dp, n_u):
    count = len(terms) + 1
    anywhere = pl.BlockSpec(memory_space=pl.ANY)
    local = pl.BlockSpec(memory_space=pltpu.VMEM)
    longest = n_dp // 2
    whole = (blocks.shape[0] * blocks.shape[1], blocks.shape[2])
    sizes = [(r // n_dp, c) for r, c in [t.shape for t in terms] + [whole]]
    dma = pltpu.SemaphoreType.DMA
    return pl.pallas_call(
        functools.partial(reduce_kernel, n_dp, n_u, count),
        in_specs=[local] * count,
        out_specs=[anywhere] * count,
        out_shape=[jax.ShapeDtypeStruct((n_u,) + b, jnp.bfloat16) for b in sizes],
        scratch_shapes=[pltpu.VMEM((2, longest) + b, jnp.bfloat16) for b in sizes]
        + [pltpu.VMEM(b, jnp.bfloat16) for b in sizes]
        + [
            pltpu.VMEM(whole, jnp.bfloat16),
            dma((count, 2, longest)), dma((count, 2, longest)), dma((count, n_u - 1)), dma((count, n_u - 1)),
            dma((n_u - 1,)), dma((n_u - 1,)), dma((count + 1,)),
        ],
        compiler_params=pltpu.CompilerParams(vmem_limit_bytes=VMEM_LIMIT, collective_id=1, has_side_effects=True),
        cost_estimate=cost(),
        name="reduce_all",
    )(blocks, *terms)


START = 0.9
LATENCY = 2.0
RATES = {"ring": 36.0, "x": 50.0, "core": 250.0}


class Flight:
    def __init__(self, value, arrival):
        self.value, self.arrival = value, arrival


class Sequence:
    def __init__(self):
        self.last = ()
        self.now = 0.0
        self.free = {}
        self.sources = []
        self.fillers = []

    def tie(self, *values):
        tied, _ = lax.optimization_barrier((values, self.last))
        self.last = tied
        return tied

    def run(self, cost, function, *values):
        self.poll()
        out = function(*self.tie(*values))
        self.now += cost
        if isinstance(out, (tuple, list)):
            return self.tie(*out)
        return self.tie(out)[0]

    def fly(self, value, axis, pairs, link, kind):
        (value,) = self.tie(value)
        got = lax.ppermute(value, axis, pairs)
        start = max(self.now + START, self.free.get(link, 0.0))
        end = start + value.size * value.dtype.itemsize / 1000.0 / RATES[kind]
        self.free[link] = end
        self.now += START
        return Flight(got, end + LATENCY)

    def land(self, *flights):
        self.idle(max(f.arrival for f in flights))
        return self.tie(*[f.value for f in flights])

    def poll(self):
        moved = True
        while moved:
            moved = any([source.poll(self.now) for source in self.sources])

    def later(self, cost, ready, function):
        self.fillers.append((cost, ready, function))

    def fill(self):
        for at, (cost, ready, function) in enumerate(self.fillers):
            if ready():
                self.fillers.pop(at)
                function()
                return True
        return False

    def idle(self, until):
        while True:
            self.poll()
            if self.now >= until:
                return
            if until - self.now > 2.0 and self.fill():
                continue
            events = [e for source in self.sources for e in [source.next()] if e is not None]
            self.now = max(self.now, min(events + [until]))

    def drain(self, done):
        while not done():
            self.poll()
            if done():
                return
            if self.fill():
                continue
            events = [e for source in self.sources for e in [source.next()] if e is not None]
            assert events
            self.now = max(self.now, min(events))


def pick(value, index):
    return lax.dynamic_index_in_dim(value, index, 0, keepdims=False, allow_negative_indices=False)


def ring_order(count):
    evens = list(range(0, count, 2))
    odds = list(range(1, count, 2))
    return evens + odds[::-1]


class Ring:
    def __init__(self, axis):
        self.axis = axis
        self.count = lax.axis_size(axis)
        order = ring_order(self.count)
        place = [0] * self.count
        for position, index in enumerate(order):
            place[index] = position
        me = lax.axis_index(axis)
        owners = [[order[(place[i] + o) % self.count] for o in range(self.count)] for i in range(self.count)]
        self.owners = pick(jnp.array(owners, jnp.int32), me)
        following = [(order[k], order[(k + 1) % self.count]) for k in range(self.count)]
        self.pairs = (following, [(b, a) for a, b in following])

    def reach(self, more_ahead):
        longer = self.count // 2
        shorter = self.count - 1 - longer
        return (longer, shorter) if more_ahead else (shorter, longer)

    def owner(self, offset):
        return self.owners[offset % self.count]


class ReduceChain:
    def __init__(self, ring, more_ahead):
        self.ring = ring
        self.reach = ring.reach(more_ahead)
        self.terms = None
        self.moving = [None, None]
        self.seen = [None, None]

    def have(self, *parts):
        self.terms = parts

    def ready(self, way, step):
        return self.terms is not None and (step == self.reach[way] or self.seen[way] == step + 1)

    def entries(self, way):
        return [(self, step) for step in range(self.reach[way], 0, -1)]

    def operand(self, way, step):
        offset = (step if way == 0 else -step) % self.ring.count
        arrived = [self.moving[way]] if step < self.reach[way] else []
        return (self.terms, offset, arrived)

    def deliver(self, way, step, value):
        self.moving[way] = value
        self.seen[way] = step


def totals(seq, *chains):
    return apply_sums(seq, [(c.terms, 0, list(c.moving)) for c in chains])


def apply_sums(seq, chains):
    flat = []
    for parts, _, arrived in chains:
        flat.extend([terms for terms, _ in parts] + arrived)

    def call(*values):
        values = list(values)
        rebuilt = []
        for parts, offset, arrived in chains:
            new = [(values.pop(0), at) for _, at in parts]
            rebuilt.append((new, offset, [values.pop(0) for _ in arrived]))
        return tuple(ring_sums(rebuilt))

    return seq.run(1.6 * len(chains) + 0.8, call, *flat)


def alternate(*lists):
    out = []
    for at in range(max(len(x) for x in lists)):
        out.extend(x[at] for x in lists if at < len(x))
    return out


class Pump:
    def __init__(self, seq, ring, queues, window):
        self.seq, self.ring, self.queues = seq, ring, queues
        self.window = window
        self.flying = ([], [])
        self.busy = False
        seq.sources.append(self)

    def send(self):
        sends = []
        for way in (0, 1):
            room = self.window - len(self.flying[way])
            while self.queues[way] and room > 0 and self.queues[way][0][0].ready(way, self.queues[way][0][1]):
                chain, step = self.queues[way].pop(0)
                sends.append((way, chain, step, chain.operand(way, step)))
                room -= 1
        if not sends:
            return False
        self.busy = True
        sums = [k for k, s in enumerate(sends) if isinstance(s[1], ReduceChain)]
        values = [s[3] for s in sends]
        if sums:
            for k, value in zip(sums, apply_sums(self.seq, [values[k] for k in sums])):
                values[k] = value
        for (way, chain, step, _), value in zip(sends, values):
            flight = self.seq.fly(value, self.ring.axis, self.ring.pairs[way], ("ring", way), "ring")
            self.flying[way].append((chain, step, flight))
        self.busy = False
        return True

    def poll(self, now):
        if self.busy:
            return False
        waits = []
        for way in (0, 1):
            if self.flying[way] and self.flying[way][0][2].arrival <= now + 0.5:
                waits.append((way,) + self.flying[way].pop(0))
        if waits:
            values = self.seq.tie(*[w[3].value for w in waits])
            for (way, chain, step, _), value in zip(waits, values):
                chain.deliver(way, step, value)
        return self.send() or bool(waits)

    def next(self):
        arrivals = [f[0][2].arrival for f in self.flying if f]
        return min(arrivals) if arrivals else None

    def left(self, *chains):
        return any(e[0] in chains for way in (0, 1) for e in self.queues[way] + self.flying[way])

    def until(self, *chains):
        self.seq.drain(lambda: not self.left(*chains))


class Cube:
    def __init__(self, axis, seq):
        self.axis = axis
        self.seq = seq
        self.count = lax.axis_size(axis)
        self.me = lax.axis_index(axis)
        bits = []
        bit = 1
        while bit < self.count:
            bits.append(bit)
            bit *= 2
        self.bits = bits

    def swap(self, value, bit):
        kind = "core" if bit == 1 else "x"
        return self.seq.fly(value, self.axis, [(i, i ^ bit) for i in range(self.count)], kind, kind)

    def gather(self, item):
        keys, blocks = [[0]], [item[None]]
        for bit in self.bits[::-1]:
            order = sorted((key, at, sub) for at, ks in enumerate(keys) for sub, key in enumerate(ks))
            if len(order) > 1:
                sent = self.seq.run(
                    2.0, lambda *b: jnp.concatenate([b[at][sub : sub + 1] for _, at, sub in order]), *blocks
                )
            else:
                sent = blocks[0]
            (got,) = yield [self.swap(sent, bit)]
            keys = keys + [[key ^ bit for key, _, _ in order]]
            blocks = blocks + [got]
        return (keys, blocks)

    def joined(self, held):
        keys, blocks = held
        order = sorted((key, at, sub) for at, ks in enumerate(keys) for sub, key in enumerate(ks))
        return self.seq.run(3.0, lambda *b: jnp.concatenate([b[at][sub : sub + 1] for _, at, sub in order]), *blocks)

    def reduce(self, keep, send):
        for bit in self.bits:
            (got,) = yield [self.swap(send, bit)]
            if bit != self.bits[-1]:
                keep, send = self.seq.run(4.4, halve, keep, got)
        return (keep[0], got[0])

    def turn(self, blocks):
        got = yield [self.swap(blocks[bit], bit) for bit in range(1, self.count)]
        return [blocks[0]] + list(got)

    def total(self, value, axes):
        for axis in axes:
            count = lax.axis_size(axis)
            bit = 1
            while bit < count:
                pairs = [(i, i ^ bit) for i in range(count)]
                (got,) = yield [self.seq.fly(value, axis, pairs, "sum", "ring")]
                value = self.seq.run(1.0, lambda a, b: a + b, value, got)
                bit *= 2
        return value


class Task:
    def __init__(self, seq, generator, urgent=True):
        self.seq, self.generator = seq, generator
        self.value, self.flights, self.over, self.busy = None, None, False, False
        seq.sources.append(self)
        self.go(None)

    def go(self, values):
        self.busy = True
        try:
            self.flights = self.generator.send(values)
        except StopIteration as stop:
            self.value, self.over = stop.value, True
            self.seq.sources.remove(self)
        self.busy = False

    def next(self):
        return None if self.busy or self.over else max(f.arrival for f in self.flights)

    def poll(self, now):
        if self.busy or self.over or self.next() > now + 0.5:
            return False
        self.go(self.seq.tie(*[f.value for f in self.flights]))
        return True

    def finish(self):
        while not self.over:
            if self.busy:
                raise RuntimeError
            self.seq.idle(self.next())
        return self.value


def dot(a, b):
    return jnp.einsum("mk,kn->mn", a, b, preferred_element_type=jnp.float32)


def dot_nt(a, b):
    return jnp.einsum("mk,nk->mn", a, b, preferred_element_type=jnp.float32)


def dot_tn(a, b):
    return jnp.einsum("km,kn->mn", a, b, preferred_element_type=jnp.float32)


def low(value):
    return value.astype(jnp.bfloat16)


def high(value):
    return value.astype(jnp.float32)


def shards(
    tokens,
    seq_lengths,
    cotangent,
    norm1_gain,
    input_weight,
    query_gain,
    key_gain,
    output_weight,
    norm2_gain,
    perceptron_input_weight,
    down_weight,
):
    _, rows, width = tokens.shape
    seq = Sequence()
    cube = Cube("ulysses", seq)
    ring = Ring("dp")
    n_dp = ring.count
    n_u, me = cube.count, cube.me
    bucket = rows * n_u
    depth = width // n_dp
    heads = QUERY_HEADS // n_u
    kv_heads = KEY_VALUE_HEADS // n_u
    copies = QUERY_HEADS // KEY_VALUE_HEADS
    head_width = HEAD_DIMENSION
    q_w, kv_w = heads * head_width, kv_heads * head_width
    query_width = QUERY_HEADS * head_width
    kv_all = KEY_VALUE_HEADS * head_width
    ff_strip = FF // n_dp // n_u
    ff_local = FF // n_u
    half = width // 2
    out_cols = width // n_u
    place = jnp.stack([seq_lengths[0], me])
    length = seq_lengths[0]
    q_gain, k_gain = query_gain[None], key_gain[None]
    gain_one, gain_two = norm1_gain[None], norm2_gain[None]
    positions = me * rows + jnp.arange(rows)
    def cut(value, start, size):
        return lax.dynamic_slice_in_dim(value, start, size, 1)

    def task(generator):
        return Task(seq, generator)

    r_gate = ReduceChain(ring, True)
    pump = Pump(seq, ring, [r_gate.entries(way) for way in (0, 1)], 1)

    frequency = np.float32(ROPE_BASE) ** (np.float32(-2.0) * np.arange(head_width // 2, dtype=np.float32) / head_width)
    angles = np.arange(bucket, dtype=np.float32)[:, None] * frequency.astype(np.float32)[None, :]
    cosine, sine = np.cos(angles), np.sin(angles)
    tables = (
        jnp.asarray(np.concatenate([cosine, cosine], axis=1), jnp.float32),
        jnp.asarray(np.concatenate([-sine, sine], axis=1), jnp.float32),
    )

    gate_item, up_item = seq.run(
        4.9, lambda p, w: take_strips(p, w, n_dp, n_u, ff_strip), place, perceptron_input_weight
    )
    out_item, qk_item, vg_item, grad_own, down_item = seq.run(
        3.0,
        lambda o, w, c, d: (
            cut(o, me * out_cols, out_cols),
            jnp.concatenate([cut(w, me * q_w, q_w), cut(w, query_width + me * kv_w, kv_w)], axis=1),
            jnp.concatenate(
                [
                    cut(w, query_width + kv_all + me * kv_w, kv_w),
                    cut(w, query_width + 2 * kv_all + me * q_w, q_w),
                ],
                axis=1,
            ),
            jnp.where((positions < length)[:, None], c, jnp.zeros_like(c)),
            lax.dynamic_slice_in_dim(d, me * ff_strip, ff_strip, 0),
        ),
        output_weight,
        input_weight,
        cotangent[0],
        down_weight,
    )
    (
        w_qk, w_vg, w_gate, w_up, w_down, normed, grad_result, second,
        raw_qk, raw_vg, queries, keys, values, gate, attended, gated, log_totals, w_out, hidden_in,
    ) = seq.run(
        250.0,
        lambda t, g, *items: forward(
            seq_lengths, t, (gain_one, gain_two, q_gain, k_gain), tables, g, items, n_dp, n_u, heads, kv_heads
        ),
        tokens[0], grad_own, out_item, qk_item, vg_item, gate_item, up_item, down_item,
    )
    normed, grad_result = normed.reshape(bucket, width), grad_result.reshape(bucket, width)
    second, gated = second.reshape(bucket, width), gated.reshape(bucket, q_w)

    def even_odd(value):
        value = low(value).reshape(n_u, rows, width)
        return (value[0::2], value[1::2])

    act_gate, act_up, hidden = seq.run(20.0, gate_up, second, w_gate, w_up)
    down_own = lax.psum_scatter(
        seq.run(10.7, lambda h, g: low(dot_tn(h, g)), hidden, grad_result), "dp", scatter_dimension=0, tiled=True
    )

    grad_gate, grad_up = seq.run(15.5, down_back, grad_result, act_gate, act_up, w_down)
    gate_terms = seq.run(12.5, lambda a, b: outer_terms(a, b, n_dp), second, grad_gate)
    r_gate.have((gate_terms.reshape(n_dp, depth, ff_local), ring.owners))
    pump.send()

    def input_grads(a, b, first, second):
        return back_matmul(a, b, first, second, rows)

    two_keep, two_send = seq.run(20.5, input_grads, grad_gate, grad_up, w_gate, w_up)
    t_two = task(cube.reduce(two_keep, two_send))
    up_own = lax.psum_scatter(
        seq.run(12.5, lambda a, b: outer_terms(a, b, n_dp), second, grad_up), "dp", scatter_dimension=0, tiled=True
    )
    down_keep, down_send = seq.run(11.5, lambda h, w: even_odd(dot(h, w)), hidden, w_down)
    grad_hidden_in, branch_own, gain_two_own = seq.run(
        5.8, lambda *a: norm_back(*a, True), hidden_in, *t_two.finish(), grad_own, gain_two
    )
    t_branch_grad = task(cube.gather(branch_own))
    branch_grad = cube.joined(t_branch_grad.finish()).reshape(bucket, width)

    grad_gated = seq.run(3.8, dot_nt, branch_grad, w_out)
    pump.until(r_gate)
    t_gate_all = task(cube.gather(totals(seq, r_gate)[0]))
    t_down = task(cube.reduce(down_keep, down_send))
    t_down_all = task(cube.gather(seq.tie(down_own)[0]))
    grad_qk, grad_vg, gain_query_own, gain_key_own = seq.run(
        20.0,
        attend_back,
        place, raw_qk, queries, keys, values, gate, attended, grad_gated.reshape(n_u, rows, q_w), log_totals,
        q_gain, k_gain, *tables,
    )
    grad_qk, grad_vg = grad_qk.reshape(bucket, -1), grad_vg.reshape(bucket, -1)
    one_keep, one_send = seq.run(12.0, input_grads, grad_qk, grad_vg, w_qk, w_vg)
    t_one = task(cube.reduce(one_keep, one_send))
    out_parts = seq.run(7.0, lambda p, a, b: out_terms(p, a, b, n_u), place, gated, branch_grad)
    qk_terms = seq.run(9.3, lambda a, b: outer_terms(a, b, n_dp), normed, grad_qk)
    vg_terms = seq.run(9.3, lambda a, b: outer_terms(a, b, n_dp), normed, grad_vg)

    qk_all, vg_all, out_all = seq.run(
        100.0, lambda b, *t: reduce_all(b, t, n_dp, n_u), out_parts, qk_terms, vg_terms
    )
    t_up_all = task(cube.gather(seq.tie(up_own)[0]))
    tokens_grad, gain_one_own = seq.run(
        5.6, lambda *a: norm_back(*a, False), tokens[0], *t_one.finish(), grad_hidden_in, gain_one
    )
    gains = seq.run(
        1.0, lambda *g: jnp.concatenate(g, axis=1)[0], gain_one_own, gain_query_own, gain_key_own, gain_two_own
    )
    t_gains = task(cube.total(gains, ("ulysses", "dp")))
    keys_all = [list(range(n_u))]
    in_all = seq.run(
        5.5,
        lambda p, a, b: put_columns(
            p, [(keys_all, [a]), (keys_all, [b])], [[(0, q_w), (q_w, kv_w)], [(0, kv_w), (kv_w, q_w)]]
        ),
        place, qk_all, vg_all,
    )
    out_all = seq.run(4.0, lambda p, a: put_columns(p, [(keys_all, [a])], [[(0, out_cols)]]), place, out_all)
    down_held = t_down_all.finish()
    down_all = seq.run(5.3, lambda p, *b: put_rows(p, (down_held[0], b)), place, *down_held[1])
    up_held = t_up_all.finish()
    gate_held = t_gate_all.finish()

    def whole_mlp(p, *blocks):
        count = len(blocks) // 2
        both = [(up_held[0], blocks[:count]), (up_held[0], blocks[count:])]
        return put_strips(p, both, n_dp, ff_strip)

    mlp_all = seq.run(10.0, whole_mlp, place, *gate_held[1], *up_held[1])
    layer_out = seq.run(2.2, lambda a, b, c: a + high(b) + high(c), hidden_in, *t_down.finish())
    gains = t_gains.finish()

    gain_one_sum = gains[:width]
    gain_query_sum = gains[width : width + head_width]
    gain_key_sum = gains[width + head_width : width + 2 * head_width]
    gain_two_sum = gains[width + 2 * head_width :]
    return (
        layer_out[None],
        tokens_grad[None],
        gain_one_sum,
        in_all,
        gain_query_sum,
        gain_key_sum,
        out_all,
        gain_two_sum,
        mlp_all,
        down_all,
    )


def solution(mesh):
    placed = (
        P("dp", "ulysses", None),
        P("dp"),
        P("dp", "ulysses", None),
        P(),
        P("dp", None),
        P(),
        P(),
        P("dp", None),
        P(),
        P("dp", None),
        P("dp", None),
    )
    return jax.shard_map(
        shards,
        mesh=mesh,
        in_specs=placed,
        out_specs=(
            P("dp", "ulysses", None),
            P("dp", "ulysses", None),
            P(),
            P("dp", None),
            P(),
            P(),
            P("dp", None),
            P(),
            P("dp", None),
            P("dp", None),
        ),
        check_vma=False,
    )
```

```python
import functools

import jax
import jax.numpy as jnp
import numpy as np
from jax import lax
from jax.experimental import pallas as pl
from jax.experimental.pallas import tpu as pltpu
from jax.sharding import PartitionSpec as P

QUERY_HEADS = 16
KEY_VALUE_HEADS = 8
HEAD_DIMENSION = 128
FF = 6144


EPSILON = 1e-06
ROPE_BASE = 1000000.0
MASKED = -1e30


def rms_scale(values):
    return lax.rsqrt(jnp.mean(values * values, axis=-1, keepdims=True) + EPSILON)


VMEM_LIMIT = 56 * 1024 * 1024
NT = (((1,), (1,)), ((), ()))
TN = (((0,), (0,)), ((), ()))


def params():
    return pltpu.CompilerParams(vmem_limit_bytes=VMEM_LIMIT)


def cost(*_):
    return pl.CostEstimate(flops=1, bytes_accessed=1, transcendentals=0)


def steady(shape):
    return pl.BlockSpec(shape, lambda *_: (0,) * len(shape), pipeline_mode=pl.Buffered(1))


def tile_of(size):
    return 256 if size % 256 == 0 else 128


def head_scale(raw):
    return lax.rsqrt(jnp.mean(raw * raw, axis=-1, keepdims=True) + EPSILON)


def turn_pairs(value, cosine, sine):
    return value * cosine + pltpu.roll(value, HEAD_DIMENSION // 2, 1) * sine


def masked_scores(q, k, first_row, length):
    scores = lax.dot_general(q, k, NT, preferred_element_type=jnp.float32)
    scores = scores * HEAD_DIMENSION ** (-0.5)
    row = first_row + lax.broadcasted_iota(jnp.int32, scores.shape, 0)
    column = lax.broadcasted_iota(jnp.int32, scores.shape, 1)
    return jnp.where((column <= row) & (column < length), scores, MASKED)


def in_order(ref, me):
    return jnp.concatenate([ref[me ^ t] for t in range(ref.shape[0])], axis=0)


def attend_back_kernel(
    block, copies, heads, kv_heads, place_ref, q_raw, k_raw, q_ref, k_ref, v_ref, gate_ref, attended_ref, up_ref,
    total_ref, q_gain, k_gain, cosine, sine, qk_out, vg_out, q_gain_out, k_gain_out, grad_ref, dq_ref, dk_ref, dv_ref,
):
    group = pl.program_id(0)
    bucket, size = k_ref.shape
    n_u, rows_own, _ = q_raw.shape
    scale = size ** (-0.5)
    length, me = place_ref[0], place_ref[1]

    @pl.when(group == 0)
    def _():
        q_gain_out[...] = jnp.zeros_like(q_gain_out)
        k_gain_out[...] = jnp.zeros_like(k_gain_out)

    def store(out, at, width, value):
        for t in range(n_u):
            out[me ^ t, :, pl.ds(pl.multiple_of(at, size), width)] = value[t * rows_own : (t + 1) * rows_own]

    up, gate = in_order(up_ref, me), gate_ref[...]
    grad_ref[...] = (up * gate).astype(jnp.bfloat16)
    grad_gate = (up * attended_ref[...].astype(jnp.float32) * gate * (1.0 - gate)).astype(jnp.bfloat16)
    store(vg_out, (kv_heads + group * copies) * size, copies * size, grad_gate)
    dk_ref[...] = jnp.zeros_like(dk_ref)
    dv_ref[...] = jnp.zeros_like(dv_ref)

    def norm_grad(raw, gain, upstream, gain_out):
        factor = head_scale(raw)
        weighted = upstream * gain
        inner = jnp.mean(weighted * raw, axis=-1, keepdims=True)
        gain_out[...] += jnp.sum(upstream * raw * factor, axis=0, keepdims=True)
        return (factor * weighted - raw * (factor * factor * factor) * inner).astype(jnp.bfloat16)

    raw_q = in_order(q_raw, me)
    for copy in range(copies):
        columns = slice(copy * size, (copy + 1) * size)
        for first in range(0, bucket, block):
            rows = slice(first, first + block)
            reach = slice(0, first + block)
            q, g = q_ref[rows, columns], grad_ref[rows, columns]
            soft = jnp.exp(masked_scores(q, k_ref[reach], first, length) - total_ref[copy, rows])
            soft_grad = lax.dot_general(g, v_ref[reach], NT, preferred_element_type=jnp.float32)
            inner = jnp.sum(soft * soft_grad, axis=-1, keepdims=True)
            score_grad = (soft * (soft_grad - inner)).astype(jnp.bfloat16)
            dq_ref[rows] = jnp.dot(score_grad, k_ref[reach], preferred_element_type=jnp.float32) * scale
            dk_ref[reach] += lax.dot_general(score_grad, q, TN, preferred_element_type=jnp.float32)
            dv_ref[reach] += lax.dot_general(soft.astype(jnp.bfloat16), g, TN, preferred_element_type=jnp.float32)
        plain = turn_pairs(dq_ref[...].astype(jnp.bfloat16).astype(jnp.float32), cosine[...], -sine[...])
        store(qk_out, (group * copies + copy) * size, size, norm_grad(raw_q[:, columns], q_gain[...], plain, q_gain_out))
    plain = turn_pairs((dk_ref[...] * scale).astype(jnp.bfloat16).astype(jnp.float32), cosine[...], -sine[...])
    store(qk_out, (heads + group) * size, size, norm_grad(in_order(k_raw, me), k_gain[...], plain, k_gain_out))
    store(vg_out, group * size, size, dv_ref[...].astype(jnp.bfloat16))


def attend_back(place, raw_qk, q, k, v, gate, attended, upstream, totals, q_gain, k_gain, cosine, sine):
    size = HEAD_DIMENSION
    n_u, rows_own, _ = raw_qk.shape
    bucket = n_u * rows_own
    heads, kv_heads = q.shape[1] // size, k.shape[1] // size
    copies = heads // kv_heads

    def blocks(width, start):
        return pl.BlockSpec((n_u, rows_own, width), lambda g: (0, 0, start + g))

    wide = pl.BlockSpec((bucket, copies * size), lambda g: (0, g))
    slim = pl.BlockSpec((bucket, size), lambda g: (0, g))
    total = (heads + kv_heads) * size
    whole = pl.BlockSpec((n_u, rows_own, total), lambda g: (0, 0, 0))
    gain = pl.BlockSpec((1, size), lambda g: (0, 0))
    return pl.pallas_call(
        functools.partial(attend_back_kernel, min(256, bucket), copies, heads, kv_heads),
        grid=(kv_heads,),
        in_specs=[
            pl.BlockSpec(memory_space=pltpu.SMEM),
            blocks(copies * size, 0),
            blocks(size, heads),
            wide,
            slim,
            slim,
            wide,
            wide,
            blocks(copies * size, 0),
            pl.BlockSpec((copies, bucket, 1), lambda g: (g, 0, 0)),
            steady((1, size)),
            steady((1, size)),
            steady((bucket, size)),
            steady((bucket, size)),
        ],
        out_specs=[whole, whole, gain, gain],
        out_shape=[
            jax.ShapeDtypeStruct((n_u, rows_own, total), jnp.bfloat16),
            jax.ShapeDtypeStruct((n_u, rows_own, total), jnp.bfloat16),
            jax.ShapeDtypeStruct((1, size), jnp.float32),
            jax.ShapeDtypeStruct((1, size), jnp.float32),
        ],
        scratch_shapes=[
            pltpu.VMEM((bucket, copies * size), jnp.bfloat16),
            pltpu.VMEM((bucket, size), jnp.float32),
            pltpu.VMEM((bucket, size), jnp.float32),
            pltpu.VMEM((bucket, size), jnp.float32),
        ],
        compiler_params=params(),
        cost_estimate=cost(5 * heads * bucket * bucket * size, 24 * bucket * heads * size, heads * bucket * bucket // 2),
        name="attention_back",
    )(place, raw_qk, raw_qk, q, k, v, gate, attended, upstream, totals, q_gain, k_gain, cosine, sine)


def back_matmul(a, b, first, second, rows):
    m, n = a.shape
    width = first.shape[0]
    part = 256

    def kernel(a_ref, b_ref, first_ref, second_ref, keep_ref, send_ref):
        for at in range(0, width, part):
            where = slice(at, at + part)
            out = lax.dot_general(a_ref[...], first_ref[where], NT, preferred_element_type=jnp.float32)
            out += lax.dot_general(b_ref[...], second_ref[where], NT, preferred_element_type=jnp.float32)
            out = out.astype(jnp.bfloat16)
            keep_ref[0, :, where] = out[:rows]
            send_ref[0, :, where] = out[rows:]

    step = pl.BlockSpec((2 * rows, n), lambda i: (i, 0))
    out = pl.BlockSpec((1, rows, width), lambda i: (i, 0, 0))
    shape = jax.ShapeDtypeStruct((m // rows // 2, rows, width), jnp.bfloat16)
    return pl.pallas_call(
        kernel,
        grid=(m // rows // 2,),
        in_specs=[step, step, steady(first.shape), steady(second.shape)],
        out_specs=[out, out],
        out_shape=[shape, shape],
        compiler_params=params(),
        cost_estimate=cost(),
        name="back_matmul",
    )(a, b, first, second)


def outer_terms(x, y, count):
    m, width = x.shape
    n = y.shape[1]
    depth = width // count

    def kernel(x_ref, y_ref, out_ref):
        out_ref[...] = lax.dot_general(x_ref[...], y_ref[...], TN, preferred_element_type=jnp.float32).astype(jnp.bfloat16)

    return pl.pallas_call(
        kernel,
        grid=(count,),
        in_specs=[pl.BlockSpec((m, depth), lambda k: (0, k)), steady((m, n))],
        out_specs=pl.BlockSpec((depth, n), lambda k: (k, 0)),
        out_shape=jax.ShapeDtypeStruct((width, n), jnp.bfloat16),
        compiler_params=params(),
        cost_estimate=cost(2 * m * n * width, 2 * m * width + 2 * m * n + 2 * n * width),
        name="outer_terms",
    )(x, y)


def down_back(upstream, a, b, weight):
    m, width = upstream.shape
    n = a.shape[1]
    rows = min(256, m)

    def kernel(up_ref, a_ref, b_ref, weight_ref, gate_out, up_out):
        grad = lax.dot_general(up_ref[...], weight_ref[...], NT, preferred_element_type=jnp.float32)
        a, b = a_ref[...], b_ref[...]
        sig = jax.nn.sigmoid(a)
        gate_out[...] = (grad * b * sig * (1.0 + a * (1.0 - sig))).astype(jnp.bfloat16)
        up_out[...] = (grad * a * sig).astype(jnp.bfloat16)

    step = pl.BlockSpec((rows, n), lambda i: (i, 0))
    shape = jax.ShapeDtypeStruct((m, n), jnp.bfloat16)
    return pl.pallas_call(
        kernel,
        grid=(m // rows,),
        in_specs=[pl.BlockSpec((rows, width), lambda i: (i, 0)), step, step, steady((n, width))],
        out_specs=[step, step],
        out_shape=[shape, shape],
        compiler_params=params(),
        cost_estimate=cost(2 * m * n * width, 2 * m * width + 12 * m * n + 2 * n * width),
        name="down_back",
    )(upstream, a, b, weight)


def strips_kernel(n_dp, n_u, strip, place_ref, w_ref, gate_ref, up_ref):
    for t in range(n_u):

        @pl.when(place_ref[1] == t)
        def _():
            for half, out in enumerate((gate_ref, up_ref)):
                starts = [((half * n_dp + b) * n_u + t) * strip for b in range(n_dp)]
                out[...] = jnp.concatenate([w_ref[:, s : s + strip] for s in starts], axis=1)


def take_strips(place, w, n_dp, n_u, strip):
    depth, total = w.shape
    rows = 64
    out = pl.BlockSpec((rows, n_dp * strip), lambda i: (i, 0))
    shape = jax.ShapeDtypeStruct((depth, n_dp * strip), w.dtype)
    return pl.pallas_call(
        functools.partial(strips_kernel, n_dp, n_u, strip),
        grid=(depth // rows,),
        in_specs=[pl.BlockSpec(memory_space=pltpu.SMEM), pl.BlockSpec((rows, total), lambda i: (i, 0))],
        out_specs=[out, out],
        out_shape=[shape, shape],
        compiler_params=params(),
        cost_estimate=cost(0, 2 * depth * total + 4 * depth * n_dp * strip),
        name="take_strips",
    )(place, w)


def fill(scratch, keys, refs):
    for key_list, ref in zip(keys, refs):
        for at, key in enumerate(key_list):
            scratch[key] = ref[at]


def put_call(kernel, place, helds, grid, blocks, at, out_block, out_at, out_shape, name):
    n_u = sum(len(k) for k in helds[0][0])
    count = sum(len(b) for _, b in helds)

    def body(place_ref, *refs):
        refs = list(refs)
        scratches = refs[count + 1 :]
        for (keys, _), scratch in zip(helds, scratches):
            fill(scratch, keys, [refs.pop(0) for _ in keys])
        kernel(place_ref[1], scratches, refs[0])

    return pl.pallas_call(
        body,
        grid=(grid,),
        in_specs=[pl.BlockSpec(memory_space=pltpu.SMEM)]
        + [pl.BlockSpec((len(k),) + block, at) for (keys, _), block in zip(helds, blocks) for k in keys],
        out_specs=pl.BlockSpec(out_block, out_at),
        out_shape=jax.ShapeDtypeStruct(out_shape, jnp.float32),
        scratch_shapes=[pltpu.VMEM((n_u,) + block, jnp.bfloat16) for block in blocks],
        compiler_params=params(),
        cost_estimate=cost(0, 6 * out_shape[0] * out_shape[1]),
        name=name,
    )(place, *[v for _, held in helds for v in held])


def put_strips(place, helds, n_dp, strip):
    n_u = sum(len(k) for k in helds[0][0])
    depth, width = helds[0][1][0].shape[1:]
    rows = min(32, depth)

    def kernel(me, scratches, out_ref):
        size = n_u * strip
        for h, scratch in enumerate(scratches):
            parts = [scratch[me ^ t].astype(jnp.float32) for t in range(n_u)]
            for b in range(n_dp):
                at = (h * n_dp + b) * size
                out_ref[:, at : at + size] = jnp.concatenate(
                    [p[:, b * strip : (b + 1) * strip] for p in parts], axis=1
                )

    total = len(helds) * n_u * width
    return put_call(
        kernel, place, helds, depth // rows, [(rows, width)] * len(helds), lambda i: (0, i, 0),
        (rows, total), lambda i: (i, 0), (depth, total), "put_strips",
    )


def put_columns(place, helds, sections):
    n_u = sum(len(k) for k in helds[0][0])
    depth = helds[0][1][0].shape[1]
    rows = min(64, depth)

    def kernel(me, scratches, out_ref):
        at = 0
        for scratch, parts in zip(scratches, sections):
            for start, size in parts:
                for t in range(n_u):
                    out_ref[:, at : at + size] = scratch[me ^ t, :, start : start + size].astype(jnp.float32)
                    at += size

    total = n_u * sum(size for parts in sections for _, size in parts)
    return put_call(
        kernel, place, helds, depth // rows, [(rows, held[0].shape[2]) for _, held in helds], lambda i: (0, i, 0),
        (rows, total), lambda i: (i, 0), (depth, total), "put_columns",
    )


def put_rows(place, held):
    n_u = sum(len(k) for k in held[0])
    depth, width = held[1][0].shape[1:]
    tile = 512

    def kernel(me, scratches, out_ref):
        for t in range(n_u):
            out_ref[t * depth : (t + 1) * depth] = scratches[0][me ^ t].astype(jnp.float32)

    return put_call(
        kernel, place, [held], width // tile, [(depth, tile)], lambda i: (0, 0, i),
        (n_u * depth, tile), lambda i: (0, i), (n_u * depth, width), "put_rows",
    )


def norm_call(kernel, inputs, gain, outs, gain_sum, name):
    r, width = inputs[0].shape
    tile = min(64, r)
    step = pl.BlockSpec((tile, width), lambda i: (i, 0))
    one = pl.BlockSpec((1, width), lambda i: (0, 0))
    shapes = [jax.ShapeDtypeStruct((r, width), o) for o in outs]
    if gain_sum:
        shapes.append(jax.ShapeDtypeStruct((1, width), jnp.float32))
    return pl.pallas_call(
        kernel,
        grid=(r // tile,),
        in_specs=[step] * len(inputs) + [one],
        out_specs=[step] * len(outs) + [one] * gain_sum,
        out_shape=shapes,
        compiler_params=params(),
        cost_estimate=cost(0, sum(4 * v.size for v in inputs)),
        name=name,
    )(*inputs, gain)


def norm_back(source, keep, got, residual, gain, rounded):
    def kernel(source_ref, keep_ref, got_ref, residual_ref, gain_ref, *outs):
        @pl.when(pl.program_id(0) == 0)
        def _():
            outs[-1][...] = jnp.zeros_like(outs[-1])

        up = keep_ref[...] + got_ref[...].astype(jnp.float32)
        source = source_ref[...].astype(jnp.float32)
        factor = head_scale(source)
        weighted = up * gain_ref[...]
        inner = jnp.mean(weighted * source, axis=-1, keepdims=True)
        total = residual_ref[...].astype(jnp.float32) + factor * weighted
        total = total - source * (factor * factor * factor) * inner
        outs[0][...] = total
        if rounded:
            outs[1][...] = total.astype(jnp.bfloat16)
        outs[-1][...] += jnp.sum(up * source * factor, axis=0, keepdims=True)

    outs = [jnp.float32] + [jnp.bfloat16] * rounded
    return norm_call(kernel, (source, keep, got, residual), gain, outs, 1, "norm_back")


def halve(keep, got):
    pairs, (r, c) = keep.shape[0] // 2, keep.shape[1:]
    tile = min(64, r)

    def kernel(keep_ref, got_ref, even_ref, odd_ref):
        even_ref[0] = keep_ref[0].astype(jnp.float32) + got_ref[0].astype(jnp.float32)
        odd_ref[0] = (keep_ref[1].astype(jnp.float32) + got_ref[1].astype(jnp.float32)).astype(jnp.bfloat16)

    two = pl.BlockSpec((2, tile, c), lambda p, i: (p, i, 0))
    one = pl.BlockSpec((1, tile, c), lambda p, i: (p, i, 0))
    return pl.pallas_call(
        kernel,
        grid=(pairs, r // tile),
        in_specs=[two, two],
        out_specs=[one, one],
        out_shape=[jax.ShapeDtypeStruct((pairs, r, c), jnp.float32), jax.ShapeDtypeStruct((pairs, r, c), jnp.bfloat16)],
        compiler_params=params(),
        cost_estimate=cost(0, 16 * pairs * r * c),
        name="halve",
    )(keep, got)


def out_terms(place, gated, upstream, n_u):
    m, q = gated.shape
    c = upstream.shape[1] // n_u

    def kernel(place_ref, x_ref, y_ref, out_ref):
        out_ref[0] = lax.dot_general(x_ref[...], y_ref[...], TN, preferred_element_type=jnp.float32).astype(jnp.bfloat16)

    return pl.pallas_call(
        kernel,
        grid_spec=pltpu.PrefetchScalarGridSpec(
            num_scalar_prefetch=1,
            grid=(n_u,),
            in_specs=[
                pl.BlockSpec((m, q), lambda k, p: (0, 0)),
                pl.BlockSpec((m, c), lambda k, p: (0, p[1] ^ k)),
            ],
            out_specs=pl.BlockSpec((1, q, c), lambda k, p: (k, 0, 0)),
        ),
        out_shape=jax.ShapeDtypeStruct((n_u, q, c), jnp.bfloat16),
        compiler_params=params(),
        cost_estimate=cost(2 * m * q * c * n_u, 2 * m * q + 4 * m * c * n_u),
        name="out_terms",
    )(place, gated, upstream)


MESH = pl.DeviceIdType.MESH


class Group:
    def __init__(self, n_dp, n_u):
        self.n_dp, self.n_u = n_dp, n_u
        index = lax.axis_index("dp")
        self.me = lax.axis_index("ulysses")
        odd = index % 2
        self.position = (1 - odd) * (index // 2) + odd * (n_dp - 1 - index // 2)
        self.next = (self.owner(1), self.owner(-1))
        self.bits = [1 << k for k in range(n_u.bit_length() - 1)]

    def owner(self, offset):
        place = (self.position + offset + self.n_dp) % self.n_dp
        late = place // (self.n_dp // 2)
        return (1 - late) * (2 * place) + late * (2 * (self.n_dp - 1 - place) + 1)

    def greet(self):
        barrier = pltpu.get_barrier_semaphore()
        for way in (0, 1):
            pl.semaphore_signal(barrier, inc=1, device_id={"dp": self.next[way]}, device_id_type=MESH)
        for other in range(1, self.n_u):
            pl.semaphore_signal(barrier, inc=1, device_id={"ulysses": self.me ^ other}, device_id_type=MESH)
        pl.semaphore_wait(barrier, 1 + self.n_u)

    def to_ring(self, way, source, target, send, recv):
        copy = pltpu.make_async_remote_copy(
            src_ref=source, dst_ref=target, send_sem=send, recv_sem=recv,
            device_id={"dp": self.next[way]}, device_id_type=MESH,
        )
        copy.start()
        return copy

    def to_cube(self, bit, source, target, send, recv):
        copy = pltpu.make_async_remote_copy(
            src_ref=source, dst_ref=target, send_sem=send, recv_sem=recv,
            device_id={"ulysses": self.me ^ bit}, device_id_type=MESH,
        )
        copy.start()
        return copy

    def reach(self, more_ahead):
        longer = self.n_dp // 2
        shorter = self.n_dp - 1 - longer
        return (longer, shorter) if more_ahead else (shorter, longer)


class Spread:
    def __init__(self, group, own, out, send, recv):
        self.group, self.own, self.out, self.send, self.recv = group, own, out, send, recv
        self.keys, self.levels, self.copies, self.used, self.waited = [0], group.bits[::-1], [], 0, 0

    def level(self):
        for copy in self.copies[self.waited :]:
            copy.wait_recv()
        self.waited = len(self.copies)
        if not self.levels:
            return False
        bit = self.levels.pop(0)
        for key in sorted(self.keys):
            source = self.own if key == 0 else self.out.at[key]
            at = self.used
            self.copies.append(
                self.group.to_cube(bit, source, self.out.at[key ^ bit], self.send.at[at], self.recv.at[at])
            )
            self.used += 1
        self.keys += [key ^ bit for key in self.keys]
        return True

    def finish(self):
        while self.level():
            pass
        for copy in self.copies:
            copy.wait_send()


class RingGather:
    def __init__(self, group, chains, send, recv):
        self.group, self.chains, self.send_sems, self.recv_sems = group, chains, send, recv
        self.copies = {}

    def place(self, c, owner):
        _, out, block, low, rows, _ = self.chains[c]
        return out.at[pl.ds(pl.multiple_of(owner * block + low, 16), rows)]

    def item(self, c):
        item, _, _, low, rows, _ = self.chains[c]
        return item.at[low : low + rows]

    def reach(self, c, way):
        return self.group.reach(self.chains[c][5])[way]

    def send(self, c, way, step):
        owner = self.group.owner(1 - step if way == 0 else step - 1)
        source = self.item(c) if step == 1 else self.place(c, owner)
        sems = (c, way, step - 1)
        self.copies[sems] = self.group.to_ring(
            way, source, self.place(c, owner), self.send_sems.at[sems], self.recv_sems.at[sems]
        )

    def start(self, c):
        for way in (0, 1):
            self.send(c, way, 1)

    def event(self, c, way, step):
        if step <= self.reach(c, way):
            self.copies[c, way, step - 1].wait_recv()
            if step < self.reach(c, way):
                self.send(c, way, step + 1)

    def finish(self):
        for copy in self.copies.values():
            copy.wait_send()


def by_rows(count, tile, function):
    def body(i, carry):
        function(pl.ds(pl.multiple_of(i * tile, tile), tile))
        return carry

    lax.fori_loop(0, count // tile, body, 0)


def forward_kernel(
    n_dp, n_u, heads, kv_heads, length_ref, tokens_ref, gain_one, gain_two, q_gain, k_gain, cosine, sine, grad_ref,
    out_item, qk_item, vg_item, gate_item, up_item, down_item,
    w_qk, w_vg, w_gate, w_up, w_down, normed_out, grad_out, second_out, act_gate, act_up, act_hidden,
    raw_qk, raw_vg, q_out, k_out, v_out, gate_out, attended_out, gated_out, total_out, w_out, hidden_out,
    normed, own, qk_local, vg_local, columns, turned, parts, core_got, total, second_own, gate_stage, up_stage, hidden_stage,
    ring_send, ring_recv, cube_send, cube_recv, turn_send, turn_recv, sum_send, sum_recv, local,
):
    rows_own, width = tokens_ref.shape
    bucket = rows_own * n_u
    size = HEAD_DIMENSION
    copies = heads // kv_heads
    depth = width // n_dp
    group = Group(n_dp, n_u)
    me, mine = group.me, group.owner(0)
    group.greet()
    strip = down_item.shape[0]
    halves = 2 if strip % 32 == 0 else 1
    chains = [
        (out_item, columns, depth, 0, depth, True),
        (qk_item, w_qk, depth, 0, depth, False),
        (vg_item, w_vg, depth, 0, depth, True),
        (gate_item, w_gate, depth, 0, depth, True),
        (up_item, w_up, depth, 0, depth, False),
    ]
    for p in range(halves):
        chains.append((down_item, w_down, strip, p * strip // halves, strip // halves, p == 0))
    ring = RingGather(group, chains, ring_send, ring_recv)
    kept = []

    def keep(source, target):
        copy = pltpu.make_async_copy(source, target, local.at[len(kept)])
        copy.start()
        kept.append(copy)
        return copy

    for c in (0, 1, 2):
        ring.start(c)
    own_rows = lambda out, block: out.at[pl.ds(pl.multiple_of(mine * block, 16), block)]
    for item, out, block in (
        (out_item, columns, depth), (qk_item, w_qk, depth), (vg_item, w_vg, depth),
        (gate_item, w_gate, depth), (up_item, w_up, depth), (down_item, w_down, strip),
    ):
        keep(item, own_rows(out, block))

    def first(rows):
        x = tokens_ref[rows].astype(jnp.float32)
        own[rows] = (x * head_scale(x) * gain_one[...]).astype(jnp.bfloat16)

    by_rows(rows_own, 64, first)
    keep(own, normed.at[0]).wait()
    keep(grad_ref, grad_out.at[0])
    spreads = [
        Spread(group, own, normed, cube_send.at[0], cube_recv.at[0]),
        Spread(group, grad_ref, grad_out, cube_send.at[1], cube_recv.at[1]),
    ]
    spreads[0].level()
    longest = n_dp // 2
    for step in range(1, longest + 1):
        for c in (0, 1, 2):
            for way in (0, 1):
                ring.event(c, way, step)
        if step == 1:
            spreads[1].level()
        if step < longest:
            spreads[0 if step % 2 == 1 else 1].level()
        if step == longest - 1:
            for c in (3, 4):
                ring.start(c)
    spreads[0].finish()
    events = []
    for step in range(1, longest + 1):
        events += [[(3, 0, step), (4, 1, step)], [(4, 0, step), (3, 1, step)]]
        if step == longest - 1:
            events.append([("start",)])
    for step in range(1, longest + 1):
        if halves == 2:
            events += [[(5, 0, step), (6, 1, step)], [(6, 0, step), (5, 1, step)]]
        else:
            events += [[(5, 0, step), (5, 1, step)]]

    def pump(count=1):
        while count and events:
            pair = events.pop(0)
            if pair[0][0] == "start":
                for c in range(5, len(chains)):
                    ring.start(c)
                continue
            for event in pair:
                ring.event(*event)
            count -= 1

    for copy in kept[:3]:
        copy.wait()
    share = depth * n_dp // n_u
    turns = []
    for k in range(1, n_u):
        source = columns.at[pl.ds(pl.multiple_of((me ^ k) * share, 16), share)]
        turns.append(group.to_cube(k, source, turned.at[k], turn_send.at[k - 1], turn_recv.at[k - 1]))
    keep(columns.at[pl.ds(pl.multiple_of(me * share, 16), share)], turned.at[0]).wait()
    one, two = keep(w_qk, qk_local), keep(w_vg, vg_local)
    normed_copy = keep(normed, normed_out)
    one.wait()
    two.wait()

    def project(b, carry):
        x = normed[b]
        raw_qk[b] = jnp.dot(x, qk_local[...], preferred_element_type=jnp.float32)
        raw_vg[b] = jnp.dot(x, vg_local[...], preferred_element_type=jnp.float32)
        return carry

    lax.fori_loop(0, n_u, project, 0)
    normed_copy.wait()
    pump()

    length = length_ref[0]
    block = min(256, bucket)

    def attention(h, carry):
        def column(ref, at):
            at = pl.multiple_of(at * size, size)
            return jnp.concatenate([ref[me ^ t, :, pl.ds(at, size)] for t in range(n_u)], axis=0)

        at = pl.ds(pl.multiple_of(h * size, size), size)
        kv = pl.ds(pl.multiple_of(h // copies * size, size), size)
        q = column(raw_qk, h)
        q = turn_pairs(q * head_scale(q) * q_gain[...], cosine[...], sine[...]).astype(jnp.bfloat16)
        q_out[:, at] = q
        k = column(raw_qk, heads + h // copies)
        k = turn_pairs(k * head_scale(k) * k_gain[...], cosine[...], sine[...]).astype(jnp.bfloat16)
        k_out[:, kv] = k
        v = column(raw_vg, h // copies).astype(jnp.bfloat16)
        v_out[:, kv] = v
        gate = jax.nn.sigmoid(column(raw_vg, kv_heads + h))
        gate_out[:, at] = gate
        for start in range(0, bucket, block):
            rows = slice(start, start + block)
            scores = masked_scores(q[rows], k[: start + block], start, length)
            top = jnp.max(scores, axis=-1, keepdims=True)
            soft = jnp.exp(scores - top)
            sums = jnp.sum(soft, axis=-1, keepdims=True)
            out = jnp.dot(soft.astype(jnp.bfloat16), v[: start + block], preferred_element_type=jnp.float32) / sums
            out = out.astype(jnp.bfloat16)
            attended_out[rows, at] = out
            total_out[h, rows] = top + jnp.log(sums)
            gated = (out.astype(jnp.float32) * gate[rows]).astype(jnp.bfloat16)
            for t in range(start // rows_own, (start + block) // rows_own):
                inside = slice(t * rows_own - start, (t + 1) * rows_own - start)
                gated_out[me ^ t, :, at] = gated[inside]
        return carry

    lax.fori_loop(0, heads, attention, 0)
    pump()
    for copy in turns:
        copy.wait_recv()
    c_width = columns.shape[1]
    for k in range(n_u):
        w_out[:, pl.ds(pl.multiple_of((me ^ k) * c_width, c_width), c_width)] = turned[k]

    def branch(b, carry):
        parts[b] = jnp.dot(gated_out[b], w_out[...], preferred_element_type=jnp.float32).astype(jnp.bfloat16)
        return carry

    lax.fori_loop(0, n_u, branch, 0)
    held = list(range(n_u))
    used = 0
    sums = []
    for bit in group.bits:
        keys = [key for key in held if not key & bit]
        level = []
        for key in keys:
            level.append(
                group.to_cube(bit, parts.at[key | bit], core_got.at[used], sum_send.at[used], sum_recv.at[used])
            )
            used += 1
        sums += level
        pump()
        for at, (key, copy) in enumerate(zip(keys, level)):
            copy.wait_recv()
            slot = used - len(keys) + at

            def add(rows, key=key, slot=slot):
                got = core_got[slot, rows].astype(jnp.float32)
                if key:
                    parts[key, rows] = (parts[key, rows].astype(jnp.float32) + got).astype(jnp.bfloat16)
                elif bit == 1:
                    total[rows] = tokens_ref[rows].astype(jnp.float32) + parts[0, rows].astype(jnp.float32) + got
                else:
                    total[rows] = total[rows] + got

            by_rows(rows_own, 64, add)
        held = keys

    def second(rows):
        hidden = total[rows]
        hidden_out[rows] = hidden
        second_own[rows] = (hidden * head_scale(hidden) * gain_two[...]).astype(jnp.bfloat16)

    by_rows(rows_own, 64, second)
    spread = Spread(group, second_own, normed, cube_send.at[2], cube_recv.at[2])
    keep(second_own, normed.at[0])
    while spread.level():
        pump(2)
    kept[12].wait()
    second_copy = keep(normed, second_out)
    while events and events[0][0][0] in ("start", 3, 4):
        pump(1)
    for copy in kept[3:5]:
        copy.wait()
    n = qk_local.shape[1]
    for part in range(w_gate.shape[1] // n):
        where = slice(part * n, (part + 1) * n)
        at = 14 + 5 * part
        loads = [
            pltpu.make_async_copy(w_gate.at[:, where], qk_local, local.at[at]),
            pltpu.make_async_copy(w_up.at[:, where], vg_local, local.at[at + 1]),
        ]
        for copy in loads:
            copy.start()
        for copy in loads:
            copy.wait()

        def expand(b, carry):
            x = normed[b]
            one = jnp.dot(x, qk_local[...], preferred_element_type=jnp.float32)
            two = jnp.dot(x, vg_local[...], preferred_element_type=jnp.float32)
            gate_stage[b] = one
            up_stage[b] = two
            hidden_stage[b] = (one * jax.nn.sigmoid(one) * two).astype(jnp.bfloat16)
            return carry

        lax.fori_loop(0, n_u, expand, 0)
        stores = []
        for k, (stage, out) in enumerate(((gate_stage, act_gate), (up_stage, act_up), (hidden_stage, act_hidden))):
            copy = pltpu.make_async_copy(stage, out.at[:, :, where], local.at[at + 2 + k])
            copy.start()
            stores.append(copy)
        pump(2)
        for copy in stores:
            copy.wait()
    second_copy.wait()
    spreads[1].finish()
    spread.finish()
    pump(1000)
    ring.finish()
    for copy in turns + sums:
        copy.wait_send()
    for copy in kept[5:6] + kept[7:8]:
        copy.wait()


def forward(length, tokens_own, gains, tables, grad_own, items, n_dp, n_u, heads, kv_heads):
    anywhere = pl.BlockSpec(memory_space=pl.ANY)
    local = pl.BlockSpec(memory_space=pltpu.VMEM)
    rows, width = tokens_own.shape
    bucket, size = rows * n_u, HEAD_DIMENSION
    total = (heads + kv_heads) * size
    depth = width // n_dp
    columns = items[0].shape[1]
    share = width // n_u
    longest = n_dp // 2

    def shape(*dims, dtype=jnp.bfloat16):
        return jax.ShapeDtypeStruct(dims, dtype)

    out_shape = [shape(n_dp * i.shape[0], i.shape[1]) for i in items[1:]]
    out_shape += [shape(n_u, rows, width)] * 3
    hidden = items[4].shape[1]
    out_shape += [shape(n_u, rows, hidden, dtype=jnp.float32)] * 2 + [shape(n_u, rows, hidden)]
    out_shape += [shape(n_u, rows, total, dtype=jnp.float32)] * 2
    out_shape += [
        shape(bucket, heads * size), shape(bucket, kv_heads * size), shape(bucket, kv_heads * size),
        shape(bucket, heads * size, dtype=jnp.float32), shape(bucket, heads * size),
        shape(n_u, rows, heads * size), shape(heads, bucket, 1, dtype=jnp.float32),
        shape(share, width), shape(rows, width, dtype=jnp.float32),
    ]
    dma = pltpu.SemaphoreType.DMA
    return pl.pallas_call(
        functools.partial(forward_kernel, n_dp, n_u, heads, kv_heads),
        in_specs=[pl.BlockSpec(memory_space=pltpu.SMEM)] + [local] * 7 + [anywhere] * 7,
        out_specs=[anywhere] * 11 + [local] * 11,
        out_shape=out_shape,
        scratch_shapes=[
            pltpu.VMEM((n_u, rows, width), jnp.bfloat16),
            pltpu.VMEM((rows, width), jnp.bfloat16),
            pltpu.VMEM((width, total), jnp.bfloat16),
            pltpu.VMEM((width, total), jnp.bfloat16),
            pltpu.VMEM((width, columns), jnp.bfloat16),
            pltpu.VMEM((n_u, share, columns), jnp.bfloat16),
            pltpu.VMEM((n_u, rows, width), jnp.bfloat16),
            pltpu.VMEM((n_u - 1, rows, width), jnp.bfloat16),
            pltpu.VMEM((rows, width), jnp.float32),
            pltpu.VMEM((rows, width), jnp.bfloat16),
            pltpu.VMEM((n_u, rows, total), jnp.float32),
            pltpu.VMEM((n_u, rows, total), jnp.float32),
            pltpu.VMEM((n_u, rows, total), jnp.bfloat16),
            dma((7, 2, longest)), dma((7, 2, longest)), dma((3, n_u - 1)), dma((3, n_u - 1)),
            dma((n_u - 1,)), dma((n_u - 1,)), dma((n_u - 1,)), dma((n_u - 1,)), dma((14 + 5 * (hidden // total),)),
        ],
        compiler_params=pltpu.CompilerParams(vmem_limit_bytes=60 * 1024 * 1024, collective_id=0, has_side_effects=True),
        cost_estimate=cost(),
        name="forward",
    )(length, tokens_own, *gains, *tables, grad_own, *items)


def reduce_kernel(n_dp, n_u, count, blocks_ref, *refs):
    terms, outs = list(refs[: count - 1]), refs[count - 1 : 2 * count - 1]
    refs = refs[2 * count - 1 :]
    slots, sums = refs[:count], refs[count : 2 * count]
    out_terms_ref, ring_send, ring_recv, cube_send, cube_recv, turn_send, turn_recv, local = refs[2 * count :]
    terms.append(out_terms_ref)
    group = Group(n_dp, n_u)
    group.greet()
    copies = {}
    reaches = [group.reach(c % 2 == 0) for c in range(count)]
    longest = n_dp // 2
    share = blocks_ref.shape[1]
    here = out_terms_ref.at[pl.ds(pl.multiple_of(group.me * share, share), share)]

    def add(c, target, offset, others):
        r = target.shape[0]
        tile = 16
        first = group.owner(offset) * r

        def body(i, carry):
            rows = pl.ds(pl.multiple_of(i * tile, tile), tile)
            total = terms[c][pl.ds(pl.multiple_of(first + i * tile, tile), tile)].astype(jnp.float32)
            for other in others:
                total = total + other[rows].astype(jnp.float32)
            target[rows] = total.astype(jnp.bfloat16)
            return carry

        lax.fori_loop(0, r // tile, body, 0)

    def slot(c, way, step):
        return slots[c].at[way, step]

    def send(c, way, step):
        reach = reaches[c][way]
        offset = (reach - step) if way == 0 else (step - reach)
        if step == 0:
            r = sums[c].shape[0]
            source = terms[c].at[pl.ds(pl.multiple_of(group.owner(offset) * r, r), r)]
        else:
            source = slot(c, way, step - 1)
            add(c, source, offset, [source])
        sems = (c, way, step)
        copies[sems] = group.to_ring(way, source, slot(c, way, step), ring_send.at[sems], ring_recv.at[sems])

    def start(chains):
        for c in chains:
            for way in (0, 1):
                send(c, way, 0)

    phases = [(0, 1), (2, 3)]
    start(phases[0])
    turns = []
    for k in range(1, n_u):
        turns.append(group.to_cube(k, blocks_ref.at[k], here, turn_send.at[k - 1], turn_recv.at[k - 1]))
    own = pltpu.make_async_copy(blocks_ref.at[0], here, local.at[count])
    own.start()
    own.wait()
    spreads, kept = [], []
    for phase, chains in enumerate(phases):
        for step in range(longest):
            for c in chains:
                for way in (0, 1):
                    if step < reaches[c][way]:
                        copies[c, way, step].wait_recv()
                        if step + 1 < reaches[c][way]:
                            send(c, way, step + 1)
            if step == longest - 2 and phase == 0:
                for copy in turns:
                    copy.wait_recv()
                start(phases[1])
            if phase == 1 and step % 2 == 1 and step < longest - 1:
                for spread in spreads:
                    spread.level()
            if step == longest - 1:
                for c in chains:
                    add(c, sums[c], 0, [slot(c, way, reaches[c][way] - 1) for way in (0, 1)])
                    spread = Spread(group, sums[c], outs[c], cube_send.at[c], cube_recv.at[c])
                    copy = pltpu.make_async_copy(sums[c], outs[c].at[0], local.at[c])
                    copy.start()
                    kept.append(copy)
                    spread.level()
                    spreads.append(spread)
    for spread in spreads:
        spread.level()
    for spread in spreads:
        spread.finish()
    for copy in list(copies.values()) + turns:
        copy.wait_send()
    for copy in kept:
        copy.wait()


def reduce_all(blocks, terms, n_dp, n_u):
    count = len(terms) + 1
    anywhere = pl.BlockSpec(memory_space=pl.ANY)
    local = pl.BlockSpec(memory_space=pltpu.VMEM)
    longest = n_dp // 2
    whole = (blocks.shape[0] * blocks.shape[1], blocks.shape[2])
    sizes = [(r // n_dp, c) for r, c in [t.shape for t in terms] + [whole]]
    dma = pltpu.SemaphoreType.DMA
    return pl.pallas_call(
        functools.partial(reduce_kernel, n_dp, n_u, count),
        in_specs=[local] * count,
        out_specs=[anywhere] * count,
        out_shape=[jax.ShapeDtypeStruct((n_u,) + b, jnp.bfloat16) for b in sizes],
        scratch_shapes=[pltpu.VMEM((2, longest) + b, jnp.bfloat16) for b in sizes]
        + [pltpu.VMEM(b, jnp.bfloat16) for b in sizes]
        + [
            pltpu.VMEM(whole, jnp.bfloat16),
            dma((count, 2, longest)), dma((count, 2, longest)), dma((count, n_u - 1)), dma((count, n_u - 1)),
            dma((n_u - 1,)), dma((n_u - 1,)), dma((count + 1,)),
        ],
        compiler_params=pltpu.CompilerParams(vmem_limit_bytes=VMEM_LIMIT, collective_id=1, has_side_effects=True),
        cost_estimate=cost(),
        name="reduce_all",
    )(blocks, *terms)


START = 0.9
LATENCY = 2.0
RATES = {"ring": 50.0, "x": 50.0, "core": 250.0}


class Flight:
    def __init__(self, value, arrival):
        self.value, self.arrival = value, arrival


class Sequence:
    def __init__(self):
        self.last = ()
        self.now = 0.0
        self.free = {}
        self.sources = []
        self.fillers = []

    def tie(self, *values):
        tied, _ = lax.optimization_barrier((values, self.last))
        self.last = tied
        return tied

    def run(self, cost, function, *values, take=True):
        if take:
            self.poll()
        out = function(*self.tie(*values))
        self.now += cost
        if isinstance(out, (tuple, list)):
            return self.tie(*out)
        return self.tie(out)[0]

    def fly(self, value, axis, pairs, link, kind):
        (value,) = self.tie(value)
        got = lax.ppermute(value, axis, pairs)
        start = max(self.now + START, self.free.get(link, 0.0))
        end = start + value.size * value.dtype.itemsize / 1000.0 / RATES[kind]
        self.free[link] = end
        self.now += START
        return Flight(got, end + LATENCY)

    def land(self, *flights):
        self.idle(max(f.arrival for f in flights))
        return self.tie(*[f.value for f in flights])

    def poll(self):
        moved = True
        while moved:
            moved = any([source.poll(self.now) for source in self.sources])

    def later(self, cost, ready, function):
        self.fillers.append((cost, ready, function))

    def fill(self):
        for at, (cost, ready, function) in enumerate(self.fillers):
            if ready():
                self.fillers.pop(at)
                function()
                return True
        return False

    def idle(self, until):
        while True:
            self.poll()
            if self.now >= until:
                return
            if until - self.now > 2.0 and self.fill():
                continue
            events = [e for source in self.sources for e in [source.next()] if e is not None]
            self.now = max(self.now, min(events + [until]))

    def drain(self, done):
        while not done():
            self.poll()
            if done():
                return
            if self.fill():
                continue
            events = [e for source in self.sources for e in [source.next()] if e is not None]
            assert events
            self.now = max(self.now, min(events))


def pick(value, index):
    return lax.dynamic_index_in_dim(value, index, 0, keepdims=False, allow_negative_indices=False)


class Cube:
    def __init__(self, axis, seq):
        self.axis = axis
        self.seq = seq
        self.count = lax.axis_size(axis)
        self.me = lax.axis_index(axis)
        bits = []
        bit = 1
        while bit < self.count:
            bits.append(bit)
            bit *= 2
        self.bits = bits

    def swap(self, value, bit):
        kind = "core" if bit == 1 else "x"
        return self.seq.fly(value, self.axis, [(i, i ^ bit) for i in range(self.count)], kind, kind)

    def gather(self, item):
        keys, blocks = [[0]], [item[None]]
        for bit in self.bits[::-1]:
            order = sorted((key, at, sub) for at, ks in enumerate(keys) for sub, key in enumerate(ks))
            if len(order) > 1:
                sent = self.seq.run(
                    2.0, lambda *b: jnp.concatenate([b[at][sub : sub + 1] for _, at, sub in order]), *blocks
                )
            else:
                sent = blocks[0]
            (got,) = yield [self.swap(sent, bit)]
            keys = keys + [[key ^ bit for key, _, _ in order]]
            blocks = blocks + [got]
        return (keys, blocks)

    def joined(self, held):
        keys, blocks = held
        order = sorted((key, at, sub) for at, ks in enumerate(keys) for sub, key in enumerate(ks))
        return self.seq.run(3.0, lambda *b: jnp.concatenate([b[at][sub : sub + 1] for _, at, sub in order]), *blocks)

    def reduce(self, keep, send):
        for bit in self.bits:
            (got,) = yield [self.swap(send, bit)]
            if bit != self.bits[-1]:
                keep, send = self.seq.run(4.4, halve, keep, got)
        return (keep[0], got[0])

    def turn(self, blocks):
        got = yield [self.swap(blocks[bit], bit) for bit in range(1, self.count)]
        return [blocks[0]] + list(got)

    def total(self, value, axes):
        for axis in axes:
            count = lax.axis_size(axis)
            bit = 1
            while bit < count:
                pairs = [(i, i ^ bit) for i in range(count)]
                (got,) = yield [self.seq.fly(value, axis, pairs, "sum", "ring")]
                value = self.seq.run(1.0, lambda a, b: a + b, value, got)
                bit *= 2
        return value


class Task:
    def __init__(self, seq, generator, urgent=True):
        self.seq, self.generator = seq, generator
        self.value, self.flights, self.over, self.busy = None, None, False, False
        seq.sources.append(self)
        self.go(None)

    def go(self, values):
        self.busy = True
        try:
            self.flights = self.generator.send(values)
        except StopIteration as stop:
            self.value, self.over = stop.value, True
            self.seq.sources.remove(self)
        self.busy = False

    def next(self):
        return None if self.busy or self.over else max(f.arrival for f in self.flights)

    def poll(self, now):
        if self.busy or self.over or self.next() > now + 0.5:
            return False
        self.go(self.seq.tie(*[f.value for f in self.flights]))
        return True

    def finish(self):
        while not self.over:
            if self.busy:
                raise RuntimeError
            self.seq.idle(self.next())
        return self.value


def dot(a, b):
    return jnp.einsum("mk,kn->mn", a, b, preferred_element_type=jnp.float32)


def dot_nt(a, b):
    return jnp.einsum("mk,nk->mn", a, b, preferred_element_type=jnp.float32)


def dot_tn(a, b):
    return jnp.einsum("km,kn->mn", a, b, preferred_element_type=jnp.float32)


def low(value):
    return value.astype(jnp.bfloat16)


def high(value):
    return value.astype(jnp.float32)


def shards(
    tokens,
    seq_lengths,
    cotangent,
    norm1_gain,
    input_weight,
    query_gain,
    key_gain,
    output_weight,
    norm2_gain,
    perceptron_input_weight,
    down_weight,
):
    _, rows, width = tokens.shape
    seq = Sequence()
    cube = Cube("ulysses", seq)
    n_dp = lax.axis_size("dp")
    n_u, me = cube.count, cube.me
    bucket = rows * n_u
    depth = width // n_dp
    heads = QUERY_HEADS // n_u
    kv_heads = KEY_VALUE_HEADS // n_u
    copies = QUERY_HEADS // KEY_VALUE_HEADS
    head_width = HEAD_DIMENSION
    q_w, kv_w = heads * head_width, kv_heads * head_width
    query_width = QUERY_HEADS * head_width
    kv_all = KEY_VALUE_HEADS * head_width
    ff_strip = FF // n_dp // n_u
    ff_local = FF // n_u
    half = width // 2
    out_cols = width // n_u
    place = jnp.stack([seq_lengths[0], me])
    length = seq_lengths[0]
    q_gain, k_gain = query_gain[None], key_gain[None]
    gain_one, gain_two = norm1_gain[None], norm2_gain[None]
    positions = me * rows + jnp.arange(rows)
    def cut(value, start, size):
        return lax.dynamic_slice_in_dim(value, start, size, 1)

    def task(generator):
        return Task(seq, generator)

    frequency = np.float32(ROPE_BASE) ** (np.float32(-2.0) * np.arange(head_width // 2, dtype=np.float32) / head_width)
    angles = np.arange(bucket, dtype=np.float32)[:, None] * frequency.astype(np.float32)[None, :]
    cosine, sine = np.cos(angles), np.sin(angles)
    tables = (
        jnp.asarray(np.concatenate([cosine, cosine], axis=1), jnp.float32),
        jnp.asarray(np.concatenate([-sine, sine], axis=1), jnp.float32),
    )

    gate_item, up_item = seq.run(
        4.9, lambda p, w: take_strips(p, w, n_dp, n_u, ff_strip), place, perceptron_input_weight
    )
    out_item, qk_item, vg_item, grad_own, down_item = seq.run(
        3.0,
        lambda o, w, c, d: (
            cut(o, me * out_cols, out_cols),
            jnp.concatenate([cut(w, me * q_w, q_w), cut(w, query_width + me * kv_w, kv_w)], axis=1),
            jnp.concatenate(
                [
                    cut(w, query_width + kv_all + me * kv_w, kv_w),
                    cut(w, query_width + 2 * kv_all + me * q_w, q_w),
                ],
                axis=1,
            ),
            jnp.where((positions < length)[:, None], c, jnp.zeros_like(c)),
            lax.dynamic_slice_in_dim(d, me * ff_strip, ff_strip, 0),
        ),
        output_weight,
        input_weight,
        cotangent[0],
        down_weight,
    )
    (
        w_qk, w_vg, w_gate, w_up, w_down, normed, grad_result, second, act_gate, act_up, hidden,
        raw_qk, raw_vg, queries, keys, values, gate, attended, gated, log_totals, w_out, hidden_in,
    ) = seq.run(
        250.0,
        lambda t, g, *items: forward(
            seq_lengths, t, (gain_one, gain_two, q_gain, k_gain), tables, g, items, n_dp, n_u, heads, kv_heads
        ),
        tokens[0], grad_own, out_item, qk_item, vg_item, gate_item, up_item, down_item,
    )
    normed, grad_result = normed.reshape(bucket, width), grad_result.reshape(bucket, width)
    second, gated = second.reshape(bucket, width), gated.reshape(bucket, q_w)

    def even_odd(value):
        value = low(value).reshape(n_u, rows, width)
        return (value[0::2], value[1::2])

    act_gate, act_up, hidden = (v.reshape(bucket, ff_local) for v in (act_gate, act_up, hidden))
    down_own = lax.psum_scatter(
        seq.run(10.7, lambda h, g: low(dot_tn(h, g)), hidden, grad_result), "dp", scatter_dimension=0, tiled=True
    )

    grad_gate, grad_up = seq.run(15.5, down_back, grad_result, act_gate, act_up, w_down)

    def input_grads(a, b, first, second):
        return back_matmul(a, b, first, second, rows)

    two_keep, two_send = seq.run(20.5, input_grads, grad_gate, grad_up, w_gate, w_up)
    t_two = task(cube.reduce(two_keep, two_send))
    seq.idle(t_two.next())
    up_own = lax.psum_scatter(
        seq.run(12.5, lambda a, b: outer_terms(a, b, n_dp), second, grad_up), "dp", scatter_dimension=0, tiled=True
    )
    down_keep, down_send = seq.run(11.5, lambda h, w: even_odd(dot(h, w)), hidden, w_down)
    grad_hidden_in, branch_own, gain_two_own = seq.run(
        5.8, lambda *a: norm_back(*a, True), hidden_in, *t_two.finish(), grad_own, gain_two
    )
    t_branch_grad = task(cube.gather(branch_own))
    gate_terms = seq.run(12.5, lambda a, b: outer_terms(a, b, n_dp), second, grad_gate)
    branch_grad = cube.joined(t_branch_grad.finish()).reshape(bucket, width)

    grad_gated = seq.run(3.8, dot_nt, branch_grad, w_out)
    t_down = task(cube.reduce(down_keep, down_send))
    t_down_all = task(cube.gather(seq.tie(down_own)[0]))
    grad_qk, grad_vg, gain_query_own, gain_key_own = seq.run(
        20.0,
        attend_back,
        place, raw_qk, queries, keys, values, gate, attended, grad_gated.reshape(n_u, rows, q_w), log_totals,
        q_gain, k_gain, *tables,
    )
    grad_qk, grad_vg = grad_qk.reshape(bucket, -1), grad_vg.reshape(bucket, -1)
    one_keep, one_send = seq.run(12.0, input_grads, grad_qk, grad_vg, w_qk, w_vg)
    t_one = task(cube.reduce(one_keep, one_send))
    out_parts = seq.run(7.0, lambda p, a, b: out_terms(p, a, b, n_u), place, gated, branch_grad)
    qk_terms = seq.run(9.3, lambda a, b: outer_terms(a, b, n_dp), normed, grad_qk)
    vg_terms = seq.run(9.3, lambda a, b: outer_terms(a, b, n_dp), normed, grad_vg)

    gate_all, qk_all, vg_all, out_all = seq.run(
        150.0, lambda b, *t: reduce_all(b, t, n_dp, n_u), out_parts, gate_terms, qk_terms, vg_terms, take=False
    )
    t_up_all = task(cube.gather(seq.tie(up_own)[0]))
    tokens_grad, gain_one_own = seq.run(
        5.6, lambda *a: norm_back(*a, False), tokens[0], *t_one.finish(), grad_hidden_in, gain_one
    )
    gains = seq.run(
        1.0, lambda *g: jnp.concatenate(g, axis=1)[0], gain_one_own, gain_query_own, gain_key_own, gain_two_own
    )
    t_gains = task(cube.total(gains, ("ulysses", "dp")))
    keys_all = [list(range(n_u))]
    in_all = seq.run(
        5.5,
        lambda p, a, b: put_columns(
            p, [(keys_all, [a]), (keys_all, [b])], [[(0, q_w), (q_w, kv_w)], [(0, kv_w), (kv_w, q_w)]]
        ),
        place, qk_all, vg_all,
    )
    out_all = seq.run(4.0, lambda p, a: put_columns(p, [(keys_all, [a])], [[(0, out_cols)]]), place, out_all)
    down_held = t_down_all.finish()
    down_all = seq.run(5.3, lambda p, *b: put_rows(p, (down_held[0], b)), place, *down_held[1])
    up_held = t_up_all.finish()
    mlp_all = seq.run(
        10.0, lambda p, a, *b: put_strips(p, [(keys_all, [a]), (up_held[0], b)], n_dp, ff_strip), place, gate_all, *up_held[1]
    )
    layer_out = seq.run(2.2, lambda a, b, c: a + high(b) + high(c), hidden_in, *t_down.finish())
    gains = t_gains.finish()

    gain_one_sum = gains[:width]
    gain_query_sum = gains[width : width + head_width]
    gain_key_sum = gains[width + head_width : width + 2 * head_width]
    gain_two_sum = gains[width + 2 * head_width :]
    return (
        layer_out[None],
        tokens_grad[None],
        gain_one_sum,
        in_all,
        gain_query_sum,
        gain_key_sum,
        out_all,
        gain_two_sum,
        mlp_all,
        down_all,
    )


def solution(mesh):
    placed = (
        P("dp", "ulysses", None),
        P("dp"),
        P("dp", "ulysses", None),
        P(),
        P("dp", None),
        P(),
        P(),
        P("dp", None),
        P(),
        P("dp", None),
        P("dp", None),
    )
    return jax.shard_map(
        shards,
        mesh=mesh,
        in_specs=placed,
        out_specs=(
            P("dp", "ulysses", None),
            P("dp", "ulysses", None),
            P(),
            P("dp", None),
            P(),
            P(),
            P("dp", None),
            P(),
            P("dp", None),
            P("dp", None),
        ),
        check_vma=False,
    )
```

```python
import functools

import jax
import jax.numpy as jnp
import numpy as np
from jax import lax
from jax.experimental import pallas as pl
from jax.experimental.pallas import tpu as pltpu
from jax.sharding import PartitionSpec as P

QUERY_HEADS = 16
KEY_VALUE_HEADS = 8
HEAD_DIMENSION = 128
FF = 6144


EPSILON = 1e-06
ROPE_BASE = 1000000.0
MASKED = -1e30


def rms_scale(values):
    return lax.rsqrt(jnp.mean(values * values, axis=-1, keepdims=True) + EPSILON)


VMEM_LIMIT = 56 * 1024 * 1024
NT = (((1,), (1,)), ((), ()))
TN = (((0,), (0,)), ((), ()))


def params():
    return pltpu.CompilerParams(vmem_limit_bytes=VMEM_LIMIT)


def cost(*_):
    return pl.CostEstimate(flops=1, bytes_accessed=1, transcendentals=0)


def steady(shape):
    return pl.BlockSpec(shape, lambda *_: (0,) * len(shape), pipeline_mode=pl.Buffered(1))


def tile_of(size):
    return 256 if size % 256 == 0 else 128


def head_scale(raw):
    return lax.rsqrt(jnp.mean(raw * raw, axis=-1, keepdims=True) + EPSILON)


def turn_pairs(value, cosine, sine):
    return value * cosine + pltpu.roll(value, HEAD_DIMENSION // 2, 1) * sine


def masked_scores(q, k, first_row, length):
    scores = lax.dot_general(q, k, NT, preferred_element_type=jnp.float32)
    scores = scores * HEAD_DIMENSION ** (-0.5)
    row = first_row + lax.broadcasted_iota(jnp.int32, scores.shape, 0)
    column = lax.broadcasted_iota(jnp.int32, scores.shape, 1)
    return jnp.where((column <= row) & (column < length), scores, MASKED)


def in_order(ref, me):
    return jnp.concatenate([ref[me ^ t] for t in range(ref.shape[0])], axis=0)


def attend_back_kernel(
    block, copies, heads, kv_heads, place_ref, q_raw, k_raw, q_ref, k_ref, v_ref, gate_ref, attended_ref, up_ref,
    total_ref, q_gain, k_gain, cosine, sine, qk_out, vg_out, q_gain_out, k_gain_out, grad_ref, dq_ref, dk_ref, dv_ref,
):
    group = pl.program_id(0)
    bucket, size = k_ref.shape
    n_u, rows_own, _ = q_raw.shape
    scale = size ** (-0.5)
    length, me = place_ref[0], place_ref[1]

    @pl.when(group == 0)
    def _():
        q_gain_out[...] = jnp.zeros_like(q_gain_out)
        k_gain_out[...] = jnp.zeros_like(k_gain_out)

    def store(out, at, width, value):
        for t in range(n_u):
            out[me ^ t, :, pl.ds(pl.multiple_of(at, size), width)] = value[t * rows_own : (t + 1) * rows_own]

    up, gate = in_order(up_ref, me), gate_ref[...]
    grad_ref[...] = (up * gate).astype(jnp.bfloat16)
    grad_gate = (up * attended_ref[...].astype(jnp.float32) * gate * (1.0 - gate)).astype(jnp.bfloat16)
    store(vg_out, (kv_heads + group * copies) * size, copies * size, grad_gate)
    dk_ref[...] = jnp.zeros_like(dk_ref)
    dv_ref[...] = jnp.zeros_like(dv_ref)

    def norm_grad(raw, gain, upstream, gain_out):
        factor = head_scale(raw)
        weighted = upstream * gain
        inner = jnp.mean(weighted * raw, axis=-1, keepdims=True)
        gain_out[...] += jnp.sum(upstream * raw * factor, axis=0, keepdims=True)
        return (factor * weighted - raw * (factor * factor * factor) * inner).astype(jnp.bfloat16)

    raw_q = in_order(q_raw, me)
    for copy in range(copies):
        columns = slice(copy * size, (copy + 1) * size)
        for first in range(0, bucket, block):
            rows = slice(first, first + block)
            reach = slice(0, first + block)
            q, g = q_ref[rows, columns], grad_ref[rows, columns]
            soft = jnp.exp(masked_scores(q, k_ref[reach], first, length) - total_ref[copy, rows])
            soft_grad = lax.dot_general(g, v_ref[reach], NT, preferred_element_type=jnp.float32)
            inner = jnp.sum(soft * soft_grad, axis=-1, keepdims=True)
            score_grad = (soft * (soft_grad - inner)).astype(jnp.bfloat16)
            dq_ref[rows] = jnp.dot(score_grad, k_ref[reach], preferred_element_type=jnp.float32) * scale
            dk_ref[reach] += lax.dot_general(score_grad, q, TN, preferred_element_type=jnp.float32)
            dv_ref[reach] += lax.dot_general(soft.astype(jnp.bfloat16), g, TN, preferred_element_type=jnp.float32)
        plain = turn_pairs(dq_ref[...].astype(jnp.bfloat16).astype(jnp.float32), cosine[...], -sine[...])
        store(qk_out, (group * copies + copy) * size, size, norm_grad(raw_q[:, columns], q_gain[...], plain, q_gain_out))
    plain = turn_pairs((dk_ref[...] * scale).astype(jnp.bfloat16).astype(jnp.float32), cosine[...], -sine[...])
    store(qk_out, (heads + group) * size, size, norm_grad(in_order(k_raw, me), k_gain[...], plain, k_gain_out))
    store(vg_out, group * size, size, dv_ref[...].astype(jnp.bfloat16))


def attend_back(place, raw_qk, q, k, v, gate, attended, upstream, totals, q_gain, k_gain, cosine, sine):
    size = HEAD_DIMENSION
    n_u, rows_own, _ = raw_qk.shape
    bucket = n_u * rows_own
    heads, kv_heads = q.shape[1] // size, k.shape[1] // size
    copies = heads // kv_heads

    def blocks(width, start):
        return pl.BlockSpec((n_u, rows_own, width), lambda g: (0, 0, start + g))

    wide = pl.BlockSpec((bucket, copies * size), lambda g: (0, g))
    slim = pl.BlockSpec((bucket, size), lambda g: (0, g))
    total = (heads + kv_heads) * size
    whole = pl.BlockSpec((n_u, rows_own, total), lambda g: (0, 0, 0))
    gain = pl.BlockSpec((1, size), lambda g: (0, 0))
    return pl.pallas_call(
        functools.partial(attend_back_kernel, min(256, bucket), copies, heads, kv_heads),
        grid=(kv_heads,),
        in_specs=[
            pl.BlockSpec(memory_space=pltpu.SMEM),
            blocks(copies * size, 0),
            blocks(size, heads),
            wide,
            slim,
            slim,
            wide,
            wide,
            blocks(copies * size, 0),
            pl.BlockSpec((copies, bucket, 1), lambda g: (g, 0, 0)),
            steady((1, size)),
            steady((1, size)),
            steady((bucket, size)),
            steady((bucket, size)),
        ],
        out_specs=[whole, whole, gain, gain],
        out_shape=[
            jax.ShapeDtypeStruct((n_u, rows_own, total), jnp.bfloat16),
            jax.ShapeDtypeStruct((n_u, rows_own, total), jnp.bfloat16),
            jax.ShapeDtypeStruct((1, size), jnp.float32),
            jax.ShapeDtypeStruct((1, size), jnp.float32),
        ],
        scratch_shapes=[
            pltpu.VMEM((bucket, copies * size), jnp.bfloat16),
            pltpu.VMEM((bucket, size), jnp.float32),
            pltpu.VMEM((bucket, size), jnp.float32),
            pltpu.VMEM((bucket, size), jnp.float32),
        ],
        compiler_params=params(),
        cost_estimate=cost(5 * heads * bucket * bucket * size, 24 * bucket * heads * size, heads * bucket * bucket // 2),
        name="attention_back",
    )(place, raw_qk, raw_qk, q, k, v, gate, attended, upstream, totals, q_gain, k_gain, cosine, sine)


def back_matmul(a, b, first, second, rows):
    m, n = a.shape
    width = first.shape[0]
    part = 512
    pairs = m // rows // 2

    def kernel(a_ref, b_ref, first_ref, second_ref, keep_ref, send_ref):
        for pair in range(pairs):
            at = slice(2 * pair * rows, (2 * pair + 2) * rows)
            out = lax.dot_general(a_ref[at], first_ref[...], NT, preferred_element_type=jnp.float32)
            out += lax.dot_general(b_ref[at], second_ref[...], NT, preferred_element_type=jnp.float32)
            out = out.astype(jnp.bfloat16)
            keep_ref[pair] = out[:rows]
            send_ref[pair] = out[rows:]

    weight = pl.BlockSpec((part, n), lambda i: (i, 0))
    out = pl.BlockSpec((pairs, rows, part), lambda i: (0, 0, i))
    shape = jax.ShapeDtypeStruct((pairs, rows, width), jnp.bfloat16)
    return pl.pallas_call(
        kernel,
        grid=(width // part,),
        in_specs=[steady((m, n)), steady((m, n)), weight, weight],
        out_specs=[out, out],
        out_shape=[shape, shape],
        compiler_params=params(),
        cost_estimate=cost(),
        name="back_matmul",
    )(a, b, first, second)


def outer_terms(x, y, count):
    m, width = x.shape
    n = y.shape[1]
    count = count // 2
    depth = width // count

    def kernel(x_ref, y_ref, out_ref):
        out_ref[...] = lax.dot_general(x_ref[...], y_ref[...], TN, preferred_element_type=jnp.float32).astype(jnp.bfloat16)

    return pl.pallas_call(
        kernel,
        grid=(count,),
        in_specs=[pl.BlockSpec((m, depth), lambda k: (0, k)), steady((m, n))],
        out_specs=pl.BlockSpec((depth, n), lambda k: (k, 0)),
        out_shape=jax.ShapeDtypeStruct((width, n), jnp.bfloat16),
        compiler_params=params(),
        cost_estimate=cost(2 * m * n * width, 2 * m * width + 2 * m * n + 2 * n * width),
        name="outer_terms",
    )(x, y)


def down_back(upstream, a, b, weight):
    m, width = upstream.shape
    n = a.shape[1]
    tile = tile_of(n)
    rows = min(512, m)

    def kernel(up_ref, a_ref, b_ref, weight_ref, gate_out, up_out):
        for at in range(0, m, rows):
            where = slice(at, at + rows)
            grad = lax.dot_general(up_ref[where], weight_ref[...], NT, preferred_element_type=jnp.float32)
            a, b = a_ref[where], b_ref[where]
            sig = jax.nn.sigmoid(a)
            gate_out[where] = (grad * b * sig * (1.0 + a * (1.0 - sig))).astype(jnp.bfloat16)
            up_out[where] = (grad * a * sig).astype(jnp.bfloat16)

    step = pl.BlockSpec((m, tile), lambda i: (0, i))
    shape = jax.ShapeDtypeStruct((m, n), jnp.bfloat16)
    return pl.pallas_call(
        kernel,
        grid=(n // tile,),
        in_specs=[steady((m, width)), step, step, pl.BlockSpec((tile, width), lambda i: (i, 0))],
        out_specs=[step, step],
        out_shape=[shape, shape],
        compiler_params=params(),
        cost_estimate=cost(),
        name="down_back",
    )(upstream, a, b, weight)


def strips_kernel(n_dp, n_u, strip, place_ref, w_ref, gate_ref, up_ref):
    for t in range(n_u):

        @pl.when(place_ref[1] == t)
        def _():
            for half, out in enumerate((gate_ref, up_ref)):
                starts = [((half * n_dp + b) * n_u + t) * strip for b in range(n_dp)]
                out[...] = jnp.concatenate([w_ref[:, s : s + strip] for s in starts], axis=1)


def take_strips(place, w, n_dp, n_u, strip):
    depth, total = w.shape
    rows = 64
    out = pl.BlockSpec((rows, n_dp * strip), lambda i: (i, 0))
    shape = jax.ShapeDtypeStruct((depth, n_dp * strip), w.dtype)
    return pl.pallas_call(
        functools.partial(strips_kernel, n_dp, n_u, strip),
        grid=(depth // rows,),
        in_specs=[pl.BlockSpec(memory_space=pltpu.SMEM), pl.BlockSpec((rows, total), lambda i: (i, 0))],
        out_specs=[out, out],
        out_shape=[shape, shape],
        compiler_params=params(),
        cost_estimate=cost(0, 2 * depth * total + 4 * depth * n_dp * strip),
        name="take_strips",
    )(place, w)


def fill(scratch, keys, refs):
    for key_list, ref in zip(keys, refs):
        for at, key in enumerate(key_list):
            scratch[key] = ref[at]


def put_call(kernel, place, helds, grid, blocks, at, out_block, out_at, out_shape, name):
    n_u = sum(len(k) for k in helds[0][0])
    count = sum(len(b) for _, b in helds)

    def body(place_ref, *refs):
        refs = list(refs)
        scratches = refs[count + 1 :]
        for (keys, _), scratch in zip(helds, scratches):
            fill(scratch, keys, [refs.pop(0) for _ in keys])
        kernel(place_ref[1], scratches, refs[0])

    return pl.pallas_call(
        body,
        grid=(grid,),
        in_specs=[pl.BlockSpec(memory_space=pltpu.SMEM)]
        + [pl.BlockSpec((len(k),) + block, at) for (keys, _), block in zip(helds, blocks) for k in keys],
        out_specs=pl.BlockSpec(out_block, out_at),
        out_shape=jax.ShapeDtypeStruct(out_shape, jnp.float32),
        scratch_shapes=[pltpu.VMEM((n_u,) + block, jnp.bfloat16) for block in blocks],
        compiler_params=params(),
        cost_estimate=cost(0, 6 * out_shape[0] * out_shape[1]),
        name=name,
    )(place, *[v for _, held in helds for v in held])


def put_strips(place, helds, n_dp, strip):
    n_u = sum(len(k) for k in helds[0][0])
    depth, width = helds[0][1][0].shape[1:]
    rows = min(32, depth)

    def kernel(me, scratches, out_ref):
        size = n_u * strip
        for h, scratch in enumerate(scratches):
            parts = [scratch[me ^ t].astype(jnp.float32) for t in range(n_u)]
            for b in range(n_dp):
                at = (h * n_dp + b) * size
                out_ref[:, at : at + size] = jnp.concatenate(
                    [p[:, b * strip : (b + 1) * strip] for p in parts], axis=1
                )

    total = len(helds) * n_u * width
    return put_call(
        kernel, place, helds, depth // rows, [(rows, width)] * len(helds), lambda i: (0, i, 0),
        (rows, total), lambda i: (i, 0), (depth, total), "put_strips",
    )


def put_columns(place, helds, sections):
    n_u = sum(len(k) for k in helds[0][0])
    depth = helds[0][1][0].shape[1]
    rows = min(64, depth)

    def kernel(me, scratches, out_ref):
        at = 0
        for scratch, parts in zip(scratches, sections):
            for start, size in parts:
                for t in range(n_u):
                    out_ref[:, at : at + size] = scratch[me ^ t, :, start : start + size].astype(jnp.float32)
                    at += size

    total = n_u * sum(size for parts in sections for _, size in parts)
    return put_call(
        kernel, place, helds, depth // rows, [(rows, held[0].shape[2]) for _, held in helds], lambda i: (0, i, 0),
        (rows, total), lambda i: (i, 0), (depth, total), "put_columns",
    )


def put_rows(place, held):
    n_u = sum(len(k) for k in held[0])
    depth, width = held[1][0].shape[1:]
    tile = 512

    def kernel(me, scratches, out_ref):
        for t in range(n_u):
            out_ref[t * depth : (t + 1) * depth] = scratches[0][me ^ t].astype(jnp.float32)

    return put_call(
        kernel, place, [held], width // tile, [(depth, tile)], lambda i: (0, 0, i),
        (n_u * depth, tile), lambda i: (0, i), (n_u * depth, width), "put_rows",
    )


def norm_call(kernel, inputs, gain, outs, gain_sum, name):
    r, width = inputs[0].shape
    tile = min(64, r)
    step = pl.BlockSpec((tile, width), lambda i: (i, 0))
    one = pl.BlockSpec((1, width), lambda i: (0, 0))
    shapes = [jax.ShapeDtypeStruct((r, width), o) for o in outs]
    if gain_sum:
        shapes.append(jax.ShapeDtypeStruct((1, width), jnp.float32))
    return pl.pallas_call(
        kernel,
        grid=(r // tile,),
        in_specs=[step] * len(inputs) + [one],
        out_specs=[step] * len(outs) + [one] * gain_sum,
        out_shape=shapes,
        compiler_params=params(),
        cost_estimate=cost(0, sum(4 * v.size for v in inputs)),
        name=name,
    )(*inputs, gain)


def norm_back(source, keep, got, residual, gain, rounded):
    def kernel(source_ref, keep_ref, got_ref, residual_ref, gain_ref, *outs):
        @pl.when(pl.program_id(0) == 0)
        def _():
            outs[-1][...] = jnp.zeros_like(outs[-1])

        up = keep_ref[...] + got_ref[...].astype(jnp.float32)
        source = source_ref[...].astype(jnp.float32)
        factor = head_scale(source)
        weighted = up * gain_ref[...]
        inner = jnp.mean(weighted * source, axis=-1, keepdims=True)
        total = residual_ref[...].astype(jnp.float32) + factor * weighted
        total = total - source * (factor * factor * factor) * inner
        outs[0][...] = total
        if rounded:
            outs[1][...] = total.astype(jnp.bfloat16)
        outs[-1][...] += jnp.sum(up * source * factor, axis=0, keepdims=True)

    outs = [jnp.float32] + [jnp.bfloat16] * rounded
    return norm_call(kernel, (source, keep, got, residual), gain, outs, 1, "norm_back")


def halve(keep, got):
    pairs, (r, c) = keep.shape[0] // 2, keep.shape[1:]
    tile = min(64, r)

    def kernel(keep_ref, got_ref, even_ref, odd_ref):
        even_ref[0] = keep_ref[0].astype(jnp.float32) + got_ref[0].astype(jnp.float32)
        odd_ref[0] = (keep_ref[1].astype(jnp.float32) + got_ref[1].astype(jnp.float32)).astype(jnp.bfloat16)

    two = pl.BlockSpec((2, tile, c), lambda p, i: (p, i, 0))
    one = pl.BlockSpec((1, tile, c), lambda p, i: (p, i, 0))
    return pl.pallas_call(
        kernel,
        grid=(pairs, r // tile),
        in_specs=[two, two],
        out_specs=[one, one],
        out_shape=[jax.ShapeDtypeStruct((pairs, r, c), jnp.float32), jax.ShapeDtypeStruct((pairs, r, c), jnp.bfloat16)],
        compiler_params=params(),
        cost_estimate=cost(0, 16 * pairs * r * c),
        name="halve",
    )(keep, got)


def out_terms(place, gated, upstream, n_u):
    m, q = gated.shape
    c = upstream.shape[1] // n_u

    def kernel(place_ref, x_ref, y_ref, out_ref):
        out_ref[0] = lax.dot_general(x_ref[...], y_ref[...], TN, preferred_element_type=jnp.float32).astype(jnp.bfloat16)

    return pl.pallas_call(
        kernel,
        grid_spec=pltpu.PrefetchScalarGridSpec(
            num_scalar_prefetch=1,
            grid=(n_u,),
            in_specs=[
                pl.BlockSpec((m, q), lambda k, p: (0, 0)),
                pl.BlockSpec((m, c), lambda k, p: (0, p[1] ^ k)),
            ],
            out_specs=pl.BlockSpec((1, q, c), lambda k, p: (k, 0, 0)),
        ),
        out_shape=jax.ShapeDtypeStruct((n_u, q, c), jnp.bfloat16),
        compiler_params=params(),
        cost_estimate=cost(2 * m * q * c * n_u, 2 * m * q + 4 * m * c * n_u),
        name="out_terms",
    )(place, gated, upstream)


MESH = pl.DeviceIdType.MESH


class Group:
    def __init__(self, n_dp, n_u):
        self.n_dp, self.n_u = n_dp, n_u
        index = lax.axis_index("dp")
        self.me = lax.axis_index("ulysses")
        odd = index % 2
        self.position = (1 - odd) * (index // 2) + odd * (n_dp - 1 - index // 2)
        self.next = (self.owner(1), self.owner(-1))
        self.bits = [1 << k for k in range(n_u.bit_length() - 1)]

    def owner(self, offset):
        place = (self.position + offset + self.n_dp) % self.n_dp
        late = place // (self.n_dp // 2)
        return (1 - late) * (2 * place) + late * (2 * (self.n_dp - 1 - place) + 1)

    def greet(self):
        barrier = pltpu.get_barrier_semaphore()
        for way in (0, 1):
            pl.semaphore_signal(barrier, inc=1, device_id={"dp": self.next[way]}, device_id_type=MESH)
        for other in range(1, self.n_u):
            pl.semaphore_signal(barrier, inc=1, device_id={"ulysses": self.me ^ other}, device_id_type=MESH)
        pl.semaphore_wait(barrier, 1 + self.n_u)

    def to_ring(self, way, source, target, send, recv):
        copy = pltpu.make_async_remote_copy(
            src_ref=source, dst_ref=target, send_sem=send, recv_sem=recv,
            device_id={"dp": self.next[way]}, device_id_type=MESH,
        )
        copy.start()
        return copy

    def to_cube(self, bit, source, target, send, recv):
        copy = pltpu.make_async_remote_copy(
            src_ref=source, dst_ref=target, send_sem=send, recv_sem=recv,
            device_id={"ulysses": self.me ^ bit}, device_id_type=MESH,
        )
        copy.start()
        return copy

    def reach(self, more_ahead):
        longer = self.n_dp // 2
        shorter = self.n_dp - 1 - longer
        return (longer, shorter) if more_ahead else (shorter, longer)


class Spread:
    def __init__(self, group, own, out, send, recv):
        self.group, self.own, self.out, self.send, self.recv = group, own, out, send, recv
        self.keys, self.levels, self.copies, self.used, self.waited = [0], group.bits[::-1], [], 0, 0

    def level(self):
        for copy in self.copies[self.waited :]:
            copy.wait_recv()
        self.waited = len(self.copies)
        if not self.levels:
            return False
        bit = self.levels.pop(0)
        for key in sorted(self.keys):
            source = self.own if key == 0 else self.out.at[key]
            at = self.used
            self.copies.append(
                self.group.to_cube(bit, source, self.out.at[key ^ bit], self.send.at[at], self.recv.at[at])
            )
            self.used += 1
        self.keys += [key ^ bit for key in self.keys]
        return True

    def finish(self):
        while self.level():
            pass
        for copy in self.copies:
            copy.wait_send()


class RingGather:
    def __init__(self, group, chains, send, recv):
        self.group, self.chains, self.send_sems, self.recv_sems = group, chains, send, recv
        self.copies = {}

    def place(self, c, owner):
        _, out, block, low, rows, _ = self.chains[c]
        return out.at[pl.ds(pl.multiple_of(owner * block + low, 16), rows)]

    def item(self, c):
        item, _, _, low, rows, _ = self.chains[c]
        return item.at[low : low + rows]

    def reach(self, c, way):
        return self.group.reach(self.chains[c][5])[way]

    def send(self, c, way, step):
        owner = self.group.owner(1 - step if way == 0 else step - 1)
        source = self.item(c) if step == 1 else self.place(c, owner)
        sems = (c, way, step - 1)
        self.copies[sems] = self.group.to_ring(
            way, source, self.place(c, owner), self.send_sems.at[sems], self.recv_sems.at[sems]
        )

    def start(self, c):
        for way in (0, 1):
            self.send(c, way, 1)

    def event(self, c, way, step):
        if step <= self.reach(c, way):
            self.copies[c, way, step - 1].wait_recv()
            if step < self.reach(c, way):
                self.send(c, way, step + 1)

    def finish(self):
        for copy in self.copies.values():
            copy.wait_send()


def by_rows(count, tile, function):
    def body(i, carry):
        function(pl.ds(pl.multiple_of(i * tile, tile), tile))
        return carry

    lax.fori_loop(0, count // tile, body, 0)


def forward_kernel(
    n_dp, n_u, heads, kv_heads, length_ref, tokens_ref, gain_one, gain_two, q_gain, k_gain, cosine, sine, grad_ref,
    out_item, qk_item, vg_item, gate_item, up_item, down_item,
    w_qk, w_vg, w_gate, w_up, w_down, normed_out, grad_out, second_out, act_gate, act_up, act_hidden,
    raw_qk, raw_vg, q_out, k_out, v_out, gate_out, attended_out, gated_out, total_out, w_out, hidden_out,
    normed, own, qk_local, vg_local, columns, turned, parts, core_got, total, second_own, gate_stage, up_stage, hidden_stage,
    ring_send, ring_recv, cube_send, cube_recv, turn_send, turn_recv, sum_send, sum_recv, local,
):
    rows_own, width = tokens_ref.shape
    bucket = rows_own * n_u
    size = HEAD_DIMENSION
    copies = heads // kv_heads
    depth = width // n_dp
    group = Group(n_dp, n_u)
    me, mine = group.me, group.owner(0)
    group.greet()
    strip = down_item.shape[0]
    halves = 2 if strip % 32 == 0 else 1
    chains = [
        (out_item, columns, depth, 0, depth, True),
        (qk_item, w_qk, depth, 0, depth, False),
        (vg_item, w_vg, depth, 0, depth, True),
        (gate_item, w_gate, depth, 0, depth, True),
        (up_item, w_up, depth, 0, depth, False),
    ]
    for p in range(halves):
        chains.append((down_item, w_down, strip, p * strip // halves, strip // halves, p == 0))
    ring = RingGather(group, chains, ring_send, ring_recv)
    kept = []

    def keep(source, target):
        copy = pltpu.make_async_copy(source, target, local.at[len(kept)])
        copy.start()
        kept.append(copy)
        return copy

    for c in (0, 1, 2):
        ring.start(c)
    own_rows = lambda out, block: out.at[pl.ds(pl.multiple_of(mine * block, 16), block)]
    for item, out, block in (
        (out_item, columns, depth), (qk_item, w_qk, depth), (vg_item, w_vg, depth),
        (gate_item, w_gate, depth), (up_item, w_up, depth), (down_item, w_down, strip),
    ):
        keep(item, own_rows(out, block))

    def first(rows):
        x = tokens_ref[rows].astype(jnp.float32)
        own[rows] = (x * head_scale(x) * gain_one[...]).astype(jnp.bfloat16)

    by_rows(rows_own, 64, first)
    keep(own, normed.at[0]).wait()
    keep(grad_ref, grad_out.at[0])
    spreads = [
        Spread(group, own, normed, cube_send.at[0], cube_recv.at[0]),
        Spread(group, grad_ref, grad_out, cube_send.at[1], cube_recv.at[1]),
    ]
    spreads[0].level()
    longest = n_dp // 2
    for step in range(1, longest + 1):
        for c in (0, 1, 2):
            for way in (0, 1):
                ring.event(c, way, step)
        if step == 1:
            spreads[1].level()
        if step < longest:
            spreads[0 if step % 2 == 1 else 1].level()
        if step == longest - 1:
            for c in (3, 4):
                ring.start(c)
    spreads[0].finish()
    events = []
    for step in range(1, longest + 1):
        events += [[(3, 0, step), (4, 1, step)], [(4, 0, step), (3, 1, step)]]
        if step == longest - 1:
            events.append([("start",)])
    for step in range(1, longest + 1):
        if halves == 2:
            events += [[(5, 0, step), (6, 1, step)], [(6, 0, step), (5, 1, step)]]
        else:
            events += [[(5, 0, step), (5, 1, step)]]

    def pump(count=1):
        while count and events:
            pair = events.pop(0)
            if pair[0][0] == "start":
                for c in range(5, len(chains)):
                    ring.start(c)
                continue
            for event in pair:
                ring.event(*event)
            count -= 1

    for copy in kept[:3]:
        copy.wait()
    share = depth * n_dp // n_u
    turns = []
    for k in range(1, n_u):
        source = columns.at[pl.ds(pl.multiple_of((me ^ k) * share, 16), share)]
        turns.append(group.to_cube(k, source, turned.at[k], turn_send.at[k - 1], turn_recv.at[k - 1]))
    keep(columns.at[pl.ds(pl.multiple_of(me * share, 16), share)], turned.at[0]).wait()
    one, two = keep(w_qk, qk_local), keep(w_vg, vg_local)
    normed_copy = keep(normed, normed_out)
    one.wait()
    two.wait()

    def project(b, carry):
        x = normed[b]
        raw_qk[b] = jnp.dot(x, qk_local[...], preferred_element_type=jnp.float32)
        raw_vg[b] = jnp.dot(x, vg_local[...], preferred_element_type=jnp.float32)
        return carry

    lax.fori_loop(0, n_u, project, 0)
    normed_copy.wait()
    pump()

    length = length_ref[0]
    block = min(256, bucket)

    def attention(h, carry):
        def column(ref, at):
            at = pl.multiple_of(at * size, size)
            return jnp.concatenate([ref[me ^ t, :, pl.ds(at, size)] for t in range(n_u)], axis=0)

        at = pl.ds(pl.multiple_of(h * size, size), size)
        kv = pl.ds(pl.multiple_of(h // copies * size, size), size)
        q = column(raw_qk, h)
        q = turn_pairs(q * head_scale(q) * q_gain[...], cosine[...], sine[...]).astype(jnp.bfloat16)
        q_out[:, at] = q
        k = column(raw_qk, heads + h // copies)
        k = turn_pairs(k * head_scale(k) * k_gain[...], cosine[...], sine[...]).astype(jnp.bfloat16)
        k_out[:, kv] = k
        v = column(raw_vg, h // copies).astype(jnp.bfloat16)
        v_out[:, kv] = v
        gate = jax.nn.sigmoid(column(raw_vg, kv_heads + h))
        gate_out[:, at] = gate
        for start in range(0, bucket, block):
            rows = slice(start, start + block)
            scores = masked_scores(q[rows], k[: start + block], start, length)
            top = jnp.max(scores, axis=-1, keepdims=True)
            soft = jnp.exp(scores - top)
            sums = jnp.sum(soft, axis=-1, keepdims=True)
            out = jnp.dot(soft.astype(jnp.bfloat16), v[: start + block], preferred_element_type=jnp.float32) / sums
            out = out.astype(jnp.bfloat16)
            attended_out[rows, at] = out
            total_out[h, rows] = top + jnp.log(sums)
            gated = (out.astype(jnp.float32) * gate[rows]).astype(jnp.bfloat16)
            for t in range(start // rows_own, (start + block) // rows_own):
                inside = slice(t * rows_own - start, (t + 1) * rows_own - start)
                gated_out[me ^ t, :, at] = gated[inside]
        return carry

    lax.fori_loop(0, heads, attention, 0)
    pump()
    for copy in turns:
        copy.wait_recv()
    c_width = columns.shape[1]
    for k in range(n_u):
        w_out[:, pl.ds(pl.multiple_of((me ^ k) * c_width, c_width), c_width)] = turned[k]

    def branch(b, carry):
        parts[b] = jnp.dot(gated_out[b], w_out[...], preferred_element_type=jnp.float32).astype(jnp.bfloat16)
        return carry

    lax.fori_loop(0, n_u, branch, 0)
    held = list(range(n_u))
    used = 0
    sums = []
    for bit in group.bits:
        keys = [key for key in held if not key & bit]
        level = []
        for key in keys:
            level.append(
                group.to_cube(bit, parts.at[key | bit], core_got.at[used], sum_send.at[used], sum_recv.at[used])
            )
            used += 1
        sums += level
        pump()
        for at, (key, copy) in enumerate(zip(keys, level)):
            copy.wait_recv()
            slot = used - len(keys) + at

            def add(rows, key=key, slot=slot):
                got = core_got[slot, rows].astype(jnp.float32)
                if key:
                    parts[key, rows] = (parts[key, rows].astype(jnp.float32) + got).astype(jnp.bfloat16)
                elif bit == 1:
                    total[rows] = tokens_ref[rows].astype(jnp.float32) + parts[0, rows].astype(jnp.float32) + got
                else:
                    total[rows] = total[rows] + got

            by_rows(rows_own, 64, add)
        held = keys

    def second(rows):
        hidden = total[rows]
        hidden_out[rows] = hidden
        second_own[rows] = (hidden * head_scale(hidden) * gain_two[...]).astype(jnp.bfloat16)

    by_rows(rows_own, 64, second)
    spread = Spread(group, second_own, normed, cube_send.at[2], cube_recv.at[2])
    keep(second_own, normed.at[0])
    while spread.level():
        pump(2)
    kept[12].wait()
    second_copy = keep(normed, second_out)
    while events and events[0][0][0] in ("start", 3, 4):
        pump(1)
    for copy in kept[3:5]:
        copy.wait()
    n = qk_local.shape[1]
    for part in range(w_gate.shape[1] // n):
        where = slice(part * n, (part + 1) * n)
        at = 14 + 5 * part
        loads = [
            pltpu.make_async_copy(w_gate.at[:, where], qk_local, local.at[at]),
            pltpu.make_async_copy(w_up.at[:, where], vg_local, local.at[at + 1]),
        ]
        for copy in loads:
            copy.start()
        for copy in loads:
            copy.wait()

        def expand(b, carry):
            x = normed[b]
            one = jnp.dot(x, qk_local[...], preferred_element_type=jnp.float32)
            two = jnp.dot(x, vg_local[...], preferred_element_type=jnp.float32)
            gate_stage[b] = one
            up_stage[b] = two
            hidden_stage[b] = (one * jax.nn.sigmoid(one) * two).astype(jnp.bfloat16)
            return carry

        lax.fori_loop(0, n_u, expand, 0)
        stores = []
        for k, (stage, out) in enumerate(((gate_stage, act_gate), (up_stage, act_up), (hidden_stage, act_hidden))):
            copy = pltpu.make_async_copy(stage, out.at[:, :, where], local.at[at + 2 + k])
            copy.start()
            stores.append(copy)
        pump(2)
        for copy in stores:
            copy.wait()
    second_copy.wait()
    spreads[1].finish()
    spread.finish()
    pump(1000)
    ring.finish()
    for copy in turns + sums:
        copy.wait_send()
    for copy in kept[5:6] + kept[7:8]:
        copy.wait()


def forward(length, tokens_own, gains, tables, grad_own, items, n_dp, n_u, heads, kv_heads):
    anywhere = pl.BlockSpec(memory_space=pl.ANY)
    local = pl.BlockSpec(memory_space=pltpu.VMEM)
    rows, width = tokens_own.shape
    bucket, size = rows * n_u, HEAD_DIMENSION
    total = (heads + kv_heads) * size
    depth = width // n_dp
    columns = items[0].shape[1]
    share = width // n_u
    longest = n_dp // 2

    def shape(*dims, dtype=jnp.bfloat16):
        return jax.ShapeDtypeStruct(dims, dtype)

    out_shape = [shape(n_dp * i.shape[0], i.shape[1]) for i in items[1:]]
    out_shape += [shape(n_u, rows, width)] * 3
    hidden = items[4].shape[1]
    out_shape += [shape(n_u, rows, hidden, dtype=jnp.float32)] * 2 + [shape(n_u, rows, hidden)]
    out_shape += [shape(n_u, rows, total, dtype=jnp.float32)] * 2
    out_shape += [
        shape(bucket, heads * size), shape(bucket, kv_heads * size), shape(bucket, kv_heads * size),
        shape(bucket, heads * size, dtype=jnp.float32), shape(bucket, heads * size),
        shape(n_u, rows, heads * size), shape(heads, bucket, 1, dtype=jnp.float32),
        shape(share, width), shape(rows, width, dtype=jnp.float32),
    ]
    dma = pltpu.SemaphoreType.DMA
    return pl.pallas_call(
        functools.partial(forward_kernel, n_dp, n_u, heads, kv_heads),
        in_specs=[pl.BlockSpec(memory_space=pltpu.SMEM)] + [local] * 7 + [anywhere] * 7,
        out_specs=[anywhere] * 11 + [local] * 11,
        out_shape=out_shape,
        scratch_shapes=[
            pltpu.VMEM((n_u, rows, width), jnp.bfloat16),
            pltpu.VMEM((rows, width), jnp.bfloat16),
            pltpu.VMEM((width, total), jnp.bfloat16),
            pltpu.VMEM((width, total), jnp.bfloat16),
            pltpu.VMEM((width, columns), jnp.bfloat16),
            pltpu.VMEM((n_u, share, columns), jnp.bfloat16),
            pltpu.VMEM((n_u, rows, width), jnp.bfloat16),
            pltpu.VMEM((n_u - 1, rows, width), jnp.bfloat16),
            pltpu.VMEM((rows, width), jnp.float32),
            pltpu.VMEM((rows, width), jnp.bfloat16),
            pltpu.VMEM((n_u, rows, total), jnp.float32),
            pltpu.VMEM((n_u, rows, total), jnp.float32),
            pltpu.VMEM((n_u, rows, total), jnp.bfloat16),
            dma((7, 2, longest)), dma((7, 2, longest)), dma((3, n_u - 1)), dma((3, n_u - 1)),
            dma((n_u - 1,)), dma((n_u - 1,)), dma((n_u - 1,)), dma((n_u - 1,)), dma((14 + 5 * (hidden // total),)),
        ],
        compiler_params=pltpu.CompilerParams(vmem_limit_bytes=60 * 1024 * 1024, collective_id=0, has_side_effects=True),
        cost_estimate=cost(),
        name="forward",
    )(length, tokens_own, *gains, *tables, grad_own, *items)


def reduce_kernel(n_dp, n_u, count, blocks_ref, *refs):
    given, outs = list(refs[: count - 1]), refs[count - 1 : 2 * count - 1]
    refs = refs[2 * count - 1 :]
    slots, sums, terms = refs[:count], refs[count : 2 * count], refs[2 * count : 3 * count]
    ring_send, ring_recv, cube_send, cube_recv, turn_send, turn_recv, local = refs[3 * count :]
    out_terms_ref = terms[-1]
    given.append(out_terms_ref)
    loads = {c: pltpu.make_async_copy(given[c], terms[c], local.at[count + 1 + c]) for c in range(count - 1)}
    group = Group(n_dp, n_u)
    group.greet()
    copies = {}
    reaches = [group.reach(c % 2 == 0) for c in range(count)]
    longest = n_dp // 2
    share = blocks_ref.shape[1]
    here = out_terms_ref.at[pl.ds(pl.multiple_of(group.me * share, share), share)]

    def add(c, target, offset, others):
        r = target.shape[0]
        tile = 16
        first = group.owner(offset) * r

        def body(i, carry):
            rows = pl.ds(pl.multiple_of(i * tile, tile), tile)
            total = terms[c][pl.ds(pl.multiple_of(first + i * tile, tile), tile)].astype(jnp.float32)
            for other in others:
                total = total + other[rows].astype(jnp.float32)
            target[rows] = total.astype(jnp.bfloat16)
            return carry

        lax.fori_loop(0, r // tile, body, 0)

    def slot(c, way, step):
        return slots[c].at[way, step]

    def send(c, way, step):
        reach = reaches[c][way]
        offset = (reach - step) if way == 0 else (step - reach)
        if step == 0:
            r = sums[c].shape[0]
            source = given[c].at[pl.ds(pl.multiple_of(group.owner(offset) * r, r), r)]
        else:
            if c in loads:
                loads.pop(c).wait()
            source = slot(c, way, step - 1)
            add(c, source, offset, [source])
        sems = (c, way, step)
        copies[sems] = group.to_ring(way, source, slot(c, way, step), ring_send.at[sems], ring_recv.at[sems])

    def start(chains):
        for c in chains:
            for way in (0, 1):
                send(c, way, 0)

    phases = [(0, 1), (2, 3)]
    start(phases[0])
    for copy in loads.values():
        copy.start()
    turns = []
    for k in range(1, n_u):
        turns.append(group.to_cube(k, blocks_ref.at[k], here, turn_send.at[k - 1], turn_recv.at[k - 1]))
    own = pltpu.make_async_copy(blocks_ref.at[0], here, local.at[count])
    own.start()
    own.wait()
    spreads, kept = [], []
    for phase, chains in enumerate(phases):
        for step in range(longest):
            for c in chains:
                for way in (0, 1):
                    if step < reaches[c][way]:
                        copies[c, way, step].wait_recv()
                        if step + 1 < reaches[c][way]:
                            send(c, way, step + 1)
            if step == longest - 2 and phase == 0:
                for copy in turns:
                    copy.wait_recv()
                start(phases[1])
            if phase == 1 and step % 2 == 1 and step < longest - 1:
                for spread in spreads:
                    spread.level()
            if step == longest - 1:
                for c in chains:
                    add(c, sums[c], 0, [slot(c, way, reaches[c][way] - 1) for way in (0, 1)])
                    spread = Spread(group, sums[c], outs[c], cube_send.at[c], cube_recv.at[c])
                    copy = pltpu.make_async_copy(sums[c], outs[c].at[0], local.at[c])
                    copy.start()
                    kept.append(copy)
                    spread.level()
                    spreads.append(spread)
    for spread in spreads:
        spread.level()
    for spread in spreads:
        spread.finish()
    for copy in list(copies.values()) + turns:
        copy.wait_send()
    for copy in kept:
        copy.wait()


def reduce_all(blocks, terms, n_dp, n_u):
    count = len(terms) + 1
    anywhere = pl.BlockSpec(memory_space=pl.ANY)
    local = pl.BlockSpec(memory_space=pltpu.VMEM)
    longest = n_dp // 2
    whole = (blocks.shape[0] * blocks.shape[1], blocks.shape[2])
    sizes = [(r // n_dp, c) for r, c in [t.shape for t in terms] + [whole]]
    dma = pltpu.SemaphoreType.DMA
    return pl.pallas_call(
        functools.partial(reduce_kernel, n_dp, n_u, count),
        in_specs=[anywhere] * count,
        out_specs=[anywhere] * count,
        out_shape=[jax.ShapeDtypeStruct((n_u,) + b, jnp.bfloat16) for b in sizes],
        scratch_shapes=[pltpu.VMEM((2, longest) + b, jnp.bfloat16) for b in sizes]
        + [pltpu.VMEM(b, jnp.bfloat16) for b in sizes]
        + [
            pltpu.VMEM(t.shape, jnp.bfloat16)
            for t in terms
        ]
        + [
            pltpu.VMEM(whole, jnp.bfloat16),
            dma((count, 2, longest)), dma((count, 2, longest)), dma((count, n_u - 1)), dma((count, n_u - 1)),
            dma((n_u - 1,)), dma((n_u - 1,)), dma((2 * count,)),
        ],
        compiler_params=pltpu.CompilerParams(vmem_limit_bytes=VMEM_LIMIT, collective_id=1, has_side_effects=True),
        cost_estimate=cost(),
        name="reduce_all",
    )(blocks, *terms)


START = 0.9
LATENCY = 6.0
RATES = {"ring": 50.0, "x": 50.0, "core": 250.0}


class Flight:
    def __init__(self, value, arrival):
        self.value, self.arrival = value, arrival


class Sequence:
    def __init__(self):
        self.last = ()
        self.now = 0.0
        self.free = {}
        self.sources = []
        self.fillers = []

    def tie(self, *values):
        tied, _ = lax.optimization_barrier((values, self.last))
        self.last = tied
        return tied

    def run(self, cost, function, *values, take=True):
        if take:
            self.poll()
        out = function(*self.tie(*values))
        self.now += cost
        if isinstance(out, (tuple, list)):
            return self.tie(*out)
        return self.tie(out)[0]

    def fly(self, value, axis, pairs, link, kind):
        (value,) = self.tie(value)
        got = lax.ppermute(value, axis, pairs)
        start = max(self.now + START, self.free.get(link, 0.0))
        end = start + value.size * value.dtype.itemsize / 1000.0 / RATES[kind]
        self.free[link] = end
        self.now += START
        return Flight(got, end + LATENCY)

    def land(self, *flights):
        self.idle(max(f.arrival for f in flights))
        return self.tie(*[f.value for f in flights])

    def poll(self):
        moved = True
        while moved:
            moved = any([source.poll(self.now) for source in self.sources])

    def later(self, cost, ready, function):
        self.fillers.append((cost, ready, function))

    def fill(self):
        for at, (cost, ready, function) in enumerate(self.fillers):
            if ready():
                self.fillers.pop(at)
                function()
                return True
        return False

    def idle(self, until):
        while True:
            self.poll()
            if self.now >= until:
                return
            if until - self.now > 2.0 and self.fill():
                continue
            events = [e for source in self.sources for e in [source.next()] if e is not None]
            self.now = max(self.now, min(events + [until]))

    def drain(self, done):
        while not done():
            self.poll()
            if done():
                return
            if self.fill():
                continue
            events = [e for source in self.sources for e in [source.next()] if e is not None]
            assert events
            self.now = max(self.now, min(events))


def pick(value, index):
    return lax.dynamic_index_in_dim(value, index, 0, keepdims=False, allow_negative_indices=False)


class Cube:
    def __init__(self, axis, seq):
        self.axis = axis
        self.seq = seq
        self.count = lax.axis_size(axis)
        self.me = lax.axis_index(axis)
        bits = []
        bit = 1
        while bit < self.count:
            bits.append(bit)
            bit *= 2
        self.bits = bits

    def swap(self, value, bit):
        kind = "core" if bit == 1 else "x"
        return self.seq.fly(value, self.axis, [(i, i ^ bit) for i in range(self.count)], kind, kind)

    def gather(self, item):
        keys, blocks = [[0]], [item[None]]
        for bit in self.bits[::-1]:
            order = sorted((key, at, sub) for at, ks in enumerate(keys) for sub, key in enumerate(ks))
            if len(order) > 1:
                sent = self.seq.run(
                    2.0, lambda *b: jnp.concatenate([b[at][sub : sub + 1] for _, at, sub in order]), *blocks
                )
            else:
                sent = blocks[0]
            (got,) = yield [self.swap(sent, bit)]
            keys = keys + [[key ^ bit for key, _, _ in order]]
            blocks = blocks + [got]
        return (keys, blocks)

    def joined(self, held):
        keys, blocks = held
        order = sorted((key, at, sub) for at, ks in enumerate(keys) for sub, key in enumerate(ks))
        return self.seq.run(3.0, lambda *b: jnp.concatenate([b[at][sub : sub + 1] for _, at, sub in order]), *blocks)

    def reduce(self, keep, send):
        for bit in self.bits:
            (got,) = yield [self.swap(send, bit)]
            if bit != self.bits[-1]:
                keep, send = self.seq.run(4.4, halve, keep, got)
        return (keep[0], got[0])

    def turn(self, blocks):
        got = yield [self.swap(blocks[bit], bit) for bit in range(1, self.count)]
        return [blocks[0]] + list(got)

    def total(self, value, axes):
        for axis in axes:
            count = lax.axis_size(axis)
            bit = 1
            while bit < count:
                pairs = [(i, i ^ bit) for i in range(count)]
                (got,) = yield [self.seq.fly(value, axis, pairs, "sum", "ring")]
                value = self.seq.run(1.0, lambda a, b: a + b, value, got)
                bit *= 2
        return value


class Task:
    def __init__(self, seq, generator, urgent=True):
        self.seq, self.generator = seq, generator
        self.value, self.flights, self.over, self.busy = None, None, False, False
        seq.sources.append(self)
        self.go(None)

    def go(self, values):
        self.busy = True
        try:
            self.flights = self.generator.send(values)
        except StopIteration as stop:
            self.value, self.over = stop.value, True
            self.seq.sources.remove(self)
        self.busy = False

    def next(self):
        return None if self.busy or self.over else max(f.arrival for f in self.flights)

    def poll(self, now):
        if self.busy or self.over or self.next() > now + 0.5:
            return False
        self.go(self.seq.tie(*[f.value for f in self.flights]))
        return True

    def finish(self):
        while not self.over:
            if self.busy:
                raise RuntimeError
            self.seq.idle(self.next())
        return self.value


def dot(a, b):
    return jnp.einsum("mk,kn->mn", a, b, preferred_element_type=jnp.float32)


def dot_nt(a, b):
    return jnp.einsum("mk,nk->mn", a, b, preferred_element_type=jnp.float32)


def dot_tn(a, b):
    return jnp.einsum("km,kn->mn", a, b, preferred_element_type=jnp.float32)


def low(value):
    return value.astype(jnp.bfloat16)


def high(value):
    return value.astype(jnp.float32)


def shards(
    tokens,
    seq_lengths,
    cotangent,
    norm1_gain,
    input_weight,
    query_gain,
    key_gain,
    output_weight,
    norm2_gain,
    perceptron_input_weight,
    down_weight,
):
    _, rows, width = tokens.shape
    seq = Sequence()
    cube = Cube("ulysses", seq)
    n_dp = lax.axis_size("dp")
    n_u, me = cube.count, cube.me
    bucket = rows * n_u
    depth = width // n_dp
    heads = QUERY_HEADS // n_u
    kv_heads = KEY_VALUE_HEADS // n_u
    copies = QUERY_HEADS // KEY_VALUE_HEADS
    head_width = HEAD_DIMENSION
    q_w, kv_w = heads * head_width, kv_heads * head_width
    query_width = QUERY_HEADS * head_width
    kv_all = KEY_VALUE_HEADS * head_width
    ff_strip = FF // n_dp // n_u
    ff_local = FF // n_u
    half = width // 2
    out_cols = width // n_u
    place = jnp.stack([seq_lengths[0], me])
    length = seq_lengths[0]
    q_gain, k_gain = query_gain[None], key_gain[None]
    gain_one, gain_two = norm1_gain[None], norm2_gain[None]
    positions = me * rows + jnp.arange(rows)
    def cut(value, start, size):
        return lax.dynamic_slice_in_dim(value, start, size, 1)

    def task(generator):
        return Task(seq, generator)

    frequency = np.float32(ROPE_BASE) ** (np.float32(-2.0) * np.arange(head_width // 2, dtype=np.float32) / head_width)
    angles = np.arange(bucket, dtype=np.float32)[:, None] * frequency.astype(np.float32)[None, :]
    cosine, sine = np.cos(angles), np.sin(angles)
    tables = (
        jnp.asarray(np.concatenate([cosine, cosine], axis=1), jnp.float32),
        jnp.asarray(np.concatenate([-sine, sine], axis=1), jnp.float32),
    )

    gate_item, up_item = seq.run(
        4.9, lambda p, w: take_strips(p, w, n_dp, n_u, ff_strip), place, perceptron_input_weight
    )
    out_item, qk_item, vg_item, grad_own, down_item = seq.run(
        3.0,
        lambda o, w, c, d: (
            cut(o, me * out_cols, out_cols),
            jnp.concatenate([cut(w, me * q_w, q_w), cut(w, query_width + me * kv_w, kv_w)], axis=1),
            jnp.concatenate(
                [
                    cut(w, query_width + kv_all + me * kv_w, kv_w),
                    cut(w, query_width + 2 * kv_all + me * q_w, q_w),
                ],
                axis=1,
            ),
            jnp.where((positions < length)[:, None], c, jnp.zeros_like(c)),
            lax.dynamic_slice_in_dim(d, me * ff_strip, ff_strip, 0),
        ),
        output_weight,
        input_weight,
        cotangent[0],
        down_weight,
    )
    (
        w_qk, w_vg, w_gate, w_up, w_down, normed, grad_result, second, act_gate, act_up, hidden,
        raw_qk, raw_vg, queries, keys, values, gate, attended, gated, log_totals, w_out, hidden_in,
    ) = seq.run(
        250.0,
        lambda t, g, *items: forward(
            seq_lengths, t, (gain_one, gain_two, q_gain, k_gain), tables, g, items, n_dp, n_u, heads, kv_heads
        ),
        tokens[0], grad_own, out_item, qk_item, vg_item, gate_item, up_item, down_item,
    )
    normed, grad_result = normed.reshape(bucket, width), grad_result.reshape(bucket, width)
    second, gated = second.reshape(bucket, width), gated.reshape(bucket, q_w)

    def even_odd(value):
        value = low(value).reshape(n_u, rows, width)
        return (value[0::2], value[1::2])

    act_gate, act_up, hidden = (v.reshape(bucket, ff_local) for v in (act_gate, act_up, hidden))
    down_own = lax.psum_scatter(
        seq.run(10.7, lambda h, g: low(dot_tn(h, g)), hidden, grad_result), "dp", scatter_dimension=0, tiled=True
    )

    grad_gate, grad_up = seq.run(15.5, down_back, grad_result, act_gate, act_up, w_down)

    def input_grads(a, b, first, second):
        return back_matmul(a, b, first, second, rows)

    two_keep, two_send = seq.run(20.5, input_grads, grad_gate, grad_up, w_gate, w_up)
    t_two = task(cube.reduce(two_keep, two_send))
    seq.idle(t_two.next())
    up_own = lax.psum_scatter(
        seq.run(12.5, lambda a, b: outer_terms(a, b, n_dp), second, grad_up), "dp", scatter_dimension=0, tiled=True
    )
    down_keep, down_send = seq.run(11.5, lambda h, w: even_odd(dot(h, w)), hidden, w_down)
    grad_hidden_in, branch_own, gain_two_own = seq.run(
        5.8, lambda *a: norm_back(*a, True), hidden_in, *t_two.finish(), grad_own, gain_two
    )
    t_branch_grad = task(cube.gather(branch_own))
    gate_terms = seq.run(12.5, lambda a, b: outer_terms(a, b, n_dp), second, grad_gate)
    branch_grad = cube.joined(t_branch_grad.finish()).reshape(bucket, width)

    grad_gated = seq.run(3.8, dot_nt, branch_grad, w_out)
    t_down = task(cube.reduce(down_keep, down_send))
    t_down_all = task(cube.gather(seq.tie(down_own)[0]))
    grad_qk, grad_vg, gain_query_own, gain_key_own = seq.run(
        20.0,
        attend_back,
        place, raw_qk, queries, keys, values, gate, attended, grad_gated.reshape(n_u, rows, q_w), log_totals,
        q_gain, k_gain, *tables,
    )
    grad_qk, grad_vg = grad_qk.reshape(bucket, -1), grad_vg.reshape(bucket, -1)
    one_keep, one_send = seq.run(12.0, input_grads, grad_qk, grad_vg, w_qk, w_vg)
    t_one = task(cube.reduce(one_keep, one_send))
    out_parts = seq.run(7.0, lambda p, a, b: out_terms(p, a, b, n_u), place, gated, branch_grad)
    qk_terms = seq.run(9.3, lambda a, b: outer_terms(a, b, n_dp), normed, grad_qk)
    vg_terms = seq.run(9.3, lambda a, b: outer_terms(a, b, n_dp), normed, grad_vg)

    gate_all, qk_all, vg_all, out_all = seq.run(
        150.0, lambda b, *t: reduce_all(b, t, n_dp, n_u), out_parts, gate_terms, qk_terms, vg_terms, take=False
    )
    t_up_all = task(cube.gather(seq.tie(up_own)[0]))
    tokens_grad, gain_one_own = seq.run(
        5.6, lambda *a: norm_back(*a, False), tokens[0], *t_one.finish(), grad_hidden_in, gain_one
    )
    gains = seq.run(
        1.0, lambda *g: jnp.concatenate(g, axis=1)[0], gain_one_own, gain_query_own, gain_key_own, gain_two_own
    )
    t_gains = task(cube.total(gains, ("ulysses", "dp")))
    keys_all = [list(range(n_u))]
    in_all = seq.run(
        5.5,
        lambda p, a, b: put_columns(
            p, [(keys_all, [a]), (keys_all, [b])], [[(0, q_w), (q_w, kv_w)], [(0, kv_w), (kv_w, q_w)]]
        ),
        place, qk_all, vg_all,
    )
    out_all = seq.run(4.0, lambda p, a: put_columns(p, [(keys_all, [a])], [[(0, out_cols)]]), place, out_all)
    down_held = t_down_all.finish()
    down_all = seq.run(5.3, lambda p, *b: put_rows(p, (down_held[0], b)), place, *down_held[1])
    up_held = t_up_all.finish()
    mlp_all = seq.run(
        10.0, lambda p, a, *b: put_strips(p, [(keys_all, [a]), (up_held[0], b)], n_dp, ff_strip), place, gate_all, *up_held[1]
    )
    layer_out = seq.run(2.2, lambda a, b, c: a + high(b) + high(c), hidden_in, *t_down.finish())
    gains = t_gains.finish()

    gain_one_sum = gains[:width]
    gain_query_sum = gains[width : width + head_width]
    gain_key_sum = gains[width + head_width : width + 2 * head_width]
    gain_two_sum = gains[width + 2 * head_width :]
    return (
        layer_out[None],
        tokens_grad[None],
        gain_one_sum,
        in_all,
        gain_query_sum,
        gain_key_sum,
        out_all,
        gain_two_sum,
        mlp_all,
        down_all,
    )


def solution(mesh):
    placed = (
        P("dp", "ulysses", None),
        P("dp"),
        P("dp", "ulysses", None),
        P(),
        P("dp", None),
        P(),
        P(),
        P("dp", None),
        P(),
        P("dp", None),
        P("dp", None),
    )
    return jax.shard_map(
        shards,
        mesh=mesh,
        in_specs=placed,
        out_specs=(
            P("dp", "ulysses", None),
            P("dp", "ulysses", None),
            P(),
            P("dp", None),
            P(),
            P(),
            P("dp", None),
            P(),
            P("dp", None),
            P("dp", None),
        ),
        check_vma=False,
    )
```

```python
import functools

import jax
import jax.numpy as jnp
import numpy as np
from jax import lax
from jax.experimental import pallas as pl
from jax.experimental.pallas import tpu as pltpu
from jax.sharding import PartitionSpec as P

QUERY_HEADS = 16
KEY_VALUE_HEADS = 8
HEAD_DIMENSION = 128
FF = 6144


EPSILON = 1e-06
ROPE_BASE = 1000000.0
MASKED = -1e30


def rms_scale(values):
    return lax.rsqrt(jnp.mean(values * values, axis=-1, keepdims=True) + EPSILON)


VMEM_LIMIT = 56 * 1024 * 1024
NT = (((1,), (1,)), ((), ()))
TN = (((0,), (0,)), ((), ()))


def params():
    return pltpu.CompilerParams(vmem_limit_bytes=VMEM_LIMIT)


def cost(*_):
    return pl.CostEstimate(flops=1, bytes_accessed=1, transcendentals=0)


def steady(shape):
    return pl.BlockSpec(shape, lambda *_: (0,) * len(shape), pipeline_mode=pl.Buffered(1))


def tile_of(size):
    return 256 if size % 256 == 0 else 128


def head_scale(raw):
    return lax.rsqrt(jnp.mean(raw * raw, axis=-1, keepdims=True) + EPSILON)


def turn_pairs(value, cosine, sine):
    return value * cosine + pltpu.roll(value, HEAD_DIMENSION // 2, 1) * sine


def masked_scores(q, k, first_row, length):
    scores = lax.dot_general(q, k, NT, preferred_element_type=jnp.float32)
    scores = scores * HEAD_DIMENSION ** (-0.5)
    row = first_row + lax.broadcasted_iota(jnp.int32, scores.shape, 0)
    column = lax.broadcasted_iota(jnp.int32, scores.shape, 1)
    return jnp.where((column <= row) & (column < length), scores, MASKED)


def in_order(ref, me):
    return jnp.concatenate([ref[me ^ t] for t in range(ref.shape[0])], axis=0)


def attend_back_kernel(
    block, copies, heads, kv_heads, place_ref, q_raw, k_raw, q_ref, k_ref, v_ref, gate_ref, attended_ref, up_ref,
    total_ref, q_gain, k_gain, cosine, sine, qk_out, vg_out, q_gain_out, k_gain_out, grad_ref, dq_ref, dk_ref, dv_ref,
):
    group = pl.program_id(0)
    bucket, size = k_ref.shape
    n_u, rows_own, _ = q_raw.shape
    scale = size ** (-0.5)
    length, me = place_ref[0], place_ref[1]

    @pl.when(group == 0)
    def _():
        q_gain_out[...] = jnp.zeros_like(q_gain_out)
        k_gain_out[...] = jnp.zeros_like(k_gain_out)

    def store(out, at, width, value):
        for t in range(n_u):
            out[me ^ t, :, pl.ds(pl.multiple_of(at, size), width)] = value[t * rows_own : (t + 1) * rows_own]

    up, gate = in_order(up_ref, me), gate_ref[...]
    grad_ref[...] = (up * gate).astype(jnp.bfloat16)
    grad_gate = (up * attended_ref[...].astype(jnp.float32) * gate * (1.0 - gate)).astype(jnp.bfloat16)
    store(vg_out, (kv_heads + group * copies) * size, copies * size, grad_gate)
    dk_ref[...] = jnp.zeros_like(dk_ref)
    dv_ref[...] = jnp.zeros_like(dv_ref)

    def norm_grad(raw, gain, upstream, gain_out):
        factor = head_scale(raw)
        weighted = upstream * gain
        inner = jnp.mean(weighted * raw, axis=-1, keepdims=True)
        gain_out[...] += jnp.sum(upstream * raw * factor, axis=0, keepdims=True)
        return (factor * weighted - raw * (factor * factor * factor) * inner).astype(jnp.bfloat16)

    raw_q = in_order(q_raw, me)
    for copy in range(copies):
        columns = slice(copy * size, (copy + 1) * size)
        for first in range(0, bucket, block):
            rows = slice(first, first + block)
            reach = slice(0, first + block)
            q, g = q_ref[rows, columns], grad_ref[rows, columns]
            soft = jnp.exp(masked_scores(q, k_ref[reach], first, length) - total_ref[copy, rows])
            soft_grad = lax.dot_general(g, v_ref[reach], NT, preferred_element_type=jnp.float32)
            inner = jnp.sum(soft * soft_grad, axis=-1, keepdims=True)
            score_grad = (soft * (soft_grad - inner)).astype(jnp.bfloat16)
            dq_ref[rows] = jnp.dot(score_grad, k_ref[reach], preferred_element_type=jnp.float32) * scale
            dk_ref[reach] += lax.dot_general(score_grad, q, TN, preferred_element_type=jnp.float32)
            dv_ref[reach] += lax.dot_general(soft.astype(jnp.bfloat16), g, TN, preferred_element_type=jnp.float32)
        plain = turn_pairs(dq_ref[...].astype(jnp.bfloat16).astype(jnp.float32), cosine[...], -sine[...])
        store(qk_out, (group * copies + copy) * size, size, norm_grad(raw_q[:, columns], q_gain[...], plain, q_gain_out))
    plain = turn_pairs((dk_ref[...] * scale).astype(jnp.bfloat16).astype(jnp.float32), cosine[...], -sine[...])
    store(qk_out, (heads + group) * size, size, norm_grad(in_order(k_raw, me), k_gain[...], plain, k_gain_out))
    store(vg_out, group * size, size, dv_ref[...].astype(jnp.bfloat16))


def attend_back(place, raw_qk, q, k, v, gate, attended, upstream, totals, q_gain, k_gain, cosine, sine):
    size = HEAD_DIMENSION
    n_u, rows_own, _ = raw_qk.shape
    bucket = n_u * rows_own
    heads, kv_heads = q.shape[1] // size, k.shape[1] // size
    copies = heads // kv_heads

    def blocks(width, start):
        return pl.BlockSpec((n_u, rows_own, width), lambda g: (0, 0, start + g))

    wide = pl.BlockSpec((bucket, copies * size), lambda g: (0, g))
    slim = pl.BlockSpec((bucket, size), lambda g: (0, g))
    total = (heads + kv_heads) * size
    whole = pl.BlockSpec((n_u, rows_own, total), lambda g: (0, 0, 0))
    gain = pl.BlockSpec((1, size), lambda g: (0, 0))
    return pl.pallas_call(
        functools.partial(attend_back_kernel, min(256, bucket), copies, heads, kv_heads),
        grid=(kv_heads,),
        in_specs=[
            pl.BlockSpec(memory_space=pltpu.SMEM),
            blocks(copies * size, 0),
            blocks(size, heads),
            wide,
            slim,
            slim,
            wide,
            wide,
            blocks(copies * size, 0),
            pl.BlockSpec((copies, bucket, 1), lambda g: (g, 0, 0)),
            steady((1, size)),
            steady((1, size)),
            steady((bucket, size)),
            steady((bucket, size)),
        ],
        out_specs=[whole, whole, gain, gain],
        out_shape=[
            jax.ShapeDtypeStruct((n_u, rows_own, total), jnp.bfloat16),
            jax.ShapeDtypeStruct((n_u, rows_own, total), jnp.bfloat16),
            jax.ShapeDtypeStruct((1, size), jnp.float32),
            jax.ShapeDtypeStruct((1, size), jnp.float32),
        ],
        scratch_shapes=[
            pltpu.VMEM((bucket, copies * size), jnp.bfloat16),
            pltpu.VMEM((bucket, size), jnp.float32),
            pltpu.VMEM((bucket, size), jnp.float32),
            pltpu.VMEM((bucket, size), jnp.float32),
        ],
        compiler_params=params(),
        cost_estimate=cost(5 * heads * bucket * bucket * size, 24 * bucket * heads * size, heads * bucket * bucket // 2),
        name="attention_back",
    )(place, raw_qk, raw_qk, q, k, v, gate, attended, upstream, totals, q_gain, k_gain, cosine, sine)


def back_matmul(a, b, first, second, rows):
    m, n = a.shape
    width = first.shape[0]
    part = 512
    pairs = m // rows // 2

    def kernel(a_ref, b_ref, first_ref, second_ref, keep_ref, send_ref):
        for pair in range(pairs):
            at = slice(2 * pair * rows, (2 * pair + 2) * rows)
            out = lax.dot_general(a_ref[at], first_ref[...], NT, preferred_element_type=jnp.float32)
            out += lax.dot_general(b_ref[at], second_ref[...], NT, preferred_element_type=jnp.float32)
            out = out.astype(jnp.bfloat16)
            keep_ref[pair] = out[:rows]
            send_ref[pair] = out[rows:]

    weight = pl.BlockSpec((part, n), lambda i: (i, 0))
    out = pl.BlockSpec((pairs, rows, part), lambda i: (0, 0, i))
    shape = jax.ShapeDtypeStruct((pairs, rows, width), jnp.bfloat16)
    return pl.pallas_call(
        kernel,
        grid=(width // part,),
        in_specs=[steady((m, n)), steady((m, n)), weight, weight],
        out_specs=[out, out],
        out_shape=[shape, shape],
        compiler_params=params(),
        cost_estimate=cost(),
        name="back_matmul",
    )(a, b, first, second)


def outer_terms(x, y, count):
    m, width = x.shape
    n = y.shape[1]
    count = count // 2
    depth = width // count

    def kernel(x_ref, y_ref, out_ref):
        out_ref[...] = lax.dot_general(x_ref[...], y_ref[...], TN, preferred_element_type=jnp.float32).astype(jnp.bfloat16)

    return pl.pallas_call(
        kernel,
        grid=(count,),
        in_specs=[pl.BlockSpec((m, depth), lambda k: (0, k)), steady((m, n))],
        out_specs=pl.BlockSpec((depth, n), lambda k: (k, 0)),
        out_shape=jax.ShapeDtypeStruct((width, n), jnp.bfloat16),
        compiler_params=params(),
        cost_estimate=cost(2 * m * n * width, 2 * m * width + 2 * m * n + 2 * n * width),
        name="outer_terms",
    )(x, y)


def down_back(upstream, a, b, weight):
    m, width = upstream.shape
    n = a.shape[1]
    tile = tile_of(n)
    rows = min(512, m)

    def kernel(up_ref, a_ref, b_ref, weight_ref, gate_out, up_out):
        for at in range(0, m, rows):
            where = slice(at, at + rows)
            grad = lax.dot_general(up_ref[where], weight_ref[...], NT, preferred_element_type=jnp.float32)
            a, b = a_ref[where], b_ref[where]
            sig = jax.nn.sigmoid(a)
            gate_out[where] = (grad * b * sig * (1.0 + a * (1.0 - sig))).astype(jnp.bfloat16)
            up_out[where] = (grad * a * sig).astype(jnp.bfloat16)

    step = pl.BlockSpec((m, tile), lambda i: (0, i))
    shape = jax.ShapeDtypeStruct((m, n), jnp.bfloat16)
    return pl.pallas_call(
        kernel,
        grid=(n // tile,),
        in_specs=[steady((m, width)), step, step, pl.BlockSpec((tile, width), lambda i: (i, 0))],
        out_specs=[step, step],
        out_shape=[shape, shape],
        compiler_params=params(),
        cost_estimate=cost(),
        name="down_back",
    )(upstream, a, b, weight)


def strips_kernel(n_dp, n_u, strip, place_ref, w_ref, gate_ref, up_ref):
    for t in range(n_u):

        @pl.when(place_ref[1] == t)
        def _():
            for half, out in enumerate((gate_ref, up_ref)):
                starts = [((half * n_dp + b) * n_u + t) * strip for b in range(n_dp)]
                out[...] = jnp.concatenate([w_ref[:, s : s + strip] for s in starts], axis=1)


def take_strips(place, w, n_dp, n_u, strip):
    depth, total = w.shape
    rows = 64
    out = pl.BlockSpec((rows, n_dp * strip), lambda i: (i, 0))
    shape = jax.ShapeDtypeStruct((depth, n_dp * strip), w.dtype)
    return pl.pallas_call(
        functools.partial(strips_kernel, n_dp, n_u, strip),
        grid=(depth // rows,),
        in_specs=[pl.BlockSpec(memory_space=pltpu.SMEM), pl.BlockSpec((rows, total), lambda i: (i, 0))],
        out_specs=[out, out],
        out_shape=[shape, shape],
        compiler_params=params(),
        cost_estimate=cost(0, 2 * depth * total + 4 * depth * n_dp * strip),
        name="take_strips",
    )(place, w)


def fill(scratch, keys, refs):
    for key_list, ref in zip(keys, refs):
        for at, key in enumerate(key_list):
            scratch[key] = ref[at]


def put_call(kernel, place, helds, grid, blocks, at, out_block, out_at, out_shape, name):
    n_u = sum(len(k) for k in helds[0][0])
    count = sum(len(b) for _, b in helds)

    def body(place_ref, *refs):
        refs = list(refs)
        scratches = refs[count + 1 :]
        for (keys, _), scratch in zip(helds, scratches):
            fill(scratch, keys, [refs.pop(0) for _ in keys])
        kernel(place_ref[1], scratches, refs[0])

    return pl.pallas_call(
        body,
        grid=(grid,),
        in_specs=[pl.BlockSpec(memory_space=pltpu.SMEM)]
        + [pl.BlockSpec((len(k),) + block, at) for (keys, _), block in zip(helds, blocks) for k in keys],
        out_specs=pl.BlockSpec(out_block, out_at),
        out_shape=jax.ShapeDtypeStruct(out_shape, jnp.float32),
        scratch_shapes=[pltpu.VMEM((n_u,) + block, jnp.bfloat16) for block in blocks],
        compiler_params=params(),
        cost_estimate=cost(0, 6 * out_shape[0] * out_shape[1]),
        name=name,
    )(place, *[v for _, held in helds for v in held])


def put_strips(place, helds, n_dp, strip):
    n_u = sum(len(k) for k in helds[0][0])
    depth, width = helds[0][1][0].shape[1:]
    rows = min(32, depth)

    def kernel(me, scratches, out_ref):
        size = n_u * strip
        for h, scratch in enumerate(scratches):
            parts = [scratch[me ^ t].astype(jnp.float32) for t in range(n_u)]
            for b in range(n_dp):
                at = (h * n_dp + b) * size
                out_ref[:, at : at + size] = jnp.concatenate(
                    [p[:, b * strip : (b + 1) * strip] for p in parts], axis=1
                )

    total = len(helds) * n_u * width
    return put_call(
        kernel, place, helds, depth // rows, [(rows, width)] * len(helds), lambda i: (0, i, 0),
        (rows, total), lambda i: (i, 0), (depth, total), "put_strips",
    )


def put_columns(place, helds, sections):
    n_u = sum(len(k) for k in helds[0][0])
    depth = helds[0][1][0].shape[1]
    rows = min(64, depth)

    def kernel(me, scratches, out_ref):
        at = 0
        for scratch, parts in zip(scratches, sections):
            for start, size in parts:
                for t in range(n_u):
                    out_ref[:, at : at + size] = scratch[me ^ t, :, start : start + size].astype(jnp.float32)
                    at += size

    total = n_u * sum(size for parts in sections for _, size in parts)
    return put_call(
        kernel, place, helds, depth // rows, [(rows, held[0].shape[2]) for _, held in helds], lambda i: (0, i, 0),
        (rows, total), lambda i: (i, 0), (depth, total), "put_columns",
    )


def put_rows(place, held):
    n_u = sum(len(k) for k in held[0])
    depth, width = held[1][0].shape[1:]
    tile = 512

    def kernel(me, scratches, out_ref):
        for t in range(n_u):
            out_ref[t * depth : (t + 1) * depth] = scratches[0][me ^ t].astype(jnp.float32)

    return put_call(
        kernel, place, [held], width // tile, [(depth, tile)], lambda i: (0, 0, i),
        (n_u * depth, tile), lambda i: (0, i), (n_u * depth, width), "put_rows",
    )


def norm_call(kernel, inputs, gain, outs, gain_sum, name):
    r, width = inputs[0].shape
    tile = min(64, r)
    step = pl.BlockSpec((tile, width), lambda i: (i, 0))
    one = pl.BlockSpec((1, width), lambda i: (0, 0))
    shapes = [jax.ShapeDtypeStruct((r, width), o) for o in outs]
    if gain_sum:
        shapes.append(jax.ShapeDtypeStruct((1, width), jnp.float32))
    return pl.pallas_call(
        kernel,
        grid=(r // tile,),
        in_specs=[step] * len(inputs) + [one],
        out_specs=[step] * len(outs) + [one] * gain_sum,
        out_shape=shapes,
        compiler_params=params(),
        cost_estimate=cost(0, sum(4 * v.size for v in inputs)),
        name=name,
    )(*inputs, gain)


def norm_back(source, keep, got, residual, gain, rounded):
    def kernel(source_ref, keep_ref, got_ref, residual_ref, gain_ref, *outs):
        @pl.when(pl.program_id(0) == 0)
        def _():
            outs[-1][...] = jnp.zeros_like(outs[-1])

        up = keep_ref[...] + got_ref[...].astype(jnp.float32)
        source = source_ref[...].astype(jnp.float32)
        factor = head_scale(source)
        weighted = up * gain_ref[...]
        inner = jnp.mean(weighted * source, axis=-1, keepdims=True)
        total = residual_ref[...].astype(jnp.float32) + factor * weighted
        total = total - source * (factor * factor * factor) * inner
        outs[0][...] = total
        if rounded:
            outs[1][...] = total.astype(jnp.bfloat16)
        outs[-1][...] += jnp.sum(up * source * factor, axis=0, keepdims=True)

    outs = [jnp.float32] + [jnp.bfloat16] * rounded
    return norm_call(kernel, (source, keep, got, residual), gain, outs, 1, "norm_back")


def halve(keep, got):
    pairs, (r, c) = keep.shape[0] // 2, keep.shape[1:]
    tile = min(64, r)

    def kernel(keep_ref, got_ref, even_ref, odd_ref):
        even_ref[0] = keep_ref[0].astype(jnp.float32) + got_ref[0].astype(jnp.float32)
        odd_ref[0] = (keep_ref[1].astype(jnp.float32) + got_ref[1].astype(jnp.float32)).astype(jnp.bfloat16)

    two = pl.BlockSpec((2, tile, c), lambda p, i: (p, i, 0))
    one = pl.BlockSpec((1, tile, c), lambda p, i: (p, i, 0))
    return pl.pallas_call(
        kernel,
        grid=(pairs, r // tile),
        in_specs=[two, two],
        out_specs=[one, one],
        out_shape=[jax.ShapeDtypeStruct((pairs, r, c), jnp.float32), jax.ShapeDtypeStruct((pairs, r, c), jnp.bfloat16)],
        compiler_params=params(),
        cost_estimate=cost(0, 16 * pairs * r * c),
        name="halve",
    )(keep, got)


def out_terms(place, gated, upstream, n_u):
    m, q = gated.shape
    c = upstream.shape[1] // n_u

    def kernel(place_ref, x_ref, y_ref, out_ref):
        out_ref[0] = lax.dot_general(x_ref[...], y_ref[...], TN, preferred_element_type=jnp.float32).astype(jnp.bfloat16)

    return pl.pallas_call(
        kernel,
        grid_spec=pltpu.PrefetchScalarGridSpec(
            num_scalar_prefetch=1,
            grid=(n_u,),
            in_specs=[
                pl.BlockSpec((m, q), lambda k, p: (0, 0)),
                pl.BlockSpec((m, c), lambda k, p: (0, p[1] ^ k)),
            ],
            out_specs=pl.BlockSpec((1, q, c), lambda k, p: (k, 0, 0)),
        ),
        out_shape=jax.ShapeDtypeStruct((n_u, q, c), jnp.bfloat16),
        compiler_params=params(),
        cost_estimate=cost(2 * m * q * c * n_u, 2 * m * q + 4 * m * c * n_u),
        name="out_terms",
    )(place, gated, upstream)


MESH = pl.DeviceIdType.MESH


class Group:
    def __init__(self, n_dp, n_u):
        self.n_dp, self.n_u = n_dp, n_u
        index = lax.axis_index("dp")
        self.me = lax.axis_index("ulysses")
        odd = index % 2
        self.position = (1 - odd) * (index // 2) + odd * (n_dp - 1 - index // 2)
        self.next = (self.owner(1), self.owner(-1))
        self.bits = [1 << k for k in range(n_u.bit_length() - 1)]

    def owner(self, offset):
        place = (self.position + offset + self.n_dp) % self.n_dp
        late = place // (self.n_dp // 2)
        return (1 - late) * (2 * place) + late * (2 * (self.n_dp - 1 - place) + 1)

    def greet(self):
        barrier = pltpu.get_barrier_semaphore()
        for way in (0, 1):
            pl.semaphore_signal(barrier, inc=1, device_id={"dp": self.next[way]}, device_id_type=MESH)
        for other in range(1, self.n_u):
            pl.semaphore_signal(barrier, inc=1, device_id={"ulysses": self.me ^ other}, device_id_type=MESH)
        pl.semaphore_wait(barrier, 1 + self.n_u)

    def to_ring(self, way, source, target, send, recv):
        copy = pltpu.make_async_remote_copy(
            src_ref=source, dst_ref=target, send_sem=send, recv_sem=recv,
            device_id={"dp": self.next[way]}, device_id_type=MESH,
        )
        copy.start()
        return copy

    def to_cube(self, bit, source, target, send, recv):
        copy = pltpu.make_async_remote_copy(
            src_ref=source, dst_ref=target, send_sem=send, recv_sem=recv,
            device_id={"ulysses": self.me ^ bit}, device_id_type=MESH,
        )
        copy.start()
        return copy

    def reach(self, more_ahead):
        longer = self.n_dp // 2
        shorter = self.n_dp - 1 - longer
        return (longer, shorter) if more_ahead else (shorter, longer)


class Spread:
    def __init__(self, group, own, out, send, recv):
        self.group, self.own, self.out, self.send, self.recv = group, own, out, send, recv
        self.keys, self.levels, self.copies, self.used, self.waited = [0], group.bits[::-1], [], 0, 0

    def level(self):
        for copy in self.copies[self.waited :]:
            copy.wait_recv()
        self.waited = len(self.copies)
        if not self.levels:
            return False
        bit = self.levels.pop(0)
        for key in sorted(self.keys):
            source = self.own if key == 0 else self.out.at[key]
            at = self.used
            self.copies.append(
                self.group.to_cube(bit, source, self.out.at[key ^ bit], self.send.at[at], self.recv.at[at])
            )
            self.used += 1
        self.keys += [key ^ bit for key in self.keys]
        return True

    def finish(self):
        while self.level():
            pass
        for copy in self.copies:
            copy.wait_send()


class RingGather:
    def __init__(self, group, chains, send, recv):
        self.group, self.chains, self.send_sems, self.recv_sems = group, chains, send, recv
        self.copies = {}

    def place(self, c, owner):
        _, out, block, low, rows, _ = self.chains[c]
        return out.at[pl.ds(pl.multiple_of(owner * block + low, 16), rows)]

    def item(self, c):
        item, _, _, low, rows, _ = self.chains[c]
        return item.at[low : low + rows]

    def reach(self, c, way):
        return self.group.reach(self.chains[c][5])[way]

    def send(self, c, way, step):
        owner = self.group.owner(1 - step if way == 0 else step - 1)
        source = self.item(c) if step == 1 else self.place(c, owner)
        sems = (c, way, step - 1)
        self.copies[sems] = self.group.to_ring(
            way, source, self.place(c, owner), self.send_sems.at[sems], self.recv_sems.at[sems]
        )

    def start(self, c):
        for way in (0, 1):
            self.send(c, way, 1)

    def event(self, c, way, step):
        if step <= self.reach(c, way):
            self.copies[c, way, step - 1].wait_recv()
            if step < self.reach(c, way):
                self.send(c, way, step + 1)

    def finish(self):
        for copy in self.copies.values():
            copy.wait_send()


def by_rows(count, tile, function):
    def body(i, carry):
        function(pl.ds(pl.multiple_of(i * tile, tile), tile))
        return carry

    lax.fori_loop(0, count // tile, body, 0)


def forward_kernel(
    n_dp, n_u, heads, kv_heads, length_ref, tokens_ref, gain_one, gain_two, q_gain, k_gain, cosine, sine, grad_ref,
    out_item, qk_item, vg_item, gate_item, up_item, down_item,
    w_qk, w_vg, w_gate, w_up, w_down, normed_out, grad_out, second_out, act_gate, act_up, act_hidden,
    raw_qk, raw_vg, q_out, k_out, v_out, gate_out, attended_out, gated_out, total_out, w_out, hidden_out,
    normed, own, qk_local, vg_local, columns, turned, parts, core_got, total, second_own, gate_stage, up_stage, hidden_stage,
    ring_send, ring_recv, cube_send, cube_recv, turn_send, turn_recv, sum_send, sum_recv, local,
):
    rows_own, width = tokens_ref.shape
    bucket = rows_own * n_u
    size = HEAD_DIMENSION
    copies = heads // kv_heads
    depth = width // n_dp
    group = Group(n_dp, n_u)
    me, mine = group.me, group.owner(0)
    group.greet()
    strip = down_item.shape[0]
    halves = 2 if strip % 32 == 0 else 1
    chains = [
        (out_item, columns, depth, 0, depth, True),
        (qk_item, w_qk, depth, 0, depth, False),
        (vg_item, w_vg, depth, 0, depth, True),
        (gate_item, w_gate, depth, 0, depth, True),
        (up_item, w_up, depth, 0, depth, False),
    ]
    for p in range(halves):
        chains.append((down_item, w_down, strip, p * strip // halves, strip // halves, p == 0))
    ring = RingGather(group, chains, ring_send, ring_recv)
    kept = []

    def keep(source, target):
        copy = pltpu.make_async_copy(source, target, local.at[len(kept)])
        copy.start()
        kept.append(copy)
        return copy

    for c in (0, 1, 2):
        ring.start(c)
    own_rows = lambda out, block: out.at[pl.ds(pl.multiple_of(mine * block, 16), block)]
    for item, out, block in (
        (out_item, columns, depth), (qk_item, w_qk, depth), (vg_item, w_vg, depth),
        (gate_item, w_gate, depth), (up_item, w_up, depth), (down_item, w_down, strip),
    ):
        keep(item, own_rows(out, block))

    def first(rows):
        x = tokens_ref[rows].astype(jnp.float32)
        own[rows] = (x * head_scale(x) * gain_one[...]).astype(jnp.bfloat16)

    by_rows(rows_own, 64, first)
    keep(own, normed.at[0]).wait()
    keep(grad_ref, grad_out.at[0])
    spreads = [
        Spread(group, own, normed, cube_send.at[0], cube_recv.at[0]),
        Spread(group, grad_ref, grad_out, cube_send.at[1], cube_recv.at[1]),
    ]
    spreads[0].level()
    longest = n_dp // 2
    for step in range(1, longest + 1):
        for c in (0, 1, 2):
            for way in (0, 1):
                ring.event(c, way, step)
        if step == 1:
            spreads[1].level()
        if step < longest:
            spreads[0 if step % 2 == 1 else 1].level()
        if step == longest - 1:
            for c in (3, 4):
                ring.start(c)
    spreads[0].finish()
    events = []
    for step in range(1, longest + 1):
        events += [[(3, 0, step), (4, 1, step)], [(4, 0, step), (3, 1, step)]]
        if step == longest - 1:
            events.append([("start",)])
    for step in range(1, longest + 1):
        if halves == 2:
            events += [[(5, 0, step), (6, 1, step)], [(6, 0, step), (5, 1, step)]]
        else:
            events += [[(5, 0, step), (5, 1, step)]]

    def pump(count=1):
        while count and events:
            pair = events.pop(0)
            if pair[0][0] == "start":
                for c in range(5, len(chains)):
                    ring.start(c)
                continue
            for event in pair:
                ring.event(*event)
            count -= 1

    for copy in kept[:3]:
        copy.wait()
    share = depth * n_dp // n_u
    turns = []
    for k in range(1, n_u):
        source = columns.at[pl.ds(pl.multiple_of((me ^ k) * share, 16), share)]
        turns.append(group.to_cube(k, source, turned.at[k], turn_send.at[k - 1], turn_recv.at[k - 1]))
    keep(columns.at[pl.ds(pl.multiple_of(me * share, 16), share)], turned.at[0]).wait()
    one, two = keep(w_qk, qk_local), keep(w_vg, vg_local)
    normed_copy = keep(normed, normed_out)
    one.wait()
    two.wait()

    def project(b, carry):
        x = normed[b]
        raw_qk[b] = jnp.dot(x, qk_local[...], preferred_element_type=jnp.float32)
        raw_vg[b] = jnp.dot(x, vg_local[...], preferred_element_type=jnp.float32)
        return carry

    lax.fori_loop(0, n_u, project, 0)
    normed_copy.wait()
    pump()

    length = length_ref[0]
    block = min(256, bucket)

    def attention(h, carry):
        def column(ref, at):
            at = pl.multiple_of(at * size, size)
            return jnp.concatenate([ref[me ^ t, :, pl.ds(at, size)] for t in range(n_u)], axis=0)

        at = pl.ds(pl.multiple_of(h * size, size), size)
        kv = pl.ds(pl.multiple_of(h // copies * size, size), size)
        q = column(raw_qk, h)
        q = turn_pairs(q * head_scale(q) * q_gain[...], cosine[...], sine[...]).astype(jnp.bfloat16)
        q_out[:, at] = q
        k = column(raw_qk, heads + h // copies)
        k = turn_pairs(k * head_scale(k) * k_gain[...], cosine[...], sine[...]).astype(jnp.bfloat16)
        k_out[:, kv] = k
        v = column(raw_vg, h // copies).astype(jnp.bfloat16)
        v_out[:, kv] = v
        gate = jax.nn.sigmoid(column(raw_vg, kv_heads + h))
        gate_out[:, at] = gate
        for start in range(0, bucket, block):
            rows = slice(start, start + block)
            scores = masked_scores(q[rows], k[: start + block], start, length)
            top = jnp.max(scores, axis=-1, keepdims=True)
            soft = jnp.exp(scores - top)
            sums = jnp.sum(soft, axis=-1, keepdims=True)
            out = jnp.dot(soft.astype(jnp.bfloat16), v[: start + block], preferred_element_type=jnp.float32) / sums
            out = out.astype(jnp.bfloat16)
            attended_out[rows, at] = out
            total_out[h, rows] = top + jnp.log(sums)
            gated = (out.astype(jnp.float32) * gate[rows]).astype(jnp.bfloat16)
            for t in range(start // rows_own, (start + block) // rows_own):
                inside = slice(t * rows_own - start, (t + 1) * rows_own - start)
                gated_out[me ^ t, :, at] = gated[inside]
        return carry

    lax.fori_loop(0, heads, attention, 0)
    pump()
    for copy in turns:
        copy.wait_recv()
    c_width = columns.shape[1]
    for k in range(n_u):
        w_out[:, pl.ds(pl.multiple_of((me ^ k) * c_width, c_width), c_width)] = turned[k]

    def branch(b, carry):
        parts[b] = jnp.dot(gated_out[b], w_out[...], preferred_element_type=jnp.float32).astype(jnp.bfloat16)
        return carry

    lax.fori_loop(0, n_u, branch, 0)
    held = list(range(n_u))
    used = 0
    sums = []
    for bit in group.bits:
        keys = [key for key in held if not key & bit]
        level = []
        for key in keys:
            level.append(
                group.to_cube(bit, parts.at[key | bit], core_got.at[used], sum_send.at[used], sum_recv.at[used])
            )
            used += 1
        sums += level
        pump()
        for at, (key, copy) in enumerate(zip(keys, level)):
            copy.wait_recv()
            slot = used - len(keys) + at

            def add(rows, key=key, slot=slot):
                got = core_got[slot, rows].astype(jnp.float32)
                if key:
                    parts[key, rows] = (parts[key, rows].astype(jnp.float32) + got).astype(jnp.bfloat16)
                elif bit == 1:
                    total[rows] = tokens_ref[rows].astype(jnp.float32) + parts[0, rows].astype(jnp.float32) + got
                else:
                    total[rows] = total[rows] + got

            by_rows(rows_own, 64, add)
        held = keys

    def second(rows):
        hidden = total[rows]
        hidden_out[rows] = hidden
        second_own[rows] = (hidden * head_scale(hidden) * gain_two[...]).astype(jnp.bfloat16)

    by_rows(rows_own, 64, second)
    spread = Spread(group, second_own, normed, cube_send.at[2], cube_recv.at[2])
    keep(second_own, normed.at[0])
    while spread.level():
        pump(2)
    kept[12].wait()
    second_copy = keep(normed, second_out)
    while events and events[0][0][0] in ("start", 3, 4):
        pump(1)
    for copy in kept[3:5]:
        copy.wait()
    n = qk_local.shape[1]
    for part in range(w_gate.shape[1] // n):
        where = slice(part * n, (part + 1) * n)
        at = 14 + 5 * part
        loads = [
            pltpu.make_async_copy(w_gate.at[:, where], qk_local, local.at[at]),
            pltpu.make_async_copy(w_up.at[:, where], vg_local, local.at[at + 1]),
        ]
        for copy in loads:
            copy.start()
        for copy in loads:
            copy.wait()

        def expand(b, carry):
            x = normed[b]
            one = jnp.dot(x, qk_local[...], preferred_element_type=jnp.float32)
            two = jnp.dot(x, vg_local[...], preferred_element_type=jnp.float32)
            gate_stage[b] = one
            up_stage[b] = two
            hidden_stage[b] = (one * jax.nn.sigmoid(one) * two).astype(jnp.bfloat16)
            return carry

        lax.fori_loop(0, n_u, expand, 0)
        stores = []
        for k, (stage, out) in enumerate(((gate_stage, act_gate), (up_stage, act_up), (hidden_stage, act_hidden))):
            copy = pltpu.make_async_copy(stage, out.at[:, :, where], local.at[at + 2 + k])
            copy.start()
            stores.append(copy)
        pump(2)
        for copy in stores:
            copy.wait()
    second_copy.wait()
    spreads[1].finish()
    spread.finish()
    pump(1000)
    ring.finish()
    for copy in turns + sums:
        copy.wait_send()
    for copy in kept[5:6] + kept[7:8]:
        copy.wait()


def forward(length, tokens_own, gains, tables, grad_own, items, n_dp, n_u, heads, kv_heads):
    anywhere = pl.BlockSpec(memory_space=pl.ANY)
    local = pl.BlockSpec(memory_space=pltpu.VMEM)
    rows, width = tokens_own.shape
    bucket, size = rows * n_u, HEAD_DIMENSION
    total = (heads + kv_heads) * size
    depth = width // n_dp
    columns = items[0].shape[1]
    share = width // n_u
    longest = n_dp // 2

    def shape(*dims, dtype=jnp.bfloat16):
        return jax.ShapeDtypeStruct(dims, dtype)

    out_shape = [shape(n_dp * i.shape[0], i.shape[1]) for i in items[1:]]
    out_shape += [shape(n_u, rows, width)] * 3
    hidden = items[4].shape[1]
    out_shape += [shape(n_u, rows, hidden, dtype=jnp.float32)] * 2 + [shape(n_u, rows, hidden)]
    out_shape += [shape(n_u, rows, total, dtype=jnp.float32)] * 2
    out_shape += [
        shape(bucket, heads * size), shape(bucket, kv_heads * size), shape(bucket, kv_heads * size),
        shape(bucket, heads * size, dtype=jnp.float32), shape(bucket, heads * size),
        shape(n_u, rows, heads * size), shape(heads, bucket, 1, dtype=jnp.float32),
        shape(share, width), shape(rows, width, dtype=jnp.float32),
    ]
    dma = pltpu.SemaphoreType.DMA
    return pl.pallas_call(
        functools.partial(forward_kernel, n_dp, n_u, heads, kv_heads),
        in_specs=[pl.BlockSpec(memory_space=pltpu.SMEM)] + [local] * 7 + [anywhere] * 7,
        out_specs=[anywhere] * 11 + [local] * 11,
        out_shape=out_shape,
        scratch_shapes=[
            pltpu.VMEM((n_u, rows, width), jnp.bfloat16),
            pltpu.VMEM((rows, width), jnp.bfloat16),
            pltpu.VMEM((width, total), jnp.bfloat16),
            pltpu.VMEM((width, total), jnp.bfloat16),
            pltpu.VMEM((width, columns), jnp.bfloat16),
            pltpu.VMEM((n_u, share, columns), jnp.bfloat16),
            pltpu.VMEM((n_u, rows, width), jnp.bfloat16),
            pltpu.VMEM((n_u - 1, rows, width), jnp.bfloat16),
            pltpu.VMEM((rows, width), jnp.float32),
            pltpu.VMEM((rows, width), jnp.bfloat16),
            pltpu.VMEM((n_u, rows, total), jnp.float32),
            pltpu.VMEM((n_u, rows, total), jnp.float32),
            pltpu.VMEM((n_u, rows, total), jnp.bfloat16),
            dma((7, 2, longest)), dma((7, 2, longest)), dma((3, n_u - 1)), dma((3, n_u - 1)),
            dma((n_u - 1,)), dma((n_u - 1,)), dma((n_u - 1,)), dma((n_u - 1,)), dma((14 + 5 * (hidden // total),)),
        ],
        compiler_params=pltpu.CompilerParams(vmem_limit_bytes=60 * 1024 * 1024, collective_id=0, has_side_effects=True),
        cost_estimate=cost(),
        name="forward",
    )(length, tokens_own, *gains, *tables, grad_own, *items)


def reduce_kernel(n_dp, n_u, count, blocks_ref, *refs):
    given, outs = list(refs[: count - 1]), refs[count - 1 : 2 * count - 1]
    refs = refs[2 * count - 1 :]
    slots, sums, terms = refs[:count], refs[count : 2 * count], refs[2 * count : 3 * count]
    ring_send, ring_recv, cube_send, cube_recv, turn_send, turn_recv, local = refs[3 * count :]
    out_terms_ref = terms[-1]
    given.append(out_terms_ref)
    loads = {c: pltpu.make_async_copy(given[c], terms[c], local.at[count + 1 + c]) for c in range(count - 1)}
    group = Group(n_dp, n_u)
    group.greet()
    copies = {}
    reaches = [group.reach(c % 2 == 0) for c in range(count)]
    longest = n_dp // 2
    share = blocks_ref.shape[1]
    here = out_terms_ref.at[pl.ds(pl.multiple_of(group.me * share, share), share)]

    def add(c, target, offset, others):
        r = target.shape[0]
        tile = 16
        first = group.owner(offset) * r

        def body(i, carry):
            rows = pl.ds(pl.multiple_of(i * tile, tile), tile)
            total = terms[c][pl.ds(pl.multiple_of(first + i * tile, tile), tile)].astype(jnp.float32)
            for other in others:
                total = total + other[rows].astype(jnp.float32)
            target[rows] = total.astype(jnp.bfloat16)
            return carry

        lax.fori_loop(0, r // tile, body, 0)

    def slot(c, way, step):
        return slots[c].at[way, step]

    def send(c, way, step):
        reach = reaches[c][way]
        offset = (reach - step) if way == 0 else (step - reach)
        if step == 0:
            r = sums[c].shape[0]
            source = given[c].at[pl.ds(pl.multiple_of(group.owner(offset) * r, r), r)]
        else:
            if c in loads:
                loads.pop(c).wait()
            source = slot(c, way, step - 1)
            add(c, source, offset, [source])
        sems = (c, way, step)
        copies[sems] = group.to_ring(way, source, slot(c, way, step), ring_send.at[sems], ring_recv.at[sems])

    def start(chains):
        for c in chains:
            for way in (0, 1):
                send(c, way, 0)

    phases = [(0, 1), (2, 3)]
    start(phases[0])
    for copy in loads.values():
        copy.start()
    turns = []
    for k in range(1, n_u):
        turns.append(group.to_cube(k, blocks_ref.at[k], here, turn_send.at[k - 1], turn_recv.at[k - 1]))
    own = pltpu.make_async_copy(blocks_ref.at[0], here, local.at[count])
    own.start()
    own.wait()
    spreads, kept = [], []
    for phase, chains in enumerate(phases):
        for step in range(longest):
            for c in chains:
                for way in (0, 1):
                    if step < reaches[c][way]:
                        copies[c, way, step].wait_recv()
                        if step + 1 < reaches[c][way]:
                            send(c, way, step + 1)
            if step == longest - 2 and phase == 0:
                for copy in turns:
                    copy.wait_recv()
                start(phases[1])
            if phase == 1 and step % 2 == 1 and step < longest - 1:
                for spread in spreads:
                    spread.level()
            if step == longest - 1:
                for c in chains:
                    add(c, sums[c], 0, [slot(c, way, reaches[c][way] - 1) for way in (0, 1)])
                    spread = Spread(group, sums[c], outs[c], cube_send.at[c], cube_recv.at[c])
                    copy = pltpu.make_async_copy(sums[c], outs[c].at[0], local.at[c])
                    copy.start()
                    kept.append(copy)
                    spread.level()
                    spreads.append(spread)
    for spread in spreads:
        spread.level()
    for spread in spreads:
        spread.finish()
    for copy in list(copies.values()) + turns:
        copy.wait_send()
    for copy in kept:
        copy.wait()


def reduce_all(blocks, terms, n_dp, n_u):
    count = len(terms) + 1
    anywhere = pl.BlockSpec(memory_space=pl.ANY)
    local = pl.BlockSpec(memory_space=pltpu.VMEM)
    longest = n_dp // 2
    whole = (blocks.shape[0] * blocks.shape[1], blocks.shape[2])
    sizes = [(r // n_dp, c) for r, c in [t.shape for t in terms] + [whole]]
    dma = pltpu.SemaphoreType.DMA
    return pl.pallas_call(
        functools.partial(reduce_kernel, n_dp, n_u, count),
        in_specs=[anywhere] * count,
        out_specs=[anywhere] * count,
        out_shape=[jax.ShapeDtypeStruct((n_u,) + b, jnp.bfloat16) for b in sizes],
        scratch_shapes=[pltpu.VMEM((2, longest) + b, jnp.bfloat16) for b in sizes]
        + [pltpu.VMEM(b, jnp.bfloat16) for b in sizes]
        + [
            pltpu.VMEM(t.shape, jnp.bfloat16)
            for t in terms
        ]
        + [
            pltpu.VMEM(whole, jnp.bfloat16),
            dma((count, 2, longest)), dma((count, 2, longest)), dma((count, n_u - 1)), dma((count, n_u - 1)),
            dma((n_u - 1,)), dma((n_u - 1,)), dma((2 * count,)),
        ],
        compiler_params=pltpu.CompilerParams(vmem_limit_bytes=VMEM_LIMIT, collective_id=1, has_side_effects=True),
        cost_estimate=cost(),
        name="reduce_all",
    )(blocks, *terms)


START = 0.9
LATENCY = 6.0
RATES = {"ring": 50.0, "x": 50.0, "core": 250.0}


class Flight:
    def __init__(self, value, arrival):
        self.value, self.arrival = value, arrival


class Sequence:
    def __init__(self):
        self.last = ()
        self.now = 0.0
        self.free = {}
        self.sources = []
        self.fillers = []

    def tie(self, *values):
        tied, _ = lax.optimization_barrier((values, self.last))
        self.last = tied
        return tied

    def run(self, cost, function, *values, take=True):
        if take:
            self.poll()
        out = function(*self.tie(*values))
        self.now += cost
        if isinstance(out, (tuple, list)):
            return self.tie(*out)
        return self.tie(out)[0]

    def fly(self, value, axis, pairs, link, kind):
        (value,) = self.tie(value)
        got = lax.ppermute(value, axis, pairs)
        start = max(self.now + START, self.free.get(link, 0.0))
        end = start + value.size * value.dtype.itemsize / 1000.0 / RATES[kind]
        self.free[link] = end
        self.now += START
        return Flight(got, end + LATENCY)

    def land(self, *flights):
        self.idle(max(f.arrival for f in flights))
        return self.tie(*[f.value for f in flights])

    def poll(self):
        moved = True
        while moved:
            moved = any([source.poll(self.now) for source in self.sources])

    def later(self, cost, ready, function):
        self.fillers.append((cost, ready, function))

    def fill(self):
        for at, (cost, ready, function) in enumerate(self.fillers):
            if ready():
                self.fillers.pop(at)
                function()
                return True
        return False

    def idle(self, until):
        while True:
            self.poll()
            if self.now >= until:
                return
            if until - self.now > 2.0 and self.fill():
                continue
            events = [e for source in self.sources for e in [source.next()] if e is not None]
            self.now = max(self.now, min(events + [until]))

    def drain(self, done):
        while not done():
            self.poll()
            if done():
                return
            if self.fill():
                continue
            events = [e for source in self.sources for e in [source.next()] if e is not None]
            assert events
            self.now = max(self.now, min(events))


def pick(value, index):
    return lax.dynamic_index_in_dim(value, index, 0, keepdims=False, allow_negative_indices=False)


class Cube:
    def __init__(self, axis, seq):
        self.axis = axis
        self.seq = seq
        self.count = lax.axis_size(axis)
        self.me = lax.axis_index(axis)
        bits = []
        bit = 1
        while bit < self.count:
            bits.append(bit)
            bit *= 2
        self.bits = bits

    def swap(self, value, bit):
        kind = "core" if bit == 1 else "x"
        return self.seq.fly(value, self.axis, [(i, i ^ bit) for i in range(self.count)], kind, kind)

    def gather(self, item):
        keys, blocks = [[0]], [item[None]]
        for bit in self.bits[::-1]:
            order = sorted((key, at, sub) for at, ks in enumerate(keys) for sub, key in enumerate(ks))
            if len(order) > 1:
                sent = self.seq.run(
                    2.0, lambda *b: jnp.concatenate([b[at][sub : sub + 1] for _, at, sub in order]), *blocks
                )
            else:
                sent = blocks[0]
            (got,) = yield [self.swap(sent, bit)]
            keys = keys + [[key ^ bit for key, _, _ in order]]
            blocks = blocks + [got]
        return (keys, blocks)

    def joined(self, held):
        keys, blocks = held
        order = sorted((key, at, sub) for at, ks in enumerate(keys) for sub, key in enumerate(ks))
        return self.seq.run(3.0, lambda *b: jnp.concatenate([b[at][sub : sub + 1] for _, at, sub in order]), *blocks)

    def reduce(self, keep, send):
        for bit in self.bits:
            (got,) = yield [self.swap(send, bit)]
            if bit != self.bits[-1]:
                keep, send = self.seq.run(4.4, halve, keep, got)
        return (keep[0], got[0])

    def turn(self, blocks):
        got = yield [self.swap(blocks[bit], bit) for bit in range(1, self.count)]
        return [blocks[0]] + list(got)

    def total(self, value, axes):
        for axis in axes:
            count = lax.axis_size(axis)
            bit = 1
            while bit < count:
                pairs = [(i, i ^ bit) for i in range(count)]
                (got,) = yield [self.seq.fly(value, axis, pairs, "sum", "ring")]
                value = self.seq.run(1.0, lambda a, b: a + b, value, got)
                bit *= 2
        return value


class Task:
    def __init__(self, seq, generator, urgent=True):
        self.seq, self.generator = seq, generator
        self.value, self.flights, self.over, self.busy = None, None, False, False
        seq.sources.append(self)
        self.go(None)

    def go(self, values):
        self.busy = True
        try:
            self.flights = self.generator.send(values)
        except StopIteration as stop:
            self.value, self.over = stop.value, True
            self.seq.sources.remove(self)
        self.busy = False

    def next(self):
        return None if self.busy or self.over else max(f.arrival for f in self.flights)

    def poll(self, now):
        if self.busy or self.over or self.next() > now + 0.5:
            return False
        self.go(self.seq.tie(*[f.value for f in self.flights]))
        return True

    def finish(self):
        while not self.over:
            if self.busy:
                raise RuntimeError
            self.seq.idle(self.next())
        return self.value


def dot(a, b):
    return jnp.einsum("mk,kn->mn", a, b, preferred_element_type=jnp.float32)


def dot_nt(a, b):
    return jnp.einsum("mk,nk->mn", a, b, preferred_element_type=jnp.float32)


def dot_tn(a, b):
    return jnp.einsum("km,kn->mn", a, b, preferred_element_type=jnp.float32)


def low(value):
    return value.astype(jnp.bfloat16)


def high(value):
    return value.astype(jnp.float32)


def shards(
    tokens,
    seq_lengths,
    cotangent,
    norm1_gain,
    input_weight,
    query_gain,
    key_gain,
    output_weight,
    norm2_gain,
    perceptron_input_weight,
    down_weight,
):
    _, rows, width = tokens.shape
    seq = Sequence()
    cube = Cube("ulysses", seq)
    n_dp = lax.axis_size("dp")
    n_u, me = cube.count, cube.me
    bucket = rows * n_u
    depth = width // n_dp
    heads = QUERY_HEADS // n_u
    kv_heads = KEY_VALUE_HEADS // n_u
    copies = QUERY_HEADS // KEY_VALUE_HEADS
    head_width = HEAD_DIMENSION
    q_w, kv_w = heads * head_width, kv_heads * head_width
    query_width = QUERY_HEADS * head_width
    kv_all = KEY_VALUE_HEADS * head_width
    ff_strip = FF // n_dp // n_u
    ff_local = FF // n_u
    half = width // 2
    out_cols = width // n_u
    place = jnp.stack([seq_lengths[0], me])
    length = seq_lengths[0]
    q_gain, k_gain = query_gain[None], key_gain[None]
    gain_one, gain_two = norm1_gain[None], norm2_gain[None]
    positions = me * rows + jnp.arange(rows)
    def cut(value, start, size):
        return lax.dynamic_slice_in_dim(value, start, size, 1)

    def task(generator):
        return Task(seq, generator)

    frequency = np.float32(ROPE_BASE) ** (np.float32(-2.0) * np.arange(head_width // 2, dtype=np.float32) / head_width)
    angles = np.arange(bucket, dtype=np.float32)[:, None] * frequency.astype(np.float32)[None, :]
    cosine, sine = np.cos(angles), np.sin(angles)
    tables = (
        jnp.asarray(np.concatenate([cosine, cosine], axis=1), jnp.float32),
        jnp.asarray(np.concatenate([-sine, sine], axis=1), jnp.float32),
    )

    gate_item, up_item = seq.run(
        4.9, lambda p, w: take_strips(p, w, n_dp, n_u, ff_strip), place, perceptron_input_weight
    )
    out_item, qk_item, vg_item, grad_own, down_item = seq.run(
        3.0,
        lambda o, w, c, d: (
            cut(o, me * out_cols, out_cols),
            jnp.concatenate([cut(w, me * q_w, q_w), cut(w, query_width + me * kv_w, kv_w)], axis=1),
            jnp.concatenate(
                [
                    cut(w, query_width + kv_all + me * kv_w, kv_w),
                    cut(w, query_width + 2 * kv_all + me * q_w, q_w),
                ],
                axis=1,
            ),
            jnp.where((positions < length)[:, None], c, jnp.zeros_like(c)),
            lax.dynamic_slice_in_dim(d, me * ff_strip, ff_strip, 0),
        ),
        output_weight,
        input_weight,
        cotangent[0],
        down_weight,
    )
    (
        w_qk, w_vg, w_gate, w_up, w_down, normed, grad_result, second, act_gate, act_up, hidden,
        raw_qk, raw_vg, queries, keys, values, gate, attended, gated, log_totals, w_out, hidden_in,
    ) = seq.run(
        250.0,
        lambda t, g, *items: forward(
            seq_lengths, t, (gain_one, gain_two, q_gain, k_gain), tables, g, items, n_dp, n_u, heads, kv_heads
        ),
        tokens[0], grad_own, out_item, qk_item, vg_item, gate_item, up_item, down_item,
    )
    normed, grad_result = normed.reshape(bucket, width), grad_result.reshape(bucket, width)
    second, gated = second.reshape(bucket, width), gated.reshape(bucket, q_w)

    def even_odd(value):
        value = low(value).reshape(n_u, rows, width)
        return (value[0::2], value[1::2])

    act_gate, act_up, hidden = (v.reshape(bucket, ff_local) for v in (act_gate, act_up, hidden))
    down_own = lax.psum_scatter(
        seq.run(10.7, lambda h, g: outer_terms(h, g, 6), hidden, grad_result), "dp", scatter_dimension=0, tiled=True
    )

    grad_gate, grad_up = seq.run(15.5, down_back, grad_result, act_gate, act_up, w_down)

    def input_grads(a, b, first, second):
        return back_matmul(a, b, first, second, rows)

    two_keep, two_send = seq.run(20.5, input_grads, grad_gate, grad_up, w_gate, w_up)
    t_two = task(cube.reduce(two_keep, two_send))
    seq.idle(t_two.next())
    up_own = lax.psum_scatter(
        seq.run(12.5, lambda a, b: outer_terms(a, b, n_dp), second, grad_up), "dp", scatter_dimension=0, tiled=True
    )
    down_keep, down_send = seq.run(11.5, lambda h, w: even_odd(dot(h, w)), hidden, w_down)
    grad_hidden_in, branch_own, gain_two_own = seq.run(
        5.8, lambda *a: norm_back(*a, True), hidden_in, *t_two.finish(), grad_own, gain_two
    )
    t_branch_grad = task(cube.gather(branch_own))
    gate_terms = seq.run(12.5, lambda a, b: outer_terms(a, b, n_dp), second, grad_gate)
    branch_grad = cube.joined(t_branch_grad.finish()).reshape(bucket, width)

    grad_gated = seq.run(3.8, dot_nt, branch_grad, w_out)
    t_down = task(cube.reduce(down_keep, down_send))
    t_down_all = task(cube.gather(seq.tie(down_own)[0]))
    grad_qk, grad_vg, gain_query_own, gain_key_own = seq.run(
        20.0,
        attend_back,
        place, raw_qk, queries, keys, values, gate, attended, grad_gated.reshape(n_u, rows, q_w), log_totals,
        q_gain, k_gain, *tables,
    )
    grad_qk, grad_vg = grad_qk.reshape(bucket, -1), grad_vg.reshape(bucket, -1)
    one_keep, one_send = seq.run(12.0, input_grads, grad_qk, grad_vg, w_qk, w_vg)
    t_one = task(cube.reduce(one_keep, one_send))
    out_parts = seq.run(7.0, lambda p, a, b: out_terms(p, a, b, n_u), place, gated, branch_grad, take=False)
    qk_terms = seq.run(9.3, lambda a, b: outer_terms(a, b, n_dp), normed, grad_qk, take=False)
    vg_terms = seq.run(9.3, lambda a, b: outer_terms(a, b, n_dp), normed, grad_vg)

    gate_all, qk_all, vg_all, out_all = seq.run(
        150.0, lambda b, *t: reduce_all(b, t, n_dp, n_u), out_parts, gate_terms, qk_terms, vg_terms, take=False
    )
    t_up_all = task(cube.gather(seq.tie(up_own)[0]))
    tokens_grad, gain_one_own = seq.run(
        5.6, lambda *a: norm_back(*a, False), tokens[0], *t_one.finish(), grad_hidden_in, gain_one
    )
    gains = seq.run(
        1.0, lambda *g: jnp.concatenate(g, axis=1)[0], gain_one_own, gain_query_own, gain_key_own, gain_two_own
    )
    t_gains = task(cube.total(gains, ("ulysses", "dp")))
    keys_all = [list(range(n_u))]
    in_all = seq.run(
        5.5,
        lambda p, a, b: put_columns(
            p, [(keys_all, [a]), (keys_all, [b])], [[(0, q_w), (q_w, kv_w)], [(0, kv_w), (kv_w, q_w)]]
        ),
        place, qk_all, vg_all,
    )
    out_all = seq.run(4.0, lambda p, a: put_columns(p, [(keys_all, [a])], [[(0, out_cols)]]), place, out_all)
    down_held = t_down_all.finish()
    down_all = seq.run(5.3, lambda p, *b: put_rows(p, (down_held[0], b)), place, *down_held[1])
    up_held = t_up_all.finish()
    mlp_all = seq.run(
        10.0, lambda p, a, *b: put_strips(p, [(keys_all, [a]), (up_held[0], b)], n_dp, ff_strip), place, gate_all, *up_held[1]
    )
    layer_out = seq.run(2.2, lambda a, b, c: a + high(b) + high(c), hidden_in, *t_down.finish())
    gains = t_gains.finish()

    gain_one_sum = gains[:width]
    gain_query_sum = gains[width : width + head_width]
    gain_key_sum = gains[width + head_width : width + 2 * head_width]
    gain_two_sum = gains[width + 2 * head_width :]
    return (
        layer_out[None],
        tokens_grad[None],
        gain_one_sum,
        in_all,
        gain_query_sum,
        gain_key_sum,
        out_all,
        gain_two_sum,
        mlp_all,
        down_all,
    )


def solution(mesh):
    placed = (
        P("dp", "ulysses", None),
        P("dp"),
        P("dp", "ulysses", None),
        P(),
        P("dp", None),
        P(),
        P(),
        P("dp", None),
        P(),
        P("dp", None),
        P("dp", None),
    )
    return jax.shard_map(
        shards,
        mesh=mesh,
        in_specs=placed,
        out_specs=(
            P("dp", "ulysses", None),
            P("dp", "ulysses", None),
            P(),
            P("dp", None),
            P(),
            P(),
            P("dp", None),
            P(),
            P("dp", None),
            P("dp", None),
        ),
        check_vma=False,
    )
```

```python
import functools

import jax
import jax.numpy as jnp
import numpy as np
from jax import lax
from jax.experimental import pallas as pl
from jax.experimental.pallas import tpu as pltpu
from jax.sharding import PartitionSpec as P

QUERY_HEADS = 16
KEY_VALUE_HEADS = 8
HEAD_DIMENSION = 128
FF = 6144


EPSILON = 1e-06
ROPE_BASE = 1000000.0
MASKED = -1e30


def rms_scale(values):
    return lax.rsqrt(jnp.mean(values * values, axis=-1, keepdims=True) + EPSILON)


VMEM_LIMIT = 56 * 1024 * 1024
NT = (((1,), (1,)), ((), ()))
TN = (((0,), (0,)), ((), ()))


def params():
    return pltpu.CompilerParams(vmem_limit_bytes=VMEM_LIMIT)


def cost(*_):
    return pl.CostEstimate(flops=1, bytes_accessed=1, transcendentals=0)


def steady(shape):
    return pl.BlockSpec(shape, lambda *_: (0,) * len(shape), pipeline_mode=pl.Buffered(1))


def tile_of(size):
    return 256 if size % 256 == 0 else 128


def head_scale(raw):
    return lax.rsqrt(jnp.mean(raw * raw, axis=-1, keepdims=True) + EPSILON)


def turn_pairs(value, cosine, sine):
    return value * cosine + pltpu.roll(value, HEAD_DIMENSION // 2, 1) * sine


def masked_scores(q, k, first_row, length):
    scores = lax.dot_general(q, k, NT, preferred_element_type=jnp.float32)
    scores = scores * HEAD_DIMENSION ** (-0.5)
    row = first_row + lax.broadcasted_iota(jnp.int32, scores.shape, 0)
    column = lax.broadcasted_iota(jnp.int32, scores.shape, 1)
    return jnp.where((column <= row) & (column < length), scores, MASKED)


def in_order(ref, me):
    return jnp.concatenate([ref[me ^ t] for t in range(ref.shape[0])], axis=0)


def attend_back_kernel(
    block, copies, heads, kv_heads, place_ref, q_raw, k_raw, q_ref, k_ref, v_ref, gate_ref, attended_ref, up_ref,
    total_ref, q_gain, k_gain, cosine, sine, qk_out, vg_out, q_gain_out, k_gain_out, grad_ref, dq_ref, dk_ref, dv_ref,
):
    group = pl.program_id(0)
    bucket, size = k_ref.shape
    n_u, rows_own, _ = q_raw.shape
    scale = size ** (-0.5)
    length, me = place_ref[0], place_ref[1]

    @pl.when(group == 0)
    def _():
        q_gain_out[...] = jnp.zeros_like(q_gain_out)
        k_gain_out[...] = jnp.zeros_like(k_gain_out)

    def store(out, at, width, value):
        for t in range(n_u):
            out[me ^ t, :, pl.ds(pl.multiple_of(at, size), width)] = value[t * rows_own : (t + 1) * rows_own]

    up, gate = in_order(up_ref, me), gate_ref[...]
    grad_ref[...] = (up * gate).astype(jnp.bfloat16)
    grad_gate = (up * attended_ref[...].astype(jnp.float32) * gate * (1.0 - gate)).astype(jnp.bfloat16)
    store(vg_out, (kv_heads + group * copies) * size, copies * size, grad_gate)
    dk_ref[...] = jnp.zeros_like(dk_ref)
    dv_ref[...] = jnp.zeros_like(dv_ref)

    def norm_grad(raw, gain, upstream, gain_out):
        factor = head_scale(raw)
        weighted = upstream * gain
        inner = jnp.mean(weighted * raw, axis=-1, keepdims=True)
        gain_out[...] += jnp.sum(upstream * raw * factor, axis=0, keepdims=True)
        return (factor * weighted - raw * (factor * factor * factor) * inner).astype(jnp.bfloat16)

    raw_q = in_order(q_raw, me)
    for copy in range(copies):
        columns = slice(copy * size, (copy + 1) * size)
        for first in range(0, bucket, block):
            rows = slice(first, first + block)
            reach = slice(0, first + block)
            q, g = q_ref[rows, columns], grad_ref[rows, columns]
            soft = jnp.exp(masked_scores(q, k_ref[reach], first, length) - total_ref[copy, rows])
            soft_grad = lax.dot_general(g, v_ref[reach], NT, preferred_element_type=jnp.float32)
            inner = jnp.sum(soft * soft_grad, axis=-1, keepdims=True)
            score_grad = (soft * (soft_grad - inner)).astype(jnp.bfloat16)
            dq_ref[rows] = jnp.dot(score_grad, k_ref[reach], preferred_element_type=jnp.float32) * scale
            dk_ref[reach] += lax.dot_general(score_grad, q, TN, preferred_element_type=jnp.float32)
            dv_ref[reach] += lax.dot_general(soft.astype(jnp.bfloat16), g, TN, preferred_element_type=jnp.float32)
        plain = turn_pairs(dq_ref[...].astype(jnp.bfloat16).astype(jnp.float32), cosine[...], -sine[...])
        store(qk_out, (group * copies + copy) * size, size, norm_grad(raw_q[:, columns], q_gain[...], plain, q_gain_out))
    plain = turn_pairs((dk_ref[...] * scale).astype(jnp.bfloat16).astype(jnp.float32), cosine[...], -sine[...])
    store(qk_out, (heads + group) * size, size, norm_grad(in_order(k_raw, me), k_gain[...], plain, k_gain_out))
    store(vg_out, group * size, size, dv_ref[...].astype(jnp.bfloat16))


def attend_back(place, raw_qk, q, k, v, gate, attended, upstream, totals, q_gain, k_gain, cosine, sine):
    size = HEAD_DIMENSION
    n_u, rows_own, _ = raw_qk.shape
    bucket = n_u * rows_own
    heads, kv_heads = q.shape[1] // size, k.shape[1] // size
    copies = heads // kv_heads

    def blocks(width, start):
        return pl.BlockSpec((n_u, rows_own, width), lambda g: (0, 0, start + g))

    wide = pl.BlockSpec((bucket, copies * size), lambda g: (0, g))
    slim = pl.BlockSpec((bucket, size), lambda g: (0, g))
    total = (heads + kv_heads) * size
    whole = pl.BlockSpec((n_u, rows_own, total), lambda g: (0, 0, 0))
    gain = pl.BlockSpec((1, size), lambda g: (0, 0))
    return pl.pallas_call(
        functools.partial(attend_back_kernel, min(256, bucket), copies, heads, kv_heads),
        grid=(kv_heads,),
        in_specs=[
            pl.BlockSpec(memory_space=pltpu.SMEM),
            blocks(copies * size, 0),
            blocks(size, heads),
            wide,
            slim,
            slim,
            wide,
            wide,
            blocks(copies * size, 0),
            pl.BlockSpec((copies, bucket, 1), lambda g: (g, 0, 0)),
            steady((1, size)),
            steady((1, size)),
            steady((bucket, size)),
            steady((bucket, size)),
        ],
        out_specs=[whole, whole, gain, gain],
        out_shape=[
            jax.ShapeDtypeStruct((n_u, rows_own, total), jnp.bfloat16),
            jax.ShapeDtypeStruct((n_u, rows_own, total), jnp.bfloat16),
            jax.ShapeDtypeStruct((1, size), jnp.float32),
            jax.ShapeDtypeStruct((1, size), jnp.float32),
        ],
        scratch_shapes=[
            pltpu.VMEM((bucket, copies * size), jnp.bfloat16),
            pltpu.VMEM((bucket, size), jnp.float32),
            pltpu.VMEM((bucket, size), jnp.float32),
            pltpu.VMEM((bucket, size), jnp.float32),
        ],
        compiler_params=params(),
        cost_estimate=cost(5 * heads * bucket * bucket * size, 24 * bucket * heads * size, heads * bucket * bucket // 2),
        name="attention_back",
    )(place, raw_qk, raw_qk, q, k, v, gate, attended, upstream, totals, q_gain, k_gain, cosine, sine)


def back_matmul(a, b, first, second, rows):
    m, n = a.shape
    width = first.shape[0]
    part = 512
    pairs = m // rows // 2

    def kernel(a_ref, b_ref, first_ref, second_ref, keep_ref, send_ref):
        for pair in range(pairs):
            at = slice(2 * pair * rows, (2 * pair + 2) * rows)
            out = lax.dot_general(a_ref[at], first_ref[...], NT, preferred_element_type=jnp.float32)
            out += lax.dot_general(b_ref[at], second_ref[...], NT, preferred_element_type=jnp.float32)
            out = out.astype(jnp.bfloat16)
            keep_ref[pair] = out[:rows]
            send_ref[pair] = out[rows:]

    weight = pl.BlockSpec((part, n), lambda i: (i, 0))
    out = pl.BlockSpec((pairs, rows, part), lambda i: (0, 0, i))
    shape = jax.ShapeDtypeStruct((pairs, rows, width), jnp.bfloat16)
    return pl.pallas_call(
        kernel,
        grid=(width // part,),
        in_specs=[steady((m, n)), steady((m, n)), weight, weight],
        out_specs=[out, out],
        out_shape=[shape, shape],
        compiler_params=params(),
        cost_estimate=cost(),
        name="back_matmul",
    )(a, b, first, second)


def outer_terms(x, y, count):
    m, width = x.shape
    n = y.shape[1]
    count = count // 2
    depth = width // count

    def kernel(x_ref, y_ref, out_ref):
        out_ref[...] = lax.dot_general(x_ref[...], y_ref[...], TN, preferred_element_type=jnp.float32).astype(jnp.bfloat16)

    return pl.pallas_call(
        kernel,
        grid=(count,),
        in_specs=[pl.BlockSpec((m, depth), lambda k: (0, k)), steady((m, n))],
        out_specs=pl.BlockSpec((depth, n), lambda k: (k, 0)),
        out_shape=jax.ShapeDtypeStruct((width, n), jnp.bfloat16),
        compiler_params=params(),
        cost_estimate=cost(2 * m * n * width, 2 * m * width + 2 * m * n + 2 * n * width),
        name="outer_terms",
    )(x, y)


def down_back(upstream, a, b, weight):
    m, width = upstream.shape
    n = a.shape[1]
    tile = tile_of(n)
    rows = min(512, m)

    def kernel(up_ref, a_ref, b_ref, weight_ref, gate_out, up_out):
        for at in range(0, m, rows):
            where = slice(at, at + rows)
            grad = lax.dot_general(up_ref[where], weight_ref[...], NT, preferred_element_type=jnp.float32)
            a, b = a_ref[where], b_ref[where]
            sig = jax.nn.sigmoid(a)
            gate_out[where] = (grad * b * sig * (1.0 + a * (1.0 - sig))).astype(jnp.bfloat16)
            up_out[where] = (grad * a * sig).astype(jnp.bfloat16)

    step = pl.BlockSpec((m, tile), lambda i: (0, i))
    shape = jax.ShapeDtypeStruct((m, n), jnp.bfloat16)
    return pl.pallas_call(
        kernel,
        grid=(n // tile,),
        in_specs=[steady((m, width)), step, step, pl.BlockSpec((tile, width), lambda i: (i, 0))],
        out_specs=[step, step],
        out_shape=[shape, shape],
        compiler_params=params(),
        cost_estimate=cost(),
        name="down_back",
    )(upstream, a, b, weight)


def strips_kernel(n_dp, n_u, strip, place_ref, w_ref, gate_ref, up_ref):
    for t in range(n_u):

        @pl.when(place_ref[1] == t)
        def _():
            for half, out in enumerate((gate_ref, up_ref)):
                starts = [((half * n_dp + b) * n_u + t) * strip for b in range(n_dp)]
                out[...] = jnp.concatenate([w_ref[:, s : s + strip] for s in starts], axis=1)


def take_strips(place, w, n_dp, n_u, strip):
    depth, total = w.shape
    rows = 64
    out = pl.BlockSpec((rows, n_dp * strip), lambda i: (i, 0))
    shape = jax.ShapeDtypeStruct((depth, n_dp * strip), w.dtype)
    return pl.pallas_call(
        functools.partial(strips_kernel, n_dp, n_u, strip),
        grid=(depth // rows,),
        in_specs=[pl.BlockSpec(memory_space=pltpu.SMEM), pl.BlockSpec((rows, total), lambda i: (i, 0))],
        out_specs=[out, out],
        out_shape=[shape, shape],
        compiler_params=params(),
        cost_estimate=cost(0, 2 * depth * total + 4 * depth * n_dp * strip),
        name="take_strips",
    )(place, w)


def fill(scratch, keys, refs):
    for key_list, ref in zip(keys, refs):
        for at, key in enumerate(key_list):
            scratch[key] = ref[at]


def put_call(kernel, place, helds, grid, blocks, at, out_block, out_at, out_shape, name):
    n_u = sum(len(k) for k in helds[0][0])
    count = sum(len(b) for _, b in helds)

    def body(place_ref, *refs):
        refs = list(refs)
        scratches = refs[count + 1 :]
        for (keys, _), scratch in zip(helds, scratches):
            fill(scratch, keys, [refs.pop(0) for _ in keys])
        kernel(place_ref[1], scratches, refs[0])

    return pl.pallas_call(
        body,
        grid=(grid,),
        in_specs=[pl.BlockSpec(memory_space=pltpu.SMEM)]
        + [pl.BlockSpec((len(k),) + block, at) for (keys, _), block in zip(helds, blocks) for k in keys],
        out_specs=pl.BlockSpec(out_block, out_at),
        out_shape=jax.ShapeDtypeStruct(out_shape, jnp.float32),
        scratch_shapes=[pltpu.VMEM((n_u,) + block, jnp.bfloat16) for block in blocks],
        compiler_params=params(),
        cost_estimate=cost(0, 6 * out_shape[0] * out_shape[1]),
        name=name,
    )(place, *[v for _, held in helds for v in held])


def put_strips(place, helds, n_dp, strip):
    n_u = sum(len(k) for k in helds[0][0])
    depth, width = helds[0][1][0].shape[1:]
    rows = min(32, depth)

    def kernel(me, scratches, out_ref):
        size = n_u * strip
        for h, scratch in enumerate(scratches):
            parts = [scratch[me ^ t].astype(jnp.float32) for t in range(n_u)]
            for b in range(n_dp):
                at = (h * n_dp + b) * size
                out_ref[:, at : at + size] = jnp.concatenate(
                    [p[:, b * strip : (b + 1) * strip] for p in parts], axis=1
                )

    total = len(helds) * n_u * width
    return put_call(
        kernel, place, helds, depth // rows, [(rows, width)] * len(helds), lambda i: (0, i, 0),
        (rows, total), lambda i: (i, 0), (depth, total), "put_strips",
    )


def put_columns(place, helds, sections):
    n_u = sum(len(k) for k in helds[0][0])
    depth = helds[0][1][0].shape[1]
    rows = min(64, depth)

    def kernel(me, scratches, out_ref):
        at = 0
        for scratch, parts in zip(scratches, sections):
            for start, size in parts:
                for t in range(n_u):
                    out_ref[:, at : at + size] = scratch[me ^ t, :, start : start + size].astype(jnp.float32)
                    at += size

    total = n_u * sum(size for parts in sections for _, size in parts)
    return put_call(
        kernel, place, helds, depth // rows, [(rows, held[0].shape[2]) for _, held in helds], lambda i: (0, i, 0),
        (rows, total), lambda i: (i, 0), (depth, total), "put_columns",
    )


def put_rows(place, held):
    n_u = sum(len(k) for k in held[0])
    depth, width = held[1][0].shape[1:]
    tile = 512

    def kernel(me, scratches, out_ref):
        for t in range(n_u):
            out_ref[t * depth : (t + 1) * depth] = scratches[0][me ^ t].astype(jnp.float32)

    return put_call(
        kernel, place, [held], width // tile, [(depth, tile)], lambda i: (0, 0, i),
        (n_u * depth, tile), lambda i: (0, i), (n_u * depth, width), "put_rows",
    )


def norm_call(kernel, inputs, gain, outs, gain_sum, name):
    r, width = inputs[0].shape
    tile = min(64, r)
    step = pl.BlockSpec((tile, width), lambda i: (i, 0))
    one = pl.BlockSpec((1, width), lambda i: (0, 0))
    shapes = [jax.ShapeDtypeStruct((r, width), o) for o in outs]
    if gain_sum:
        shapes.append(jax.ShapeDtypeStruct((1, width), jnp.float32))
    return pl.pallas_call(
        kernel,
        grid=(r // tile,),
        in_specs=[step] * len(inputs) + [one],
        out_specs=[step] * len(outs) + [one] * gain_sum,
        out_shape=shapes,
        compiler_params=params(),
        cost_estimate=cost(0, sum(4 * v.size for v in inputs)),
        name=name,
    )(*inputs, gain)


def norm_back(source, keep, got, residual, gain, rounded):
    def kernel(source_ref, keep_ref, got_ref, residual_ref, gain_ref, *outs):
        @pl.when(pl.program_id(0) == 0)
        def _():
            outs[-1][...] = jnp.zeros_like(outs[-1])

        up = keep_ref[...] + got_ref[...].astype(jnp.float32)
        source = source_ref[...].astype(jnp.float32)
        factor = head_scale(source)
        weighted = up * gain_ref[...]
        inner = jnp.mean(weighted * source, axis=-1, keepdims=True)
        total = residual_ref[...].astype(jnp.float32) + factor * weighted
        total = total - source * (factor * factor * factor) * inner
        outs[0][...] = total
        if rounded:
            outs[1][...] = total.astype(jnp.bfloat16)
        outs[-1][...] += jnp.sum(up * source * factor, axis=0, keepdims=True)

    outs = [jnp.float32] + [jnp.bfloat16] * rounded
    return norm_call(kernel, (source, keep, got, residual), gain, outs, 1, "norm_back")


def halve(keep, got):
    pairs, (r, c) = keep.shape[0] // 2, keep.shape[1:]
    tile = min(64, r)

    def kernel(keep_ref, got_ref, even_ref, odd_ref):
        even_ref[0] = keep_ref[0].astype(jnp.float32) + got_ref[0].astype(jnp.float32)
        odd_ref[0] = (keep_ref[1].astype(jnp.float32) + got_ref[1].astype(jnp.float32)).astype(jnp.bfloat16)

    two = pl.BlockSpec((2, tile, c), lambda p, i: (p, i, 0))
    one = pl.BlockSpec((1, tile, c), lambda p, i: (p, i, 0))
    return pl.pallas_call(
        kernel,
        grid=(pairs, r // tile),
        in_specs=[two, two],
        out_specs=[one, one],
        out_shape=[jax.ShapeDtypeStruct((pairs, r, c), jnp.float32), jax.ShapeDtypeStruct((pairs, r, c), jnp.bfloat16)],
        compiler_params=params(),
        cost_estimate=cost(0, 16 * pairs * r * c),
        name="halve",
    )(keep, got)


def out_terms(place, gated, upstream, n_u):
    m, q = gated.shape
    c = upstream.shape[1] // n_u

    def kernel(place_ref, x_ref, y_ref, out_ref):
        out_ref[0] = lax.dot_general(x_ref[...], y_ref[...], TN, preferred_element_type=jnp.float32).astype(jnp.bfloat16)

    return pl.pallas_call(
        kernel,
        grid_spec=pltpu.PrefetchScalarGridSpec(
            num_scalar_prefetch=1,
            grid=(n_u,),
            in_specs=[
                pl.BlockSpec((m, q), lambda k, p: (0, 0)),
                pl.BlockSpec((m, c), lambda k, p: (0, p[1] ^ k)),
            ],
            out_specs=pl.BlockSpec((1, q, c), lambda k, p: (k, 0, 0)),
        ),
        out_shape=jax.ShapeDtypeStruct((n_u, q, c), jnp.bfloat16),
        compiler_params=params(),
        cost_estimate=cost(2 * m * q * c * n_u, 2 * m * q + 4 * m * c * n_u),
        name="out_terms",
    )(place, gated, upstream)


MESH = pl.DeviceIdType.MESH


class Group:
    def __init__(self, n_dp, n_u):
        self.n_dp, self.n_u = n_dp, n_u
        index = lax.axis_index("dp")
        self.me = lax.axis_index("ulysses")
        odd = index % 2
        self.position = (1 - odd) * (index // 2) + odd * (n_dp - 1 - index // 2)
        self.next = (self.owner(1), self.owner(-1))
        self.bits = [1 << k for k in range(n_u.bit_length() - 1)]

    def owner(self, offset):
        place = (self.position + offset + self.n_dp) % self.n_dp
        late = place // (self.n_dp // 2)
        return (1 - late) * (2 * place) + late * (2 * (self.n_dp - 1 - place) + 1)

    def greet(self):
        barrier = pltpu.get_barrier_semaphore()
        for way in (0, 1):
            pl.semaphore_signal(barrier, inc=1, device_id={"dp": self.next[way]}, device_id_type=MESH)
        for other in range(1, self.n_u):
            pl.semaphore_signal(barrier, inc=1, device_id={"ulysses": self.me ^ other}, device_id_type=MESH)
        pl.semaphore_wait(barrier, 1 + self.n_u)

    def to_ring(self, way, source, target, send, recv):
        copy = pltpu.make_async_remote_copy(
            src_ref=source, dst_ref=target, send_sem=send, recv_sem=recv,
            device_id={"dp": self.next[way]}, device_id_type=MESH,
        )
        copy.start()
        return copy

    def to_cube(self, bit, source, target, send, recv):
        copy = pltpu.make_async_remote_copy(
            src_ref=source, dst_ref=target, send_sem=send, recv_sem=recv,
            device_id={"ulysses": self.me ^ bit}, device_id_type=MESH,
        )
        copy.start()
        return copy

    def reach(self, more_ahead):
        longer = self.n_dp // 2
        shorter = self.n_dp - 1 - longer
        return (longer, shorter) if more_ahead else (shorter, longer)


class Spread:
    def __init__(self, group, own, out, send, recv):
        self.group, self.own, self.out, self.send, self.recv = group, own, out, send, recv
        self.keys, self.levels, self.copies, self.used, self.waited = [0], group.bits[::-1], [], 0, 0

    def level(self):
        for copy in self.copies[self.waited :]:
            copy.wait_recv()
        self.waited = len(self.copies)
        if not self.levels:
            return False
        bit = self.levels.pop(0)
        for key in sorted(self.keys):
            source = self.own if key == 0 else self.out.at[key]
            at = self.used
            self.copies.append(
                self.group.to_cube(bit, source, self.out.at[key ^ bit], self.send.at[at], self.recv.at[at])
            )
            self.used += 1
        self.keys += [key ^ bit for key in self.keys]
        return True

    def finish(self):
        while self.level():
            pass
        for copy in self.copies:
            copy.wait_send()


class RingGather:
    def __init__(self, group, chains, send, recv):
        self.group, self.chains, self.send_sems, self.recv_sems = group, chains, send, recv
        self.copies = {}

    def place(self, c, owner):
        _, out, block, low, rows, _ = self.chains[c]
        return out.at[pl.ds(pl.multiple_of(owner * block + low, 16), rows)]

    def item(self, c):
        item, _, _, low, rows, _ = self.chains[c]
        return item.at[low : low + rows]

    def reach(self, c, way):
        return self.group.reach(self.chains[c][5])[way]

    def send(self, c, way, step):
        owner = self.group.owner(1 - step if way == 0 else step - 1)
        source = self.item(c) if step == 1 else self.place(c, owner)
        sems = (c, way, step - 1)
        self.copies[sems] = self.group.to_ring(
            way, source, self.place(c, owner), self.send_sems.at[sems], self.recv_sems.at[sems]
        )

    def start(self, c):
        for way in (0, 1):
            self.send(c, way, 1)

    def event(self, c, way, step):
        if step <= self.reach(c, way):
            self.copies[c, way, step - 1].wait_recv()
            if step < self.reach(c, way):
                self.send(c, way, step + 1)

    def finish(self):
        for copy in self.copies.values():
            copy.wait_send()


def by_rows(count, tile, function):
    def body(i, carry):
        function(pl.ds(pl.multiple_of(i * tile, tile), tile))
        return carry

    lax.fori_loop(0, count // tile, body, 0)


def forward_kernel(
    n_dp, n_u, heads, kv_heads, length_ref, tokens_ref, gain_one, gain_two, q_gain, k_gain, cosine, sine, grad_ref,
    out_item, qk_item, vg_item, gate_item, up_item, down_item,
    w_qk, w_vg, w_gate, w_up, w_down, normed_out, grad_out, second_out, act_gate, act_up, act_hidden,
    raw_qk, raw_vg, q_out, k_out, v_out, gate_out, attended_out, gated_out, total_out, w_out, hidden_out,
    normed, own, qk_local, vg_local, columns, turned, parts, core_got, total, second_own, gate_stage, up_stage, hidden_stage,
    ring_send, ring_recv, cube_send, cube_recv, turn_send, turn_recv, sum_send, sum_recv, local,
):
    rows_own, width = tokens_ref.shape
    bucket = rows_own * n_u
    size = HEAD_DIMENSION
    copies = heads // kv_heads
    depth = width // n_dp
    group = Group(n_dp, n_u)
    me, mine = group.me, group.owner(0)
    group.greet()
    strip = down_item.shape[0]
    halves = 2 if strip % 32 == 0 else 1
    chains = [
        (out_item, columns, depth, 0, depth, True),
        (qk_item, w_qk, depth, 0, depth, False),
        (vg_item, w_vg, depth, 0, depth, True),
        (gate_item, w_gate, depth, 0, depth, True),
        (up_item, w_up, depth, 0, depth, False),
    ]
    for p in range(halves):
        chains.append((down_item, w_down, strip, p * strip // halves, strip // halves, p == 0))
    ring = RingGather(group, chains, ring_send, ring_recv)
    kept = []

    def keep(source, target):
        copy = pltpu.make_async_copy(source, target, local.at[len(kept)])
        copy.start()
        kept.append(copy)
        return copy

    for c in (0, 1, 2):
        ring.start(c)
    own_rows = lambda out, block: out.at[pl.ds(pl.multiple_of(mine * block, 16), block)]
    for item, out, block in (
        (out_item, columns, depth), (qk_item, w_qk, depth), (vg_item, w_vg, depth),
        (gate_item, w_gate, depth), (up_item, w_up, depth), (down_item, w_down, strip),
    ):
        keep(item, own_rows(out, block))

    def first(rows):
        x = tokens_ref[rows].astype(jnp.float32)
        own[rows] = (x * head_scale(x) * gain_one[...]).astype(jnp.bfloat16)

    by_rows(rows_own, 64, first)
    keep(own, normed.at[0]).wait()
    keep(grad_ref, grad_out.at[0])
    spreads = [
        Spread(group, own, normed, cube_send.at[0], cube_recv.at[0]),
        Spread(group, grad_ref, grad_out, cube_send.at[1], cube_recv.at[1]),
    ]
    spreads[0].level()
    longest = n_dp // 2
    for step in range(1, longest + 1):
        for c in (0, 1, 2):
            for way in (0, 1):
                ring.event(c, way, step)
        if step == 1:
            spreads[1].level()
        if step < longest:
            spreads[0 if step % 2 == 1 else 1].level()
        if step == longest - 1:
            for c in (3, 4):
                ring.start(c)
    spreads[0].finish()
    events = []
    for step in range(1, longest + 1):
        events += [[(3, 0, step), (4, 1, step)], [(4, 0, step), (3, 1, step)]]
        if step == longest - 1:
            events.append([("start",)])
    for step in range(1, longest + 1):
        if halves == 2:
            events += [[(5, 0, step), (6, 1, step)], [(6, 0, step), (5, 1, step)]]
        else:
            events += [[(5, 0, step), (5, 1, step)]]

    def pump(count=1):
        while count and events:
            pair = events.pop(0)
            if pair[0][0] == "start":
                for c in range(5, len(chains)):
                    ring.start(c)
                continue
            for event in pair:
                ring.event(*event)
            count -= 1

    for copy in kept[:3]:
        copy.wait()
    share = depth * n_dp // n_u
    turns = []
    for k in range(1, n_u):
        source = columns.at[pl.ds(pl.multiple_of((me ^ k) * share, 16), share)]
        turns.append(group.to_cube(k, source, turned.at[k], turn_send.at[k - 1], turn_recv.at[k - 1]))
    keep(columns.at[pl.ds(pl.multiple_of(me * share, 16), share)], turned.at[0]).wait()
    one, two = keep(w_qk, qk_local), keep(w_vg, vg_local)
    normed_copy = keep(normed, normed_out)
    one.wait()
    two.wait()

    def project(b, carry):
        x = normed[b]
        raw_qk[b] = jnp.dot(x, qk_local[...], preferred_element_type=jnp.float32)
        raw_vg[b] = jnp.dot(x, vg_local[...], preferred_element_type=jnp.float32)
        return carry

    lax.fori_loop(0, n_u, project, 0)
    normed_copy.wait()
    pump()

    length = length_ref[0]
    block = min(256, bucket)

    def attention(h, carry):
        def column(ref, at):
            at = pl.multiple_of(at * size, size)
            return jnp.concatenate([ref[me ^ t, :, pl.ds(at, size)] for t in range(n_u)], axis=0)

        at = pl.ds(pl.multiple_of(h * size, size), size)
        kv = pl.ds(pl.multiple_of(h // copies * size, size), size)
        q = column(raw_qk, h)
        q = turn_pairs(q * head_scale(q) * q_gain[...], cosine[...], sine[...]).astype(jnp.bfloat16)
        q_out[:, at] = q
        k = column(raw_qk, heads + h // copies)
        k = turn_pairs(k * head_scale(k) * k_gain[...], cosine[...], sine[...]).astype(jnp.bfloat16)
        k_out[:, kv] = k
        v = column(raw_vg, h // copies).astype(jnp.bfloat16)
        v_out[:, kv] = v
        gate = jax.nn.sigmoid(column(raw_vg, kv_heads + h))
        gate_out[:, at] = gate
        for start in range(0, bucket, block):
            rows = slice(start, start + block)
            scores = masked_scores(q[rows], k[: start + block], start, length)
            top = jnp.max(scores, axis=-1, keepdims=True)
            soft = jnp.exp(scores - top)
            sums = jnp.sum(soft, axis=-1, keepdims=True)
            out = jnp.dot(soft.astype(jnp.bfloat16), v[: start + block], preferred_element_type=jnp.float32) / sums
            out = out.astype(jnp.bfloat16)
            attended_out[rows, at] = out
            total_out[h, rows] = top + jnp.log(sums)
            gated = (out.astype(jnp.float32) * gate[rows]).astype(jnp.bfloat16)
            for t in range(start // rows_own, (start + block) // rows_own):
                inside = slice(t * rows_own - start, (t + 1) * rows_own - start)
                gated_out[me ^ t, :, at] = gated[inside]
        return carry

    lax.fori_loop(0, heads, attention, 0)
    pump()
    for copy in turns:
        copy.wait_recv()
    c_width = columns.shape[1]
    for k in range(n_u):
        w_out[:, pl.ds(pl.multiple_of((me ^ k) * c_width, c_width), c_width)] = turned[k]

    def branch(b, carry):
        parts[b] = jnp.dot(gated_out[b], w_out[...], preferred_element_type=jnp.float32).astype(jnp.bfloat16)
        return carry

    lax.fori_loop(0, n_u, branch, 0)
    held = list(range(n_u))
    used = 0
    sums = []
    for bit in group.bits:
        keys = [key for key in held if not key & bit]
        level = []
        for key in keys:
            level.append(
                group.to_cube(bit, parts.at[key | bit], core_got.at[used], sum_send.at[used], sum_recv.at[used])
            )
            used += 1
        sums += level
        pump()
        for at, (key, copy) in enumerate(zip(keys, level)):
            copy.wait_recv()
            slot = used - len(keys) + at

            def add(rows, key=key, slot=slot):
                got = core_got[slot, rows].astype(jnp.float32)
                if key:
                    parts[key, rows] = (parts[key, rows].astype(jnp.float32) + got).astype(jnp.bfloat16)
                elif bit == 1:
                    total[rows] = tokens_ref[rows].astype(jnp.float32) + parts[0, rows].astype(jnp.float32) + got
                else:
                    total[rows] = total[rows] + got

            by_rows(rows_own, 64, add)
        held = keys

    def second(rows):
        hidden = total[rows]
        hidden_out[rows] = hidden
        second_own[rows] = (hidden * head_scale(hidden) * gain_two[...]).astype(jnp.bfloat16)

    by_rows(rows_own, 64, second)
    spread = Spread(group, second_own, normed, cube_send.at[2], cube_recv.at[2])
    keep(second_own, normed.at[0])
    while spread.level():
        pump(2)
    kept[12].wait()
    second_copy = keep(normed, second_out)
    while events and events[0][0][0] in ("start", 3, 4):
        pump(1)
    for copy in kept[3:5]:
        copy.wait()
    n = qk_local.shape[1]
    for part in range(w_gate.shape[1] // n):
        where = slice(part * n, (part + 1) * n)
        at = 14 + 5 * part
        loads = [
            pltpu.make_async_copy(w_gate.at[:, where], qk_local, local.at[at]),
            pltpu.make_async_copy(w_up.at[:, where], vg_local, local.at[at + 1]),
        ]
        for copy in loads:
            copy.start()
        for copy in loads:
            copy.wait()

        def expand(b, carry):
            x = normed[b]
            one = jnp.dot(x, qk_local[...], preferred_element_type=jnp.float32)
            two = jnp.dot(x, vg_local[...], preferred_element_type=jnp.float32)
            gate_stage[b] = one
            up_stage[b] = two
            hidden_stage[b] = (one * jax.nn.sigmoid(one) * two).astype(jnp.bfloat16)
            return carry

        lax.fori_loop(0, n_u, expand, 0)
        stores = []
        for k, (stage, out) in enumerate(((gate_stage, act_gate), (up_stage, act_up), (hidden_stage, act_hidden))):
            copy = pltpu.make_async_copy(stage, out.at[:, :, where], local.at[at + 2 + k])
            copy.start()
            stores.append(copy)
        pump(2)
        for copy in stores:
            copy.wait()
    second_copy.wait()
    spreads[1].finish()
    spread.finish()
    pump(1000)
    ring.finish()
    for copy in turns + sums:
        copy.wait_send()
    for copy in kept[5:6] + kept[7:8]:
        copy.wait()


def forward(length, tokens_own, gains, tables, grad_own, items, n_dp, n_u, heads, kv_heads):
    anywhere = pl.BlockSpec(memory_space=pl.ANY)
    local = pl.BlockSpec(memory_space=pltpu.VMEM)
    rows, width = tokens_own.shape
    bucket, size = rows * n_u, HEAD_DIMENSION
    total = (heads + kv_heads) * size
    depth = width // n_dp
    columns = items[0].shape[1]
    share = width // n_u
    longest = n_dp // 2

    def shape(*dims, dtype=jnp.bfloat16):
        return jax.ShapeDtypeStruct(dims, dtype)

    out_shape = [shape(n_dp * i.shape[0], i.shape[1]) for i in items[1:]]
    out_shape += [shape(n_u, rows, width)] * 3
    hidden = items[4].shape[1]
    out_shape += [shape(n_u, rows, hidden, dtype=jnp.float32)] * 2 + [shape(n_u, rows, hidden)]
    out_shape += [shape(n_u, rows, total, dtype=jnp.float32)] * 2
    out_shape += [
        shape(bucket, heads * size), shape(bucket, kv_heads * size), shape(bucket, kv_heads * size),
        shape(bucket, heads * size, dtype=jnp.float32), shape(bucket, heads * size),
        shape(n_u, rows, heads * size), shape(heads, bucket, 1, dtype=jnp.float32),
        shape(share, width), shape(rows, width, dtype=jnp.float32),
    ]
    dma = pltpu.SemaphoreType.DMA
    return pl.pallas_call(
        functools.partial(forward_kernel, n_dp, n_u, heads, kv_heads),
        in_specs=[pl.BlockSpec(memory_space=pltpu.SMEM)] + [local] * 7 + [anywhere] * 7,
        out_specs=[anywhere] * 11 + [local] * 11,
        out_shape=out_shape,
        scratch_shapes=[
            pltpu.VMEM((n_u, rows, width), jnp.bfloat16),
            pltpu.VMEM((rows, width), jnp.bfloat16),
            pltpu.VMEM((width, total), jnp.bfloat16),
            pltpu.VMEM((width, total), jnp.bfloat16),
            pltpu.VMEM((width, columns), jnp.bfloat16),
            pltpu.VMEM((n_u, share, columns), jnp.bfloat16),
            pltpu.VMEM((n_u, rows, width), jnp.bfloat16),
            pltpu.VMEM((n_u - 1, rows, width), jnp.bfloat16),
            pltpu.VMEM((rows, width), jnp.float32),
            pltpu.VMEM((rows, width), jnp.bfloat16),
            pltpu.VMEM((n_u, rows, total), jnp.float32),
            pltpu.VMEM((n_u, rows, total), jnp.float32),
            pltpu.VMEM((n_u, rows, total), jnp.bfloat16),
            dma((7, 2, longest)), dma((7, 2, longest)), dma((3, n_u - 1)), dma((3, n_u - 1)),
            dma((n_u - 1,)), dma((n_u - 1,)), dma((n_u - 1,)), dma((n_u - 1,)), dma((14 + 5 * (hidden // total),)),
        ],
        compiler_params=pltpu.CompilerParams(vmem_limit_bytes=60 * 1024 * 1024, collective_id=0, has_side_effects=True),
        cost_estimate=cost(),
        name="forward",
    )(length, tokens_own, *gains, *tables, grad_own, *items)


def reduce_kernel(n_dp, n_u, count, blocks_ref, *refs):
    given, outs = list(refs[: count - 1]), refs[count - 1 : 2 * count - 1]
    refs = refs[2 * count - 1 :]
    slots, sums, terms = refs[:count], refs[count : 2 * count], refs[2 * count : 3 * count]
    ring_send, ring_recv, cube_send, cube_recv, turn_send, turn_recv, local = refs[3 * count :]
    out_terms_ref = terms[-1]
    given.append(out_terms_ref)
    loads = {c: pltpu.make_async_copy(given[c], terms[c], local.at[count + 1 + c]) for c in range(count - 1)}
    group = Group(n_dp, n_u)
    group.greet()
    copies = {}
    reaches = [group.reach(c % 2 == 0) for c in range(count)]
    longest = n_dp // 2
    share = blocks_ref.shape[1]
    here = out_terms_ref.at[pl.ds(pl.multiple_of(group.me * share, share), share)]

    def add(c, target, offset, others):
        r = target.shape[0]
        tile = 16
        first = group.owner(offset) * r

        def body(i, carry):
            rows = pl.ds(pl.multiple_of(i * tile, tile), tile)
            total = terms[c][pl.ds(pl.multiple_of(first + i * tile, tile), tile)].astype(jnp.float32)
            for other in others:
                total = total + other[rows].astype(jnp.float32)
            target[rows] = total.astype(jnp.bfloat16)
            return carry

        lax.fori_loop(0, r // tile, body, 0)

    def slot(c, way, step):
        return slots[c].at[way, step]

    def send(c, way, step):
        reach = reaches[c][way]
        offset = (reach - step) if way == 0 else (step - reach)
        if step == 0:
            r = sums[c].shape[0]
            source = given[c].at[pl.ds(pl.multiple_of(group.owner(offset) * r, r), r)]
        else:
            if c in loads:
                loads.pop(c).wait()
            source = slot(c, way, step - 1)
            add(c, source, offset, [source])
        sems = (c, way, step)
        copies[sems] = group.to_ring(way, source, slot(c, way, step), ring_send.at[sems], ring_recv.at[sems])

    def start(chains):
        for c in chains:
            for way in (0, 1):
                send(c, way, 0)

    phases = [(0, 1), (2, 3)]
    start(phases[0])
    for copy in loads.values():
        copy.start()
    turns = []
    for k in range(1, n_u):
        turns.append(group.to_cube(k, blocks_ref.at[k], here, turn_send.at[k - 1], turn_recv.at[k - 1]))
    own = pltpu.make_async_copy(blocks_ref.at[0], here, local.at[count])
    own.start()
    own.wait()
    spreads, kept = [], []
    for phase, chains in enumerate(phases):
        for step in range(longest):
            for c in chains:
                for way in (0, 1):
                    if step < reaches[c][way]:
                        copies[c, way, step].wait_recv()
                        if step + 1 < reaches[c][way]:
                            send(c, way, step + 1)
            if step == longest - 2 and phase == 0:
                for copy in turns:
                    copy.wait_recv()
                start(phases[1])
            if phase == 1 and step % 2 == 1 and step < longest - 1:
                for spread in spreads:
                    spread.level()
            if step == longest - 1:
                for c in chains:
                    add(c, sums[c], 0, [slot(c, way, reaches[c][way] - 1) for way in (0, 1)])
                    spread = Spread(group, sums[c], outs[c], cube_send.at[c], cube_recv.at[c])
                    copy = pltpu.make_async_copy(sums[c], outs[c].at[0], local.at[c])
                    copy.start()
                    kept.append(copy)
                    spread.level()
                    spreads.append(spread)
    for spread in spreads:
        spread.level()
    for spread in spreads:
        spread.finish()
    for copy in list(copies.values()) + turns:
        copy.wait_send()
    for copy in kept:
        copy.wait()


def reduce_all(blocks, terms, n_dp, n_u):
    count = len(terms) + 1
    anywhere = pl.BlockSpec(memory_space=pl.ANY)
    local = pl.BlockSpec(memory_space=pltpu.VMEM)
    longest = n_dp // 2
    whole = (blocks.shape[0] * blocks.shape[1], blocks.shape[2])
    sizes = [(r // n_dp, c) for r, c in [t.shape for t in terms] + [whole]]
    dma = pltpu.SemaphoreType.DMA
    return pl.pallas_call(
        functools.partial(reduce_kernel, n_dp, n_u, count),
        in_specs=[anywhere] * count,
        out_specs=[anywhere] * count,
        out_shape=[jax.ShapeDtypeStruct((n_u,) + b, jnp.bfloat16) for b in sizes],
        scratch_shapes=[pltpu.VMEM((2, longest) + b, jnp.bfloat16) for b in sizes]
        + [pltpu.VMEM(b, jnp.bfloat16) for b in sizes]
        + [
            pltpu.VMEM(t.shape, jnp.bfloat16)
            for t in terms
        ]
        + [
            pltpu.VMEM(whole, jnp.bfloat16),
            dma((count, 2, longest)), dma((count, 2, longest)), dma((count, n_u - 1)), dma((count, n_u - 1)),
            dma((n_u - 1,)), dma((n_u - 1,)), dma((2 * count,)),
        ],
        compiler_params=pltpu.CompilerParams(vmem_limit_bytes=VMEM_LIMIT, collective_id=1, has_side_effects=True),
        cost_estimate=cost(),
        name="reduce_all",
    )(blocks, *terms)


START = 0.9
LATENCY = 6.0
RATES = {"ring": 50.0, "x": 50.0, "core": 250.0}


class Flight:
    def __init__(self, value, arrival):
        self.value, self.arrival = value, arrival


class Sequence:
    def __init__(self):
        self.last = ()
        self.now = 0.0
        self.free = {}
        self.sources = []
        self.fillers = []

    def tie(self, *values):
        tied, _ = lax.optimization_barrier((values, self.last))
        self.last = tied
        return tied

    def run(self, cost, function, *values, take=True):
        if take:
            self.poll()
        out = function(*self.tie(*values))
        self.now += cost
        if isinstance(out, (tuple, list)):
            return self.tie(*out)
        return self.tie(out)[0]

    def fly(self, value, axis, pairs, link, kind):
        (value,) = self.tie(value)
        got = lax.ppermute(value, axis, pairs)
        start = max(self.now + START, self.free.get(link, 0.0))
        end = start + value.size * value.dtype.itemsize / 1000.0 / RATES[kind]
        self.free[link] = end
        self.now += START
        return Flight(got, end + LATENCY)

    def land(self, *flights):
        self.idle(max(f.arrival for f in flights))
        return self.tie(*[f.value for f in flights])

    def poll(self):
        moved = True
        while moved:
            moved = any([source.poll(self.now) for source in self.sources])

    def later(self, cost, ready, function):
        self.fillers.append((cost, ready, function))

    def fill(self):
        for at, (cost, ready, function) in enumerate(self.fillers):
            if ready():
                self.fillers.pop(at)
                function()
                return True
        return False

    def idle(self, until):
        while True:
            self.poll()
            if self.now >= until:
                return
            if until - self.now > 2.0 and self.fill():
                continue
            events = [e for source in self.sources for e in [source.next()] if e is not None]
            self.now = max(self.now, min(events + [until]))

    def drain(self, done):
        while not done():
            self.poll()
            if done():
                return
            if self.fill():
                continue
            events = [e for source in self.sources for e in [source.next()] if e is not None]
            assert events
            self.now = max(self.now, min(events))


def pick(value, index):
    return lax.dynamic_index_in_dim(value, index, 0, keepdims=False, allow_negative_indices=False)


class Cube:
    def __init__(self, axis, seq):
        self.axis = axis
        self.seq = seq
        self.count = lax.axis_size(axis)
        self.me = lax.axis_index(axis)
        bits = []
        bit = 1
        while bit < self.count:
            bits.append(bit)
            bit *= 2
        self.bits = bits

    def swap(self, value, bit):
        kind = "core" if bit == 1 else "x"
        return self.seq.fly(value, self.axis, [(i, i ^ bit) for i in range(self.count)], kind, kind)

    def gather(self, item):
        keys, blocks = [[0]], [item[None]]
        for bit in self.bits[::-1]:
            order = sorted((key, at, sub) for at, ks in enumerate(keys) for sub, key in enumerate(ks))
            if len(order) > 1:
                sent = self.seq.run(
                    2.0, lambda *b: jnp.concatenate([b[at][sub : sub + 1] for _, at, sub in order]), *blocks
                )
            else:
                sent = blocks[0]
            (got,) = yield [self.swap(sent, bit)]
            keys = keys + [[key ^ bit for key, _, _ in order]]
            blocks = blocks + [got]
        return (keys, blocks)

    def joined(self, held):
        keys, blocks = held
        order = sorted((key, at, sub) for at, ks in enumerate(keys) for sub, key in enumerate(ks))
        return self.seq.run(3.0, lambda *b: jnp.concatenate([b[at][sub : sub + 1] for _, at, sub in order]), *blocks)

    def reduce(self, keep, send):
        for bit in self.bits:
            (got,) = yield [self.swap(send, bit)]
            if bit != self.bits[-1]:
                keep, send = self.seq.run(4.4, halve, keep, got)
        return (keep[0], got[0])

    def turn(self, blocks):
        got = yield [self.swap(blocks[bit], bit) for bit in range(1, self.count)]
        return [blocks[0]] + list(got)

    def total(self, value, axes):
        for axis in axes:
            count = lax.axis_size(axis)
            bit = 1
            while bit < count:
                pairs = [(i, i ^ bit) for i in range(count)]
                (got,) = yield [self.seq.fly(value, axis, pairs, "sum", "ring")]
                value = self.seq.run(1.0, lambda a, b: a + b, value, got)
                bit *= 2
        return value


class Task:
    def __init__(self, seq, generator, urgent=True):
        self.seq, self.generator = seq, generator
        self.value, self.flights, self.over, self.busy = None, None, False, False
        seq.sources.append(self)
        self.go(None)

    def go(self, values):
        self.busy = True
        try:
            self.flights = self.generator.send(values)
        except StopIteration as stop:
            self.value, self.over = stop.value, True
            self.seq.sources.remove(self)
        self.busy = False

    def next(self):
        return None if self.busy or self.over else max(f.arrival for f in self.flights)

    def poll(self, now):
        if self.busy or self.over or self.next() > now + 0.5:
            return False
        self.go(self.seq.tie(*[f.value for f in self.flights]))
        return True

    def finish(self):
        while not self.over:
            if self.busy:
                raise RuntimeError
            self.seq.idle(self.next())
        return self.value


def dot(a, b):
    return jnp.einsum("mk,kn->mn", a, b, preferred_element_type=jnp.float32)


def dot_nt(a, b):
    return jnp.einsum("mk,nk->mn", a, b, preferred_element_type=jnp.float32)


def dot_tn(a, b):
    return jnp.einsum("km,kn->mn", a, b, preferred_element_type=jnp.float32)


def low(value):
    return value.astype(jnp.bfloat16)


def high(value):
    return value.astype(jnp.float32)


def shards(
    tokens,
    seq_lengths,
    cotangent,
    norm1_gain,
    input_weight,
    query_gain,
    key_gain,
    output_weight,
    norm2_gain,
    perceptron_input_weight,
    down_weight,
):
    _, rows, width = tokens.shape
    seq = Sequence()
    cube = Cube("ulysses", seq)
    n_dp = lax.axis_size("dp")
    n_u, me = cube.count, cube.me
    bucket = rows * n_u
    depth = width // n_dp
    heads = QUERY_HEADS // n_u
    kv_heads = KEY_VALUE_HEADS // n_u
    copies = QUERY_HEADS // KEY_VALUE_HEADS
    head_width = HEAD_DIMENSION
    q_w, kv_w = heads * head_width, kv_heads * head_width
    query_width = QUERY_HEADS * head_width
    kv_all = KEY_VALUE_HEADS * head_width
    ff_strip = FF // n_dp // n_u
    ff_local = FF // n_u
    half = width // 2
    out_cols = width // n_u
    place = jnp.stack([seq_lengths[0], me])
    length = seq_lengths[0]
    q_gain, k_gain = query_gain[None], key_gain[None]
    gain_one, gain_two = norm1_gain[None], norm2_gain[None]
    positions = me * rows + jnp.arange(rows)
    def cut(value, start, size):
        return lax.dynamic_slice_in_dim(value, start, size, 1)

    def task(generator):
        return Task(seq, generator)

    frequency = np.float32(ROPE_BASE) ** (np.float32(-2.0) * np.arange(head_width // 2, dtype=np.float32) / head_width)
    angles = np.arange(bucket, dtype=np.float32)[:, None] * frequency.astype(np.float32)[None, :]
    cosine, sine = np.cos(angles), np.sin(angles)
    tables = (
        jnp.asarray(np.concatenate([cosine, cosine], axis=1), jnp.float32),
        jnp.asarray(np.concatenate([-sine, sine], axis=1), jnp.float32),
    )

    gate_item, up_item = seq.run(
        4.9, lambda p, w: take_strips(p, w, n_dp, n_u, ff_strip), place, perceptron_input_weight
    )
    out_item, qk_item, vg_item, grad_own, down_item = seq.run(
        3.0,
        lambda o, w, c, d: (
            cut(o, me * out_cols, out_cols),
            jnp.concatenate([cut(w, me * q_w, q_w), cut(w, query_width + me * kv_w, kv_w)], axis=1),
            jnp.concatenate(
                [
                    cut(w, query_width + kv_all + me * kv_w, kv_w),
                    cut(w, query_width + 2 * kv_all + me * q_w, q_w),
                ],
                axis=1,
            ),
            jnp.where((positions < length)[:, None], c, jnp.zeros_like(c)),
            lax.dynamic_slice_in_dim(d, me * ff_strip, ff_strip, 0),
        ),
        output_weight,
        input_weight,
        cotangent[0],
        down_weight,
    )
    (
        w_qk, w_vg, w_gate, w_up, w_down, normed, grad_result, second, act_gate, act_up, hidden,
        raw_qk, raw_vg, queries, keys, values, gate, attended, gated, log_totals, w_out, hidden_in,
    ) = seq.run(
        250.0,
        lambda t, g, *items: forward(
            seq_lengths, t, (gain_one, gain_two, q_gain, k_gain), tables, g, items, n_dp, n_u, heads, kv_heads
        ),
        tokens[0], grad_own, out_item, qk_item, vg_item, gate_item, up_item, down_item,
    )
    normed, grad_result = normed.reshape(bucket, width), grad_result.reshape(bucket, width)
    second, gated = second.reshape(bucket, width), gated.reshape(bucket, q_w)

    def even_odd(value):
        value = low(value).reshape(n_u, rows, width)
        return (value[0::2], value[1::2])

    act_gate, act_up, hidden = (v.reshape(bucket, ff_local) for v in (act_gate, act_up, hidden))
    down_own = lax.psum_scatter(
        seq.run(10.7, lambda h, g: outer_terms(h, g, 6), hidden, grad_result), "dp", scatter_dimension=0, tiled=True
    )

    grad_gate, grad_up = seq.run(15.5, down_back, grad_result, act_gate, act_up, w_down)

    def input_grads(a, b, first, second):
        return back_matmul(a, b, first, second, rows)

    two_keep, two_send = seq.run(20.5, input_grads, grad_gate, grad_up, w_gate, w_up)
    t_two = task(cube.reduce(two_keep, two_send))
    seq.idle(t_two.next())
    up_own = lax.psum_scatter(
        seq.run(12.5, lambda a, b: outer_terms(a, b, n_dp), second, grad_up), "dp", scatter_dimension=0, tiled=True
    )
    down_keep, down_send = seq.run(11.5, lambda h, w: even_odd(dot(h, w)), hidden, w_down)
    grad_hidden_in, branch_own, gain_two_own = seq.run(
        5.8, lambda *a: norm_back(*a, True), hidden_in, *t_two.finish(), grad_own, gain_two
    )
    t_branch_grad = task(cube.gather(branch_own))
    gate_terms = seq.run(12.5, lambda a, b: outer_terms(a, b, n_dp), second, grad_gate)
    branch_grad = cube.joined(t_branch_grad.finish()).reshape(bucket, width)

    grad_gated = seq.run(3.8, dot_nt, branch_grad, w_out)
    t_down = task(cube.reduce(down_keep, down_send))
    t_down_all = task(cube.gather(seq.tie(down_own)[0]))
    grad_qk, grad_vg, gain_query_own, gain_key_own = seq.run(
        20.0,
        attend_back,
        place, raw_qk, queries, keys, values, gate, attended, grad_gated.reshape(n_u, rows, q_w), log_totals,
        q_gain, k_gain, *tables,
    )
    grad_qk, grad_vg = grad_qk.reshape(bucket, -1), grad_vg.reshape(bucket, -1)
    one_keep, one_send = seq.run(12.0, input_grads, grad_qk, grad_vg, w_qk, w_vg)
    t_one = task(cube.reduce(one_keep, one_send))
    out_parts = seq.run(7.0, lambda p, a, b: out_terms(p, a, b, n_u), place, gated, branch_grad, take=False)
    qk_terms = seq.run(9.3, lambda a, b: outer_terms(a, b, n_dp), normed, grad_qk, take=False)
    t_one.poll(seq.now + 100.0)
    vg_terms = seq.run(9.3, lambda a, b: outer_terms(a, b, n_dp), normed, grad_vg, take=False)

    gate_all, qk_all, vg_all, out_all = seq.run(
        150.0, lambda b, *t: reduce_all(b, t, n_dp, n_u), out_parts, gate_terms, qk_terms, vg_terms, take=False
    )
    t_up_all = task(cube.gather(seq.tie(up_own)[0]))
    tokens_grad, gain_one_own = seq.run(
        5.6, lambda *a: norm_back(*a, False), tokens[0], *t_one.finish(), grad_hidden_in, gain_one
    )
    gains = seq.run(
        1.0, lambda *g: jnp.concatenate(g, axis=1)[0], gain_one_own, gain_query_own, gain_key_own, gain_two_own
    )
    t_gains = task(cube.total(gains, ("ulysses", "dp")))
    keys_all = [list(range(n_u))]
    in_all = seq.run(
        5.5,
        lambda p, a, b: put_columns(
            p, [(keys_all, [a]), (keys_all, [b])], [[(0, q_w), (q_w, kv_w)], [(0, kv_w), (kv_w, q_w)]]
        ),
        place, qk_all, vg_all,
    )
    out_all = seq.run(4.0, lambda p, a: put_columns(p, [(keys_all, [a])], [[(0, out_cols)]]), place, out_all)
    down_held = t_down_all.finish()
    down_all = seq.run(5.3, lambda p, *b: put_rows(p, (down_held[0], b)), place, *down_held[1])
    up_held = t_up_all.finish()
    mlp_all = seq.run(
        10.0, lambda p, a, *b: put_strips(p, [(keys_all, [a]), (up_held[0], b)], n_dp, ff_strip), place, gate_all, *up_held[1]
    )
    layer_out = seq.run(2.2, lambda a, b, c: a + high(b) + high(c), hidden_in, *t_down.finish())
    gains = t_gains.finish()

    gain_one_sum = gains[:width]
    gain_query_sum = gains[width : width + head_width]
    gain_key_sum = gains[width + head_width : width + 2 * head_width]
    gain_two_sum = gains[width + 2 * head_width :]
    return (
        layer_out[None],
        tokens_grad[None],
        gain_one_sum,
        in_all,
        gain_query_sum,
        gain_key_sum,
        out_all,
        gain_two_sum,
        mlp_all,
        down_all,
    )


def solution(mesh):
    placed = (
        P("dp", "ulysses", None),
        P("dp"),
        P("dp", "ulysses", None),
        P(),
        P("dp", None),
        P(),
        P(),
        P("dp", None),
        P(),
        P("dp", None),
        P("dp", None),
    )
    return jax.shard_map(
        shards,
        mesh=mesh,
        in_specs=placed,
        out_specs=(
            P("dp", "ulysses", None),
            P("dp", "ulysses", None),
            P(),
            P("dp", None),
            P(),
            P(),
            P("dp", None),
            P(),
            P("dp", None),
            P("dp", None),
        ),
        check_vma=False,
    )
```
